32 devices in a mesh: fsdp: 8 (over z, y), dp: 4 (over x, core).
Axes of the slice: x: 2, y: 2, z: 4, core: 2. Of those that a mesh axis runs over, the one named last changes fastest.
Arguments:
- tokens: bfloat16 [24576, 576], P(('fsdp', 'dp')), may hold values from -6 to 6
- cotangent: bfloat16 [24576, 576], P(('fsdp', 'dp')), may hold values from -6 to 6
- lengths: int32 [8, 3], P('fsdp'), may hold values from 1 to 1536, 2304 in all within a row
- assignment: int32 [8, 24], P('fsdp'), may hold values from 0 to 23, as said below
- norm_gains: float32 [576, 2], P('fsdp'), may hold values from 0.5 to 1.5
- gain_momentum: float32 [576, 2], P('fsdp'), may hold values from -160 to 160
- w_query: float32 [576, 576], P('fsdp'), may hold values from -0.25 to 0.25
- w_keyval: float32 [576, 2, 192], P('fsdp'), may hold values from -0.25 to 0.25
- w_out: float32 [576, 576], P('fsdp'), may hold values from -1 to 1
- w_gateup: float32 [576, 2, 1536], P('fsdp'), may hold values from -0.25 to 0.25
- w_down: float32 [1536, 576], P('fsdp'), may hold values from -0.15625 to 0.15625
- m_query: float32 [576, 576], P('fsdp'), may hold values from -160 to 160
- m_keyval: float32 [576, 2, 192], P('fsdp'), may hold values from -160 to 160
- m_out: float32 [576, 576], P('fsdp'), may hold values from -160 to 160
- m_gateup: float32 [576, 2, 1536], P('fsdp'), may hold values from -160 to 160
- m_down: float32 [1536, 576], P('fsdp'), may hold values from -160 to 160
Outputs:
- activations: bfloat16 [24576, 576], P(('fsdp', 'dp'))
- input_grad: float32 [24576, 576], P(('fsdp', 'dp'))
- gain_grads: float32 [576, 2], P('fsdp')
- gain_moments: float32 [576, 2], P('fsdp')
- gain_values: float32 [576, 2], P('fsdp')
- query_grad: float32 [576, 576], P('fsdp')
- query_moment: float32 [576, 576], P('fsdp')
- query_new: float32 [576, 576], P('fsdp')
- keyval_grad: float32 [576, 2, 192], P('fsdp')
- keyval_moment: float32 [576, 2, 192], P('fsdp')
- keyval_new: float32 [576, 2, 192], P('fsdp')
- outproj_grad: float32 [576, 576], P('fsdp')
- outproj_moment: float32 [576, 576], P('fsdp')
- outproj_new: float32 [576, 576], P('fsdp')
- gateup_grad: float32 [576, 2, 1536], P('fsdp')
- gateup_moment: float32 [576, 2, 1536], P('fsdp')
- gateup_new: float32 [576, 2, 1536], P('fsdp')
- down_grad: float32 [1536, 576], P('fsdp')
- down_moment: float32 [1536, 576], P('fsdp')
- down_new: float32 [1536, 576], P('fsdp')
The draws below stay inside these ranges and needn't reach their ends.
Inputs may be any that keep to these rules, and one draw needn't show every extreme that they name: Row g holds the lengths of the 3 sequences of group g in order; they sum to 2304. `assignment`: each row is a permutation of 0 to 23; entry b of row g places the group's b-th block in rows value * 128 to value * 128 + 127 of the group, held by the device at dp index value // 6.
All inputs are finite; a program needn't handle non-finite values.
Results may differ from the reference program's by a relative error of at most 0.023.
Values may be sent and summed in bfloat16 or wider, within the bound.
A program may use at most 192 MiB of HBM per device.

```python
import math
import jax
import jax.numpy as jnp
import numpy as np
from jax import lax

D = 576
HEADS = 9
KVH = 3
HD = 64
FF = 1536
BLK = 128
SEQS_G = 3
NS_STEPS = 5
SLOTS = 6
QW = 576
KVW = 192
GBLOCKS = 24
GROUP_ROWS = 3072
GROUPS = 8
TOKENS = 24576
LIVE_G = 2304
LEN_MAX = 1536


def draw_assignment(key, part):
    key = jax.random.fold_in(key, 7)
    device_count = GBLOCKS // SLOTS

    def one_group(group_key):
        round_key, slot_key = jax.random.split(group_key)
        device_order = jax.vmap(lambda sub_key: jax.random.permutation(sub_key, device_count))(jax.random.split(round_key, SLOTS))
        slot_order = jax.vmap(lambda sub_key: jax.random.permutation(sub_key, SLOTS))(jax.random.split(slot_key, device_count))
        round_index = jnp.arange(SLOTS)[:, None]
        within = slot_order[device_order, round_index]
        return (device_order * SLOTS + within).reshape(-1).astype(jnp.int32)
    return jax.vmap(one_group)(jax.random.split(key, GROUPS))


def shard_levels(own_key, dims, shards, low, top_value):
    def one(axis_at, parts):
        draws = jax.random.uniform(jax.random.fold_in(jax.random.fold_in(own_key, 6), axis_at), (parts,), jnp.float32, low / len(shards), top_value / len(shards))
        return jnp.repeat(jnp.exp(draws), dims[axis_at] // parts).reshape((-1,) + (1,) * (len(dims) - axis_at - 1))

    loudness = one(*shards[0])
    for cut in shards[1:]:
        loudness = loudness * one(*cut)
    return loudness


def profile(count, total, reach, skew):
    weights = [(1 << 20) // math.isqrt(grade ** skew) + 1 for grade in range(2, count + 1)]
    surplus, holding = total - reach - (count - 1), [1] * (count - 1)
    while surplus > 0:
        free = [i for i in range(count - 1) if holding[i] < reach]
        pool, budget = sum([weights[i] for i in free]), surplus
        for i in free:
            extra = min(reach - holding[i], max(1, budget * weights[i] // pool), surplus)
            holding[i] = holding[i] + extra
            surplus = surplus - extra
    return np.array([reach] + holding)


def ragged(stream_key, number_of, total, most, lean):
    if number_of == 2:
        one = jax.random.randint(stream_key, (), max(1, total - most), min(most, total - 1) + 1)
        return jnp.stack([one, total - one])
    sizes = jnp.asarray(profile(number_of, total, most, lean), jnp.int32)
    pairs = (number_of - 1) // 2
    donor, receiver = sizes[1:1 + 2 * pairs:2], sizes[2:2 + 2 * pairs:2]
    room = jnp.minimum(donor - 1, most - receiver)
    passed = jax.random.randint(jax.random.fold_in(stream_key, 1), (pairs,), 0, 1 << 20) % (room + 1)
    sizes = sizes.at[1:1 + 2 * pairs:2].set(donor - passed).at[2:2 + 2 * pairs:2].set(receiver + passed)
    return sizes[jax.random.permutation(jax.random.fold_in(stream_key, 2), number_of)]


def gaussian(own_key, extent, width, reach, pieces=(), kind=jnp.bfloat16):
    values = jax.random.normal(own_key, extent, jnp.float32) * width
    if len(pieces) > 0:
        values = shard_levels(own_key, extent, pieces, -0.22, 0.18) * values
    return jnp.clip(values, min=-reach, max=reach).astype(kind)


def setup_inputs(seed: int = 0) -> dict:
    streams_of = jax.random.split(jax.random.key(seed), 17)
    tokens = gaussian(streams_of[0], (TOKENS, D), 1.0, 6.0, ((0, 32),))
    cotangent = gaussian(streams_of[1], (TOKENS, D), 1.0, 6.0, ((0, 32),))
    lengths = jax.vmap(lambda own: ragged(own, SEQS_G, LIVE_G, LEN_MAX, 2))(jax.random.split(streams_of[2], GROUPS)).reshape((GROUPS, SEQS_G)).astype(jnp.int32)
    assignment = draw_assignment(jax.random.fold_in(streams_of[16], 71), 0)
    norm_gains = jnp.clip(1.0 + 0.1 * jax.random.normal(streams_of[4], (D, 2), jnp.float32), 0.5, 1.5)
    gain_momentum = gaussian(streams_of[5], (D, 2), (0.2 * (LIVE_G * GROUPS) ** 0.5), 160.0, ((0, 8),), jnp.float32)
    w_query = gaussian(streams_of[6], (D, QW), D ** -0.5, 0.25, ((0, 8),), jnp.float32)
    w_keyval = gaussian(streams_of[7], (D, 2, KVW), D ** -0.5, 0.25, ((0, 8),), jnp.float32)
    w_out = gaussian(streams_of[8], (QW, D), (QW // 16) ** -0.5, 1.0, ((0, 8),), jnp.float32)
    w_gateup = gaussian(streams_of[9], (D, 2, FF), D ** -0.5, 0.25, ((0, 8),), jnp.float32)
    w_down = gaussian(streams_of[10], (FF, D), FF ** -0.5, 0.15625, ((0, 8),), jnp.float32)
    m_query = gaussian(streams_of[11], (D, QW), (0.2 * (LIVE_G * GROUPS) ** 0.5), 160.0, ((0, 8),), jnp.float32)
    m_keyval = gaussian(streams_of[12], (D, 2, KVW), (0.2 * (LIVE_G * GROUPS) ** 0.5), 160.0, ((0, 8),), jnp.float32)
    m_out = gaussian(streams_of[13], (QW, D), (0.2 * (LIVE_G * GROUPS) ** 0.5), 160.0, ((0, 8),), jnp.float32)
    m_gateup = gaussian(streams_of[14], (D, 2, FF), (0.2 * (LIVE_G * GROUPS) ** 0.5), 160.0, ((0, 8),), jnp.float32)
    m_down = gaussian(streams_of[15], (FF, D), (0.2 * (LIVE_G * GROUPS) ** 0.5), 160.0, ((0, 8),), jnp.float32)
    return dict(tokens=tokens, cotangent=cotangent, lengths=lengths, assignment=assignment, norm_gains=norm_gains, gain_momentum=gain_momentum, w_query=w_query, w_keyval=w_keyval, w_out=w_out, w_gateup=w_gateup, w_down=w_down, m_query=m_query, m_keyval=m_keyval, m_out=m_out, m_gateup=m_gateup, m_down=m_down)


EPS = 1e-05
THETA = 100000.0
MOMENTUM_DECAY = 0.95
GAIN_DECAY = 0.9
MUON_RATE = 0.03
GAIN_SCALE = 0.4
COEF_A = 3.4445
COEF_B = -4.775
COEF_C = 2.0315
HIGHEST = lax.Precision.HIGHEST

@jax.custom_vjp
def low(v):
    return lax.optimization_barrier(v.astype(jnp.bfloat16)).astype(jnp.float32)

@jax.custom_vjp
def low_back(v):
    return v

def low_keep(v):
    return (low(v), None)

def low_pass(kept, grad):
    return (grad,)

def back_keep(v):
    return (v, None)

def back_low(kept, grad):
    return (low(grad),)
low.defvjp(low_keep, low_pass)
low_back.defvjp(back_keep, back_low)

def group_meta(length_row, assign_row, block_count):
    slot_index = jnp.arange(block_count, dtype=jnp.int32)
    block_sizes = ((length_row + BLK - 1) // BLK).astype(jnp.int32)
    block_start = (jnp.cumsum(block_sizes) - block_sizes).astype(jnp.int32)
    block_of = lax.optimization_barrier(jnp.sum(jnp.where(assign_row[:, None] == slot_index[None, :], slot_index[:, None], 0), axis=0)).astype(jnp.int32)
    inside = (block_of[:, None] >= block_start[None, :]) & (block_of[:, None] < (block_start + block_sizes)[None, :])
    seq_index = jnp.arange(SEQS_G, dtype=jnp.int32)
    seq_of = lax.optimization_barrier(jnp.sum(jnp.where(inside, seq_index[None, :], 0), axis=1)).astype(jnp.int32)
    first_block = lax.optimization_barrier(jnp.sum(jnp.where(inside, block_start[None, :], 0), axis=1)).astype(jnp.int32)
    seq_length = lax.optimization_barrier(jnp.sum(jnp.where(inside, length_row[None, :], 0), axis=1)).astype(jnp.int32)
    used = jnp.any(inside, axis=1)
    offset = (block_of - first_block)[:, None] * BLK + jnp.arange(BLK, dtype=jnp.int32)[None, :]
    living = used[:, None] & (offset < seq_length[:, None])
    row_index = jnp.arange(block_count * BLK, dtype=jnp.int32).reshape(block_count, BLK)
    seq_ids = jnp.where(living, seq_of[:, None], SEQS_G + row_index).astype(jnp.int32)
    positions = jnp.where(living, offset, 0).astype(jnp.int32)
    return (seq_ids.reshape(-1), positions.reshape(-1), living.reshape(-1))

def rope_tables(positions):
    freq = jnp.exp(jnp.arange(HD // 2, dtype=jnp.float32) * (-2.0 * math.log(THETA) / HD))
    angles = positions.astype(jnp.float32)[:, None] * freq[None, :]
    return (jnp.cos(angles), jnp.sin(angles))

def rotate(values, cosine, sine):
    half = HD // 2
    first = values[..., :half]
    second = values[..., half:]
    cos_part = cosine[:, None, :]
    sin_part = sine[:, None, :]
    return jnp.concatenate([first * cos_part - second * sin_part, second * cos_part + first * sin_part], axis=-1)

def attend_block(queries, query_seq, query_pos, keys, values, key_seq, key_pos):
    scores = jnp.einsum('qhjd,khd->hjqk', queries, keys, precision=HIGHEST) * (1.0 / math.sqrt(HD))
    scores = low_back(scores)
    allowed = (key_seq[None, :] == query_seq[:, None]) & (key_pos[None, :] <= query_pos[:, None])
    masked = jnp.where(allowed, scores, -1e+30)
    peak = lax.optimization_barrier(jnp.max(masked, axis=-1, keepdims=True))
    weights = jnp.where(allowed, jnp.exp(masked - peak), 0.0)
    probs = low(weights / lax.optimization_barrier(jnp.sum(weights, axis=-1, keepdims=True)))
    mixed = jnp.einsum('hjqk,khd->qhjd', probs, values, precision=HIGHEST)
    return mixed.reshape(queries.shape[0], QW)

def layer(inputs, w_q, w_kv, w_o, w_gu, w_d, gains, seq_ids, positions):
    gain_low = low(gains)
    row_count = inputs.shape[0]
    norm_one = inputs * lax.rsqrt(lax.optimization_barrier(jnp.mean(inputs * inputs, axis=-1, keepdims=True)) + EPS)
    normed = low(norm_one * gain_low[:, 0])
    query_lin = low_back(jnp.dot(normed, low(w_q), precision=HIGHEST))
    keyval_lin = low_back(jnp.dot(normed, low(w_kv).reshape(D, 2 * KVW), precision=HIGHEST))
    cosine, sine = rope_tables(positions)
    queries = low(rotate(query_lin.reshape(row_count, HEADS, HD), cosine, sine))
    keys = low(rotate(keyval_lin[:, :KVW].reshape(row_count, KVH, HD), cosine, sine))
    values = low(keyval_lin[:, KVW:].reshape(row_count, KVH, HD))
    block_rows = min(512, row_count)
    block_total = row_count // block_rows
    grouped = queries.reshape(block_total, block_rows, KVH, HEADS // KVH, HD)
    attend = jax.checkpoint(attend_block)

    def per_block(block_item):
        return attend(block_item[0], block_item[1], block_item[2], keys, values, seq_ids, positions)
    mixed = lax.map(per_block, (grouped, seq_ids.reshape(block_total, block_rows), positions.reshape(block_total, block_rows)))
    attended = low(low_back(mixed.reshape(row_count, QW)))
    branch = low_back(jnp.dot(attended, low(w_o), precision=HIGHEST))
    residual = inputs + branch
    norm_two = residual * lax.rsqrt(lax.optimization_barrier(jnp.mean(residual * residual, axis=-1, keepdims=True)) + EPS)
    second = low(norm_two * gain_low[:, 1])
    gate_up = low_back(jnp.dot(second, low(w_gu).reshape(D, 2 * FF), precision=HIGHEST))
    hidden = low(jax.nn.silu(gate_up[:, :FF]) * gate_up[:, FF:])
    return residual + low_back(jnp.dot(hidden, low(w_d), precision=HIGHEST))

def orthogonal(matrix):
    flipped = matrix.shape[0] > matrix.shape[1]
    iterate = matrix.T if flipped else matrix
    iterate = iterate / (jnp.sqrt(jnp.sum(iterate * iterate)) + 1e-07)
    for turn in range(NS_STEPS):
        gram_matrix = jnp.dot(iterate, iterate.T, precision=HIGHEST)
        polynomial = COEF_B * gram_matrix + COEF_C * jnp.dot(gram_matrix, gram_matrix, precision=HIGHEST)
        iterate = COEF_A * iterate + jnp.dot(polynomial, iterate, precision=HIGHEST)
    return iterate.T if flipped else iterate

def muon_step(matrix):
    return MUON_RATE * math.sqrt(max(matrix.shape[0], matrix.shape[1])) * orthogonal(matrix)

def reference(tokens, cotangent, lengths, assignment, norm_gains, gain_momentum, w_query, w_keyval, w_out, w_gateup, w_down, m_query, m_keyval, m_out, m_gateup, m_down):
    inputs = tokens.astype(jnp.float32).reshape(GROUPS, GROUP_ROWS, D)
    cotangents = cotangent.astype(jnp.float32).reshape(GROUPS, GROUP_ROWS, D)

    def one_group(running, group_item):
        group_in, group_cot, length_row, assign_row = group_item
        seq_ids, positions, living = group_meta(length_row, assign_row, GBLOCKS)

        def forward(values_in, w_q, w_kv, w_o, w_gu, w_d, gains):
            return layer(values_in, w_q, w_kv, w_o, w_gu, w_d, gains, seq_ids, positions)
        result, pullback = jax.vjp(forward, group_in, w_query, w_keyval, w_out, w_gateup, w_down, norm_gains)
        gradients = pullback(group_cot * living[:, None].astype(jnp.float32))
        updated = tuple((accum + gradient for accum, gradient in zip(running, gradients[1:])))
        return (updated, (result.astype(jnp.bfloat16), gradients[0]))
    start = (jnp.zeros_like(w_query), jnp.zeros_like(w_keyval), jnp.zeros_like(w_out), jnp.zeros_like(w_gateup), jnp.zeros_like(w_down), jnp.zeros_like(norm_gains))
    totals, (outputs, input_grads) = lax.scan(one_group, start, (inputs, cotangents, lengths, assignment))
    g_query, g_keyval, g_out, g_gateup, g_down, g_gains = totals
    new_query = MOMENTUM_DECAY * m_query + g_query
    new_keyval = MOMENTUM_DECAY * m_keyval + g_keyval
    new_out = MOMENTUM_DECAY * m_out + g_out
    new_gateup = MOMENTUM_DECAY * m_gateup + g_gateup
    new_down = MOMENTUM_DECAY * m_down + g_down
    step_keyval = jnp.stack([muon_step(new_keyval[:, 0, :]), muon_step(new_keyval[:, 1, :])], axis=1)
    step_gateup = jnp.stack([muon_step(new_gateup[:, 0, :]), muon_step(new_gateup[:, 1, :])], axis=1)
    gain_moments = GAIN_DECAY * gain_momentum + g_gains
    gain_rate = GAIN_SCALE / math.sqrt(LIVE_G * GROUPS)
    return (outputs.reshape(TOKENS, D), input_grads.reshape(TOKENS, D), g_gains, gain_moments, norm_gains - gain_rate * gain_moments, g_query, new_query, w_query - muon_step(new_query), g_keyval, new_keyval, w_keyval - step_keyval, g_out, new_out, w_out - muon_step(new_out), g_gateup, new_gateup, w_gateup - step_gateup, g_down, new_down, w_down - muon_step(new_down))
```

```python
from functools import partial
import math

import jax
import jax.numpy as jnp
import numpy as np
from jax import lax
from jax.experimental import pallas as pl
from jax.experimental.pallas import tpu as pltpu
from jax.sharding import PartitionSpec as P

D = 576
HEADS = 9
KVH = 3
HD = 64
FF = 1536
BLK = 128
SEQS_G = 3
NS_STEPS = 5
QW = 576
KVW = 192
LONGEST = 12

EPS = 1e-05
THETA = 100000.0
MOMENTUM_DECAY = 0.95
GAIN_DECAY = 0.9
MUON_RATE = 0.03
GAIN_SCALE = 0.4
COEF_A = 3.4445
COEF_B = -4.775
COEF_C = 2.0315
SCALE = 1.0 / math.sqrt(HD)
HALF = 768
WIDE_A = 2 * (HALF + 128)
O_AT = HALF + 128
STEP = 256
F32, BF16 = jnp.float32, jnp.bfloat16


def vmem(count=1):
    return [pl.BlockSpec(memory_space=pltpu.VMEM)] * count


def dot(a, b):
    return lax.dot_general(a, b, (((1,), (0,)), ((), ())), preferred_element_type=F32)


def dot_nt(a, b):
    return lax.dot_general(a, b, (((1,), (1,)), ((), ())), preferred_element_type=F32)


def dot_tn(a, b):
    return lax.dot_general(a, b, (((0,), (0,)), ((), ())), preferred_element_type=F32)


def block_meta(length_row, assign_row, first_slot, slots):
    entries = jnp.arange(assign_row.shape[0], dtype=jnp.int32)
    sizes = (length_row + BLK - 1) // BLK
    start = jnp.cumsum(sizes) - sizes
    mine = first_slot + jnp.arange(slots, dtype=jnp.int32)
    entry = jnp.sum(jnp.where(assign_row[None, :] == mine[:, None], entries[None, :], 0), axis=1)
    inside = (entry[:, None] >= start[None, :]) & (entry[:, None] < (start + sizes)[None, :])
    first = jnp.sum(jnp.where(inside, start[None, :], 0), axis=1)
    size = jnp.sum(jnp.where(inside, length_row[None, :], 0), axis=1)
    used = jnp.any(inside, axis=1)
    place = jnp.where(used, entry - first, 0)
    live = jnp.where(used, jnp.clip(size - place * BLK, 0, BLK), 0)
    step = jnp.arange(LONGEST, dtype=jnp.int32)
    want = first[:, None] + step[None, :]
    keys = jnp.sum(
        jnp.where(want[:, :, None] == entries[None, None, :], assign_row[None, None, :], 0), axis=2
    )
    keys = jnp.where(used[:, None] & (step[None, :] <= place[:, None]), keys, mine[:, None])
    return jnp.concatenate(
        [place[:, None], live[:, None], (place // 2 + 1)[:, None], live[:, None], keys], axis=1
    )


def rope_constants():
    freq = np.exp(np.arange(HD // 2, dtype=np.float64) * (-2.0 * math.log(THETA) / HD))
    lanes = np.tile(freq, 4)
    inner = np.arange(BLK)[:, None] * lanes[None, :]
    outer = BLK * np.arange(16)[:, None] * lanes[None, :]
    return (
        np.stack([np.cos(inner), np.sin(inner)]).astype(np.float32),
        np.stack([np.cos(outer), np.sin(outer)]).astype(np.float32),
    )


def lane_index(rows):
    return lax.broadcasted_iota(jnp.int32, (rows, 128), 1)


def rope_tables(meta, slot, inner_ref, outer_ref):
    place, live = meta[slot, 0], meta[slot, 1]
    co, so = outer_ref[0, pl.ds(place, 1), :], outer_ref[1, pl.ds(place, 1), :]
    ci, si = inner_ref[0], inner_ref[1]
    lane = lane_index(BLK)
    row = lax.broadcasted_iota(jnp.int32, (BLK, 128), 0)
    turned = (row < live) & (lane < HD)
    cosine = jnp.where(turned, co * ci - so * si, 1.0)
    sine = jnp.where(turned, so * ci + co * si, 0.0)
    return cosine, jnp.where(lane < HD // 2, sine, 0.0), jnp.where(lane < HD // 2, 0.0, sine)


def rope(tile, tables):
    cosine, sine_low, sine_high = tables
    return (
        tile * cosine - pltpu.roll(tile, 128 - HD // 2, 1) * sine_low
        + pltpu.roll(tile, HD // 2, 1) * sine_high
    )


def rope_back(tile, tables):
    cosine, sine_low, sine_high = tables
    return (
        tile * cosine + pltpu.roll(tile, 128 - HD // 2, 1) * sine_low
        - pltpu.roll(tile, HD // 2, 1) * sine_high
    )


def swap(tile):
    return pltpu.roll(tile, HD, 1)


def gain_row(packed_ref, at):
    return packed_ref[:, at : at + 128].astype(F32).T[0:1, :]


def project_kernel(meta, x_ref, wa_ref, inner_ref, outer_ref, q_ref, kv_ref):
    gain = gain_row(wa_ref, HALF)
    low_lane = lane_index(BLK) < HD

    @pl.loop(0, x_ref.shape[0] // STEP)
    def _(i):
        x = x_ref[pl.ds(pl.multiple_of(i * STEP, STEP), STEP), :].astype(F32)
        inv = lax.rsqrt(jnp.mean(x * x, axis=1, keepdims=True) + EPS)
        normed = (x * inv * gain).astype(BF16)
        qk = dot(normed, wa_ref[:, :HALF])
        ov = dot(normed, wa_ref[:, O_AT + 512 : O_AT + HALF])
        for b in range(STEP // BLK):
            tables = rope_tables(meta, i * (STEP // BLK) + b, inner_ref, outer_ref)
            rows = pl.ds(pl.multiple_of(i * STEP + b * BLK, BLK), BLK)
            part = slice(b * BLK, (b + 1) * BLK)
            tiles = [qk[part, 128 * t : 128 * t + 128] for t in range(6)]
            for head in range(HEADS):
                tile = tiles[head // 2]
                tile = jnp.where(low_lane, swap(tile) if head % 2 else tile, 0.0)
                q_ref[rows, 128 * head : 128 * head + 128] = (rope(tile, tables) * SCALE).astype(BF16)
            values = [ov[part, :128], ov[part, 128:]]
            pairs = (
                (swap(tiles[4]), values[0]),
                (tiles[5], swap(values[1])),
                (swap(tiles[5]), values[1]),
            )
            for h in range(KVH):
                tile = jnp.where(low_lane, *pairs[h])
                kv_ref[rows, 128 * h : 128 * h + 128] = rope(tile, tables).astype(BF16)


def project(meta, tokens, packed, inner, outer):
    rows = tokens.shape[0]
    return pl.pallas_call(
        project_kernel,
        out_shape=(
            jax.ShapeDtypeStruct((rows, 128 * HEADS), BF16),
            jax.ShapeDtypeStruct((rows, 2 * KVW), BF16),
        ),
        in_specs=[pl.BlockSpec(memory_space=pltpu.SMEM)] + vmem(4),
        out_specs=tuple(vmem(2)),
        compiler_params=pltpu.CompilerParams(vmem_limit_bytes=48 << 20),
        name="project",
    )(meta, tokens, packed, inner, outer)


def chunk_bias(meta, slot, chunk):
    row = lax.broadcasted_iota(jnp.int32, (BLK, 2 * BLK), 0) + meta[slot, 0] * BLK
    column = lax.broadcasted_iota(jnp.int32, (BLK, 2 * BLK), 1) + chunk * (2 * BLK)
    live_end = meta[slot, 0] * BLK + meta[slot, 1]
    allowed = (column <= row) & ((row < live_end) | (column == row))
    bias = jnp.where(allowed, 0.0, -1e30)
    return jnp.concatenate([bias] * (HEADS // KVH), axis=0)


def key_tile(kv_ref, meta, slot, chunk, h):
    lanes = slice(128 * h, 128 * h + 128)
    one = pl.ds(pl.multiple_of(meta[slot, 4 + 2 * chunk] * BLK, BLK), BLK)
    two = pl.ds(pl.multiple_of(meta[slot, 5 + 2 * chunk] * BLK, BLK), BLK)
    return jnp.concatenate([kv_ref[one, lanes], kv_ref[two, lanes]], axis=0)


def stacked(ref, rows, h):
    at = 128 * (HEADS // KVH) * h
    return jnp.concatenate(
        [ref[rows, at + 128 * j : at + 128 * j + 128] for j in range(HEADS // KVH)], axis=0
    )


def twice(value):
    return jnp.concatenate([value, value], axis=1)


def attention_forward(meta, q_ref, kv_ref, mixed_s, low_s, lse_s, peak_s, accum_s):
    group = HEADS // KVH
    low_lane = lane_index(group * BLK) < HD
    low_key = lane_index(2 * BLK) < HD

    @pl.loop(0, q_ref.shape[0] // BLK)
    def _(slot):
        rows = pl.ds(pl.multiple_of(slot * BLK, BLK), BLK)
        peak_s[...] = jnp.full_like(peak_s, -1e30)
        accum_s[...] = jnp.zeros_like(accum_s)

        @pl.loop(0, meta[slot, 2])
        def _(chunk):
            bias = chunk_bias(meta, slot, chunk)
            for h in range(KVH):
                tile = key_tile(kv_ref, meta, slot, chunk, h)
                scores = dot_nt(stacked(q_ref, rows, h), tile) + bias
                old = peak_s[h]
                new = jnp.maximum(old, jnp.max(scores, axis=1, keepdims=True))
                probs = jnp.exp(scores - twice(new)).astype(BF16)
                ones = jnp.where(low_key, jnp.ones_like(tile), tile)
                accum_s[h] = accum_s[h] * jnp.exp(old - new) + dot(probs, ones)
                peak_s[h] = new

        outs = []
        for h in range(KVH):
            accum = accum_s[h]
            other = swap(accum)
            total = jnp.where(low_lane, accum, other)
            lse_s[slot, h] = peak_s[h] + jnp.log(total)
            mixed = accum / total
            mixed_s[slot, h] = mixed
            outs += [mixed[BLK * j : BLK * j + BLK] for j in range(group)]
        one_low = lane_index(BLK) < HD
        for t in range(HEADS // 2):
            pair = jnp.where(one_low, swap(outs[2 * t]), outs[2 * t + 1])
            low_s[rows, 128 * t : 128 * t + 128] = pair.astype(BF16)
        low_s[rows, QW - HD : QW] = swap(outs[HEADS - 1])[:, :HD].astype(BF16)


def feed_forward(
    meta, x_ref, cot_ref, wa_ref, wgu_ref, wd_ref, act_ref, gres_ref, gb_ref, gain_ref,
    low_s, mixed_s, do_s, delta_s, second_s, grad_gu_s, hidden_s, gm_s,
):
    group = HEADS // KVH
    gain = gain_row(wa_ref, O_AT + HALF)
    high_lane = lane_index(BLK) >= HD
    gain_ref[...] = jnp.zeros_like(gain_ref)

    @pl.loop(0, x_ref.shape[0] // STEP)
    def _(i):
        rows = pl.ds(pl.multiple_of(i * STEP, STEP), STEP)
        w_out = wa_ref[:, O_AT : O_AT + QW]
        residual = x_ref[rows, :].astype(F32) + dot(low_s[rows, :], w_out)
        inv = lax.rsqrt(jnp.mean(residual * residual, axis=1, keepdims=True) + EPS)
        norm = residual * inv
        second = (norm * gain).astype(BF16)
        second_s[:, rows] = second.T
        row = lax.broadcasted_iota(jnp.int32, (BLK, 1), 0)
        living = jnp.concatenate(
            [
                (row < meta[i * (STEP // BLK) + b, 1]).astype(F32)
                for b in range(STEP // BLK)
            ],
            axis=0,
        )
        grad_final = cot_ref[rows, :].astype(F32) * living
        grad_mlp = grad_final.astype(BF16)
        gm_s[rows, :] = grad_mlp
        out = residual
        grad_second = jnp.zeros_like(residual)
        width = 512
        for c in range(0, FF, width):
            w_gate, w_up = wgu_ref[:, c : c + width], wgu_ref[:, FF + c : FF + c + width]
            w_down = wd_ref[c : c + width, :]
            gate, up = dot(second, w_gate), dot(second, w_up)
            sigma = jax.nn.sigmoid(gate)
            swish = gate * sigma
            hidden = (swish * up).astype(BF16)
            hidden_s[rows, c : c + width] = hidden
            out = out + dot(hidden, w_down)
            grad_hidden = dot_nt(grad_mlp, w_down)
            grad_gate = (grad_hidden * up * (sigma * (1.0 + gate * (1.0 - sigma)))).astype(BF16)
            grad_up = (grad_hidden * swish).astype(BF16)
            grad_gu_s[rows, c : c + width] = grad_gate
            grad_gu_s[rows, FF + c : FF + c + width] = grad_up
            grad_second = grad_second + dot_nt(grad_gate, w_gate) + dot_nt(grad_up, w_up)
        act_ref[rows, :] = out.astype(BF16)
        scaled = grad_second * gain
        grad_res = grad_final + inv * (scaled - norm * jnp.mean(scaled * norm, axis=1, keepdims=True))
        gres_ref[rows, :] = grad_res
        grad_branch = grad_res.astype(BF16)
        gb_ref[rows, :QW] = grad_branch
        gb_ref[rows, QW:] = jnp.zeros((STEP, 128 - HD), BF16)
        gain_ref[0:1, :] += jnp.sum(grad_second * norm, axis=0, keepdims=True)
        grad_att = dot_nt(grad_branch, w_out)
        for b in range(STEP // BLK):
            slot = i * (STEP // BLK) + b
            here = pl.ds(pl.multiple_of(i * STEP + b * BLK, BLK), BLK)
            part = slice(b * BLK, (b + 1) * BLK)
            for head in range(HEADS):
                at = 128 * (head // 2)
                if head == HEADS - 1:
                    tile = jnp.concatenate([grad_att[part, at : at + HD]] * 2, axis=1)
                else:
                    tile = grad_att[part, at : at + 128]
                    tile = tile if head % 2 else swap(tile)
                tile = jnp.where(high_lane, tile, 0.0).astype(BF16)
                do_s[here, 128 * head : 128 * head + 128] = tile
                h, j = head // group, head % group
                product = tile.astype(F32) * mixed_s[slot, h, BLK * j : BLK * j + BLK, :]
                delta = jnp.sum(product, axis=1, keepdims=True)
                delta_s[slot, h, BLK * j : BLK * j + BLK, :] = jnp.broadcast_to(delta, (BLK, 128))


def weight_grads(dgu_ref, dd_ref, second_s, grad_gu_s, hidden_s, gm_s):
    width = 512
    for c in range(0, 2 * FF, width):
        dgu_ref[:, c : c + width] = dot(second_s[...], grad_gu_s[:, c : c + width]).astype(BF16)
    for c in range(0, FF, width):
        dd_ref[c : c + width, :] = dot_tn(hidden_s[:, c : c + width], gm_s[...]).astype(BF16)


def attention_backward(meta, q_ref, kv_ref, inner_ref, outer_ref, do_s, lse_s, delta_s, gq_ref, dkv_s, dq_s):
    group = HEADS // KVH
    tall = group * BLK
    dkv_s[...] = jnp.zeros_like(dkv_s)

    @pl.loop(0, q_ref.shape[0] // BLK)
    def _(slot):
        rows = pl.ds(pl.multiple_of(slot * BLK, BLK), BLK)
        dq_s[...] = jnp.zeros_like(dq_s)

        @pl.loop(0, meta[slot, 2])
        def _(chunk):
            bias = chunk_bias(meta, slot, chunk)
            one = pl.ds(pl.multiple_of(meta[slot, 4 + 2 * chunk] * BLK, BLK), BLK)
            two = pl.ds(pl.multiple_of(meta[slot, 5 + 2 * chunk] * BLK, BLK), BLK)
            for h in range(KVH):
                lanes = slice(128 * h, 128 * h + 128)
                tile = key_tile(kv_ref, meta, slot, chunk, h)
                both = jnp.concatenate([stacked(q_ref, rows, h), stacked(do_s, rows, h)], axis=0)
                products = dot_nt(both, tile)
                probs = jnp.exp(products[:tall] + bias - twice(lse_s[slot, h]))
                grads = (probs * (products[tall:] - twice(delta_s[slot, h]))).astype(BF16)
                dq_s[h] += dot(grads, tile)
                sides = jnp.concatenate([grads, probs.astype(BF16)], axis=0)
                terms = dot_tn(sides, both)
                dkv_s[one, lanes] += terms[:BLK]
                dkv_s[two, lanes] += terms[BLK:]

        tables = rope_tables(meta, slot, inner_ref, outer_ref)
        low_lane = lane_index(BLK) < HD
        heads = [
            rope_back(dq_s[h, BLK * j : BLK * j + BLK, :] * SCALE, tables)
            for h in range(KVH)
            for j in range(group)
        ]
        for t in range(HEADS // 2):
            pair = jnp.where(low_lane, heads[2 * t], swap(heads[2 * t + 1]))
            gq_ref[rows, 128 * t : 128 * t + 128] = pair.astype(BF16)
        gq_ref[rows, QW - HD :] = jnp.where(low_lane, heads[HEADS - 1], 0.0).astype(BF16)


def layer_kernel(
    meta, x_ref, cot_ref, q_ref, kv_ref, wa_ref, wgu_ref, wd_ref, inner_ref, outer_ref,
    act_ref, gres_ref, gb_ref, low_ref, gq_ref, dkv_ref, dgu_ref, dd_ref, gain_ref,
    mixed_s, lse_s, delta_s, peak_s, accum_s, do_s, second_s, grad_gu_s, hidden_s, gm_s, dkv_s,
):
    attention_forward(meta, q_ref, kv_ref, mixed_s, low_ref, lse_s, peak_s, accum_s)
    feed_forward(
        meta, x_ref, cot_ref, wa_ref, wgu_ref, wd_ref, act_ref, gres_ref, gb_ref, gain_ref,
        low_ref, mixed_s, do_s, delta_s, second_s, grad_gu_s, hidden_s, gm_s,
    )
    weight_grads(dgu_ref, dd_ref, second_s, grad_gu_s, hidden_s, gm_s)
    attention_backward(
        meta, q_ref, kv_ref, inner_ref, outer_ref, do_s, lse_s, delta_s, gq_ref, dkv_s, accum_s
    )
    dkv_ref[...] = dkv_s[...].astype(BF16)


def layer(meta, tokens, cotangent, queries, keyval, packed, gateup, down, inner, outer):
    rows, slots, group = tokens.shape[0], tokens.shape[0] // BLK, HEADS // KVH
    keys = keyval.shape[0]
    return pl.pallas_call(
        layer_kernel,
        out_shape=(
            jax.ShapeDtypeStruct((rows, D), BF16),
            jax.ShapeDtypeStruct((rows, D), F32),
            jax.ShapeDtypeStruct((rows, QW + HD), BF16),
            jax.ShapeDtypeStruct((rows, QW), BF16),
            jax.ShapeDtypeStruct((rows, QW + HD), BF16),
            jax.ShapeDtypeStruct((keys, 2 * KVW), BF16),
            jax.ShapeDtypeStruct((D, 2 * FF), BF16),
            jax.ShapeDtypeStruct((FF, D), BF16),
            jax.ShapeDtypeStruct((8, D), F32),
        ),
        in_specs=[pl.BlockSpec(memory_space=pltpu.SMEM)] + vmem(9),
        out_specs=tuple(vmem(9)),
        scratch_shapes=[
            pltpu.VMEM((slots, KVH, group * BLK, 128), F32),
            pltpu.VMEM((slots, KVH, group * BLK, 128), F32),
            pltpu.VMEM((slots, KVH, group * BLK, 128), F32),
            pltpu.VMEM((KVH, group * BLK, 128), F32),
            pltpu.VMEM((KVH, group * BLK, 128), F32),
            pltpu.VMEM((rows, 128 * HEADS), BF16),
            pltpu.VMEM((D, rows), BF16),
            pltpu.VMEM((rows, 2 * FF), BF16),
            pltpu.VMEM((rows, FF), BF16),
            pltpu.VMEM((rows, D), BF16),
            pltpu.VMEM((keys, 2 * KVW), F32),
        ],
        compiler_params=pltpu.CompilerParams(vmem_limit_bytes=62 << 20),
        name="layer",
    )(meta, tokens, cotangent, queries, keyval, packed, gateup, down, inner, outer)


def finish_kernel(
    meta, x_ref, wa_ref, gq_ref, dkv_ref, gres_ref, gb_ref, low_ref, gain_ref, inner_ref, outer_ref,
    in_ref, da_ref, normed_s, first_s, values_s, lowt_s,
):
    gain = gain_row(wa_ref, HALF)
    low_lane = lane_index(BLK) < HD
    rows_all = x_ref.shape[0]
    gains = jnp.zeros((1, D), F32)
    for i in range(rows_all // STEP):
        rows = pl.ds(i * STEP, STEP)
        x = x_ref[rows, :].astype(F32)
        inv = lax.rsqrt(jnp.mean(x * x, axis=1, keepdims=True) + EPS)
        norm = x * inv
        normed_s[:, rows] = (norm * gain).astype(BF16).T
        lowt_s[:, rows] = low_ref[rows, :].T
        first_s[rows, :512] = gq_ref[rows, :512]
        for b in range(STEP // BLK):
            here = pl.ds(i * STEP + b * BLK, BLK)
            tables = rope_tables(meta, i * (STEP // BLK) + b, inner_ref, outer_ref)
            tiles = [
                rope_back(dkv_ref[here, 128 * h : 128 * h + 128].astype(F32), tables)
                for h in range(KVH)
            ]
            last = gq_ref[here, 512:640].astype(F32)
            first_s[here, 512:640] = jnp.where(low_lane, last, swap(tiles[0])).astype(BF16)
            first_s[here, 640:768] = jnp.where(low_lane, tiles[1], swap(tiles[2])).astype(BF16)
            values_s[here, :128] = jnp.where(low_lane, 0.0, tiles[0]).astype(BF16)
            values_s[here, 128:] = jnp.where(low_lane, swap(tiles[1]), tiles[2]).astype(BF16)
        grad_normed = dot_nt(first_s[rows, :], wa_ref[:, :HALF]) + dot_nt(
            values_s[rows, :], wa_ref[:, O_AT + 512 : O_AT + HALF]
        )
        scaled = grad_normed * gain
        in_ref[rows, :] = gres_ref[rows, :] + inv * (
            scaled - norm * jnp.mean(scaled * norm, axis=1, keepdims=True)
        )
        gains = gains + jnp.sum(grad_normed * norm, axis=0, keepdims=True)
    for c in range(0, HALF, 256):
        da_ref[:, c : c + 256] = dot(normed_s[...], first_s[:, c : c + 256]).astype(BF16)
    for c in range(0, 512, 256):
        da_ref[:, O_AT + c : O_AT + c + 256] = dot(lowt_s[...], gb_ref[:, c : c + 256]).astype(BF16)
    da_ref[:, O_AT + 512 : O_AT + 640] = (
        dot(lowt_s[...], gb_ref[:, 512:640]) + dot(normed_s[...], values_s[:, :128])
    ).astype(BF16)
    da_ref[:, O_AT + 640 : O_AT + HALF] = dot(normed_s[...], values_s[:, 128:]).astype(BF16)
    da_ref[:, HALF:O_AT] = jnp.broadcast_to(gains, (128, D)).T.astype(BF16)
    da_ref[:, O_AT + HALF :] = jnp.broadcast_to(gain_ref[0:1, :], (128, D)).T.astype(BF16)


def finish(meta, tokens, packed, gq, dkv, gres, gb, low, gain, inner, outer):
    rows = tokens.shape[0]
    return pl.pallas_call(
        finish_kernel,
        out_shape=(
            jax.ShapeDtypeStruct((rows, D), F32),
            jax.ShapeDtypeStruct((D, WIDE_A), BF16),
        ),
        in_specs=[pl.BlockSpec(memory_space=pltpu.SMEM)] + vmem(10),
        out_specs=tuple(vmem(2)),
        scratch_shapes=[
            pltpu.VMEM((D, rows), BF16),
            pltpu.VMEM((rows, HALF), BF16),
            pltpu.VMEM((rows, 256), BF16),
            pltpu.VMEM((QW, rows), BF16),
        ],
        compiler_params=pltpu.CompilerParams(vmem_limit_bytes=48 << 20),
        name="finish",
    )(meta, tokens, packed, gq, dkv, gres, gb, low, gain, inner, outer)


def pack(w_query, w_keyval, w_out, w_gateup, w_down, norm_gains):
    rows = w_query.shape[0]
    spread = [jnp.broadcast_to(norm_gains[:, g : g + 1], (rows, 128)) for g in range(2)]
    packed = jnp.concatenate(
        [w_query, w_keyval[:, 0], spread[0], w_out, w_keyval[:, 1], spread[1]], axis=1
    )
    return packed.astype(BF16), w_gateup.reshape(rows, 2 * FF).astype(BF16), w_down.astype(BF16)


def for_sending(value):
    return jax.tree.map(lambda a: a.astype(jnp.bfloat16) if a.dtype == jnp.float32 else a, value)


def orthogonal(matrix):
    flipped = matrix.shape[0] > matrix.shape[1]
    iterate = matrix.T if flipped else matrix
    iterate = iterate / (jnp.sqrt(jnp.sum(iterate * iterate)) + 1e-07)
    for turn in range(NS_STEPS):
        gram_matrix = jnp.dot(iterate, iterate.T, precision=lax.Precision.HIGHEST)
        polynomial = COEF_B * gram_matrix + COEF_C * jnp.dot(
            gram_matrix, gram_matrix, precision=lax.Precision.HIGHEST
        )
        iterate = COEF_A * iterate + jnp.dot(polynomial, iterate, precision=lax.Precision.HIGHEST)
    return iterate.T if flipped else iterate


def muon_step(matrix):
    return MUON_RATE * math.sqrt(max(matrix.shape[0], matrix.shape[1])) * orthogonal(matrix)


def owner_branch(matrix_rows, matrix_cols, widest, received):
    group_size = received.shape[0]
    shard_size = matrix_rows * matrix_cols // group_size
    full_matrix = received[:, :shard_size].reshape(matrix_rows, matrix_cols)
    update_rows = muon_step(full_matrix).reshape(group_size, shard_size)
    return jnp.pad(update_rows, ((0, 0), (0, widest - shard_size)))


def zero_branch(received):
    return jnp.zeros_like(received)


def muon_exchange(pieces):
    fsdp_size, fsdp_index = lax.axis_size("fsdp"), lax.axis_index("fsdp")
    flat_sizes = [piece.size for piece in pieces]
    widest = max(flat_sizes)
    padded = [jnp.pad(piece.reshape(-1), (0, widest - piece.size)) for piece in pieces]
    outgoing = jnp.stack(padded + [jnp.zeros((widest,), F32)] * (fsdp_size - len(pieces)))
    received = lax.all_to_all(
        outgoing.astype(BF16), "fsdp", split_axis=0, concat_axis=0, tiled=True
    ).astype(F32)
    branches = [
        partial(owner_branch, piece.shape[0] * fsdp_size, piece.shape[1], widest)
        for piece in pieces
    ] + [zero_branch]
    update_rows = lax.switch(jnp.minimum(fsdp_index, len(pieces)), branches, received)
    returned = lax.all_to_all(
        update_rows.astype(BF16), "fsdp", split_axis=0, concat_axis=0, tiled=True
    ).astype(F32)
    return [returned[m, : flat_sizes[m]].reshape(pieces[m].shape) for m in range(len(pieces))]


def gather_rows_xla(shard):
    return lax.all_gather(shard, "fsdp", axis=0, tiled=True)


def reduce_rows_xla(grads):
    return lax.psum(lax.psum_scatter(grads, "fsdp", scatter_dimension=0, tiled=True), "dp")


class Place:
    def __init__(self, lines):
        self.f, self.d = lax.axis_index("fsdp"), lax.axis_index("dp")
        self.line, self.column = self.f // 2, self.f % 2
        self.x, self.core = self.d // 2, self.d % 2
        self.lines = lines
        self.sibling = (self.f, self.d + 1 - 2 * self.core)
        self.across = (self.f, self.core + 2 * (1 - self.x))
        self.beside = (self.f + 1 - 2 * self.column, self.d)
        self.above = (self.f + 2, self.d)
        self.below = (self.f - 2, self.d)


def remote(source, target, send_sem, recv_sem, device):
    return pltpu.make_async_remote_copy(
        src_ref=source, dst_ref=target, send_sem=send_sem, recv_sem=recv_sem,
        device_id=device, device_id_type=pl.DeviceIdType.MESH,
    )


def greet(place, chips=True):
    barrier = pltpu.get_barrier_semaphore()

    def signal(device):
        pl.semaphore_signal(barrier, inc=1, device_id=device, device_id_type=pl.DeviceIdType.MESH)

    signal(place.sibling)
    signal(place.across)
    if not chips:
        pl.semaphore_wait(barrier, 2)
        return
    signal(place.beside)
    pl.when(place.line > 0)(lambda: signal(place.below))
    pl.when(place.line < place.lines - 1)(lambda: signal(place.above))
    ends = (place.line == 0).astype(jnp.int32) + (place.line == place.lines - 1).astype(jnp.int32)
    pl.semaphore_wait(barrier, 5 - ends)


PARTS = 4


def half_parts(packed, gateup, down, core):
    wide, tall = packed.shape[1] // 2, down.shape[0] // 2
    at = core * FF
    return (
        packed.at[:, pl.ds(pl.multiple_of(core * wide, 128), wide)],
        gateup.at[:, pl.ds(pl.multiple_of(at, 128), FF // 2)],
        gateup.at[:, pl.ds(pl.multiple_of(at + FF // 2, 128), FF // 2)],
        down.at[pl.ds(pl.multiple_of(core * tall, 16), tall), :],
    )


def gather_kernel(
    lines, wq_ref, wkv_ref, wo_ref, wgu_ref, wd_ref, gains_ref, a_out, gu_out, d_out, a_ref, gu_ref, d_ref,
    own_sem, in_sem, pair_sem, up_sem, down_sem, side_sem, cross_sem, mate_sem,
):
    place = Place(lines)
    rows = a_ref.shape[0]
    for side, w_ref in enumerate((wq_ref, wo_ref)):
        at = side * O_AT
        a_ref[:, at : at + QW] = w_ref[...].astype(BF16)
        a_ref[:, at + QW : at + HALF] = wkv_ref[:, side, :].astype(BF16)
        spread = jnp.broadcast_to(gains_ref[:, side : side + 1], (rows, 128))
        a_ref[:, at + HALF : at + O_AT] = spread.astype(BF16)
        gu_ref[:, side * FF : side * FF + FF] = wgu_ref[:, side, :].astype(BF16)
    d_ref[...] = wd_ref[...].astype(BF16)
    own = [
        pltpu.make_async_copy(src, dst.at[place.f], own_sem.at[i])
        for i, (src, dst) in enumerate(((a_ref, a_out), (gu_ref, gu_out), (d_ref, d_out)))
    ]
    for copy in own:
        copy.start()
    greet(place)

    def full(shard, core):
        return half_parts(a_out.at[shard], gu_out.at[shard], d_out.at[shard], core)

    mine = half_parts(a_ref, gu_ref, d_ref, place.core)

    def send(shard, k, sems, device, recv, source=None):
        target = full(shard, place.core)[k]
        return remote(target if source is None else source, target, sems.at[shard, k], recv.at[shard, k], device)

    def arrived(shard, k):
        send(shard, k, up_sem, place.sibling, in_sem).wait_recv()

    def to_pair(shard, k):
        return send(shard, k, mate_sem, place.sibling, pair_sem)

    def on_z(t, k, action):
        if t == 0:
            pl.when(place.line < lines - 1)(
                lambda: action(send(place.f, k, up_sem, place.above, in_sem, mine[k]))
            )
            pl.when(place.line > 0)(
                lambda: action(send(place.f, k, down_sem, place.below, in_sem, mine[k]))
            )
            pl.when(place.x == k % 2)(
                lambda: action(send(place.f, k, side_sem, place.beside, in_sem, mine[k]))
            )
            return
        for sign in (-1, 1):
            shard = place.f + 2 * sign * t
            there = place.line + sign * t

            def go(shard=shard, sign=sign):
                action(None, shard)
                if sign < 0:
                    pl.when(place.line < lines - 1)(
                        lambda: action(send(shard, k, up_sem, place.above, in_sem))
                    )
                else:
                    pl.when(place.line > 0)(
                        lambda: action(send(shard, k, down_sem, place.below, in_sem))
                    )
                pl.when(place.x == k % 2)(
                    lambda: action(send(shard, k, side_sem, place.beside, in_sem))
                )
                action(to_pair(shard, k))

            pl.when((there >= 0) & (there < lines))(go)

    def others(t, run):
        base = place.beside[0]
        if t == 0:
            run(base)
            return
        for sign in (-1, 1):
            there = place.line + sign * t
            pl.when((there >= 0) & (there < lines))(lambda sign=sign: run(base + 2 * sign * t))

    def on_side(t, k, action):
        def run(shard):
            action(None, shard)
            action(send(shard, k, cross_sem, place.across, in_sem))
            action(to_pair(shard, k))

        pl.when(place.x == k % 2)(lambda: others(t, run))

    def on_cross(t, k, action):
        def run(shard):
            action(None, shard)
            action(to_pair(shard, k))

        pl.when(place.x != k % 2)(lambda: others(t, run))

    def start(k):
        def action(copy, shard=None):
            if copy is None:
                arrived(shard, k)
            else:
                copy.start()

        return action

    def finish_send(copy, shard=None):
        if copy is not None:
            copy.wait_send()

    for t in range(lines + 2):
        for k in range(PARTS):
            if t < lines:
                on_z(t, k, start(k))
            if 0 <= t - 1 < lines:
                on_side(t - 1, k, start(k))
            if 0 <= t - 2 < lines:
                on_cross(t - 2, k, start(k))
    for t in range(lines):
        for k in range(PARTS):
            on_z(t, k, finish_send)
            on_side(t, k, finish_send)
            on_cross(t, k, finish_send)
            pair_half = 1 - place.core

            def got(shard, k=k):
                target = full(shard, pair_half)[k]
                remote(target, target, mate_sem.at[shard, k], pair_sem.at[shard, k], place.sibling).wait_recv()

            others(t, got)
            if t > 0:
                for sign in (-1, 1):
                    there = place.line + sign * t
                    pl.when((there >= 0) & (there < lines))(
                        lambda sign=sign: got(place.f + 2 * sign * t)
                    )
    for copy in own:
        copy.wait()


def gather_weights_remote(weights, gains, count):
    rows, tall = weights[0].shape[0], weights[4].shape[0]
    sems = pltpu.SemaphoreType.DMA((count, PARTS))
    shapes = ((rows, WIDE_A), (rows, 2 * FF), (tall, D))
    return pl.pallas_call(
        partial(gather_kernel, count // 2),
        out_shape=tuple(jax.ShapeDtypeStruct((count,) + s, BF16) for s in shapes),
        in_specs=vmem(6),
        out_specs=(pl.BlockSpec(memory_space=pl.ANY),) * 3,
        scratch_shapes=[pltpu.VMEM(s, BF16) for s in shapes]
        + [pltpu.SemaphoreType.DMA((3,))]
        + [sems] * 7,
        compiler_params=pltpu.CompilerParams(
            collective_id=0, has_side_effects=True, vmem_limit_bytes=32 << 20
        ),
        name="gather_weights",
    )(*weights, gains)


CUTS = 3


def gather_keyval_kernel(kv_ref, out_ref, own_sem, in_sem, pair_sem, cross_send, mate_send):
    place = Place(4)
    piece = kv_ref.shape[0] // CUTS
    own = pltpu.make_async_copy(kv_ref, out_ref.at[place.d], own_sem)
    own.start()
    greet(place, False)
    far = place.across[1]
    near = place.sibling[1]

    def rows(k):
        return pl.ds(k * piece, piece)

    crossing = [
        remote(kv_ref.at[rows(k)], out_ref.at[place.d, rows(k)], cross_send.at[k], in_sem.at[k], place.across)
        for k in range(CUTS)
    ]
    pairing = remote(kv_ref, out_ref.at[place.d], mate_send.at[CUTS], pair_sem.at[CUTS], place.sibling)
    for copy in crossing:
        copy.start()
    pairing.start()
    passing = []
    for k in range(CUTS):
        crossing[k].wait_recv()
        here = out_ref.at[far, rows(k)]
        copy = remote(here, here, mate_send.at[k], pair_sem.at[k], place.sibling)
        copy.start()
        passing.append(copy)
    pairing.wait()
    for k in range(CUTS):
        crossing[k].wait_send()
        passing[k].wait()
    own.wait()


def gather_keyval_remote(keyval):
    return pl.pallas_call(
        gather_keyval_kernel,
        out_shape=jax.ShapeDtypeStruct((4,) + keyval.shape, keyval.dtype),
        in_specs=[pl.BlockSpec(memory_space=pl.ANY)],
        out_specs=pl.BlockSpec(memory_space=pl.ANY),
        scratch_shapes=[
            pltpu.SemaphoreType.DMA,
            pltpu.SemaphoreType.DMA((CUTS,)),
            pltpu.SemaphoreType.DMA((CUTS + 1,)),
            pltpu.SemaphoreType.DMA((CUTS,)),
            pltpu.SemaphoreType.DMA((CUTS + 1,)),
        ],
        compiler_params=pltpu.CompilerParams(collective_id=1, has_side_effects=True),
        name="gather_keyval",
    )(keyval).reshape(4 * keyval.shape[0], keyval.shape[1])


def added(one, two):
    return one.astype(F32) + two.astype(F32)


def reduce_keyval_kernel(part_ref, out_ref, pair_s, far_s, cross_s, pair_recv, cross_recv, pair_send, cross_send):
    place = Place(4)
    greet(place, False)
    piece = out_ref.shape[0] // CUTS
    far = place.across[1]
    near_core = 1 - place.core
    targets = (near_core + 2 * (1 - place.x), near_core + 2 * place.x)

    def rows(k):
        return pl.ds(k * piece, piece)

    pairing = [
        [
            remote(part_ref.at[targets[w], rows(k)], pair_s.at[w, rows(k)], pair_send.at[w, k], pair_recv.at[w, k], place.sibling)
            for k in range(CUTS)
        ]
        for w in range(2)
    ]
    for w in range(2):
        for copy in pairing[w]:
            copy.start()
    crossing = []
    for k in range(CUTS):
        pairing[0][k].wait_recv()
        far_s[rows(k)] = added(part_ref[far, rows(k)], pair_s[0, rows(k)]).astype(BF16)
        copy = remote(far_s.at[rows(k)], cross_s.at[rows(k)], cross_send.at[k], cross_recv.at[k], place.across)
        copy.start()
        crossing.append(copy)
    for k in range(CUTS):
        pairing[1][k].wait_recv()
        crossing[k].wait_recv()
        mine = added(part_ref[place.d, rows(k)], pair_s[1, rows(k)])
        out_ref[rows(k)] = (mine + cross_s[rows(k)].astype(F32)).astype(BF16)
    for k in range(CUTS):
        pairing[0][k].wait_send()
        pairing[1][k].wait_send()
        crossing[k].wait_send()


def reduce_keyval_remote(dkv):
    rows, width = dkv.shape[0] // 4, dkv.shape[1]
    return pl.pallas_call(
        reduce_keyval_kernel,
        out_shape=jax.ShapeDtypeStruct((rows, width), BF16),
        in_specs=vmem(1),
        out_specs=vmem(1)[0],
        scratch_shapes=[
            pltpu.VMEM((2, rows, width), BF16),
            pltpu.VMEM((rows, width), BF16),
            pltpu.VMEM((rows, width), BF16),
            pltpu.SemaphoreType.DMA((2, CUTS)),
            pltpu.SemaphoreType.DMA((CUTS,)),
            pltpu.SemaphoreType.DMA((2, CUTS)),
            pltpu.SemaphoreType.DMA((CUTS,)),
        ],
        compiler_params=pltpu.CompilerParams(
            collective_id=2, has_side_effects=True, vmem_limit_bytes=32 << 20
        ),
        name="reduce_keyval",
    )(dkv.reshape(4, rows, width))


def visit_order(lines):
    return [sorted(range(lines), key=lambda other: (-abs(other - line), -other)) for line in range(lines)]


def sum_kernel(
    lines, a_ref, gu_ref, d_ref, a_out, gu_out, d_out,
    a_s, gu_s, d_s, a_in, gu_in, d_in, pair_recv, recv, last_recv, pair_send, send, last_send,
):
    place = Place(lines)
    greet(place)
    order_table = visit_order(lines)
    home = lines * 2

    def order(t):
        spot = jnp.int32(0)
        for line in range(lines):
            spot = spot + order_table[line][t] * (place.line == line).astype(jnp.int32)
        return spot

    def pieces(shard, core):
        return half_parts(a_ref.at[shard], gu_ref.at[shard], d_ref.at[shard], core)

    def running(shard):
        half = FF // 2
        return (
            a_s.at[shard], gu_s.at[shard, :, pl.ds(0, half)], gu_s.at[shard, :, pl.ds(half, half)],
            d_s.at[shard],
        )

    def inbox(way, spot):
        half = FF // 2
        return (
            a_in.at[way, spot], gu_in.at[way, spot, :, pl.ds(0, half)],
            gu_in.at[way, spot, :, pl.ds(half, half)], d_in.at[way, spot],
        )

    def to_pair(shard, k):
        return remote(
            pieces(shard, 1 - place.core)[k], running(shard)[k],
            pair_send.at[shard, k], pair_recv.at[shard, k], place.sibling,
        )

    def pass_on(shard, k, way, spot, device):
        return remote(
            running(shard)[k], inbox(way, spot)[k], send.at[way, spot, k], recv.at[way, spot, k], device
        )

    def add(shard, k, other):
        total = running(shard)[k]
        total[...] = added(total[...], other[...]).astype(BF16)

    def collect(shard, k, way, spot):
        pass_on(shard, k, way, spot, place.sibling).wait_recv()
        add(shard, k, inbox(way, spot)[k])

    def first_sum(shard, k):
        to_pair(shard, k).wait_recv()
        add(shard, k, pieces(shard, place.core)[k])

    def stage_pair(t):
        spot = order(t)
        shard = 2 * spot + 1 - place.column
        for k in range(PARTS):
            first_sum(shard, k)
            pl.when(place.x != k % 2)(lambda k=k: pass_on(shard, k, 0, spot, place.across).start())

    def stage_side(t):
        spot = order(t)
        shard = 2 * spot + 1 - place.column
        for k in range(PARTS):

            def go(k=k):
                collect(shard, k, 0, spot)
                pass_on(shard, k, 1, spot, place.beside).start()

            pl.when(place.x == k % 2)(go)
        for k in range(PARTS):
            first_sum(2 * spot + place.column, k)

    def stage_line(t):
        spot = order(t)
        shard = 2 * spot + place.column
        for k in range(PARTS):
            pl.when(place.x == k % 2)(lambda k=k: collect(shard, k, 1, spot))

            def up(k=k):
                pl.when(place.line > 0)(lambda: collect(shard, k, 2, spot))
                pass_on(shard, k, 2, spot, place.above).start()

            def down(k=k):
                pl.when(place.line < lines - 1)(lambda: collect(shard, k, 3, spot))
                pass_on(shard, k, 3, spot, place.below).start()

            if t < lines - 1:
                pl.when(spot > place.line)(up)
                pl.when(spot < place.line)(down)
            else:
                pl.when(place.line > 0)(lambda k=k: collect(shard, k, 2, spot))
                pl.when(place.line < lines - 1)(lambda k=k: collect(shard, k, 3, spot))
                last(k).start()

    def last(k):
        return remote(
            running(place.f)[k], inbox(4, 0)[k], last_send.at[0, k], last_recv.at[0, k], place.across
        )

    def share(k):
        target = half_parts(a_out, gu_out, d_out, place.core)[k]
        return remote(target, target, last_send.at[1, k], last_recv.at[1, k], place.sibling)

    for t in range(lines):
        spot = order(t)
        for column in (1 - place.column, place.column):
            for k in range(PARTS):
                to_pair(2 * spot + column, k).start()
    for t in range(lines + 2):
        if t < lines:
            stage_pair(t)
        if 0 <= t - 1 < lines:
            stage_side(t - 1)
        if 0 <= t - 2 < lines:
            stage_line(t - 2)
    for k in range(PARTS):
        last(k).wait_recv()
        target = half_parts(a_out, gu_out, d_out, place.core)[k]
        target[...] = added(running(place.f)[k][...], inbox(4, 0)[k][...]).astype(BF16)
        share(k).start()
    for k in range(PARTS):
        target = half_parts(a_out, gu_out, d_out, 1 - place.core)[k]
        remote(target, target, last_send.at[1, k], last_recv.at[1, k], place.sibling).wait_recv()
        share(k).wait_send()
        last(k).wait_send()
    for t in range(lines):
        spot = order(t)
        for k in range(PARTS):
            for column in range(2):
                to_pair(2 * spot + column, k).wait_send()
            shard = 2 * spot + 1 - place.column
            pl.when(place.x != k % 2)(lambda k=k: pass_on(shard, k, 0, spot, place.across).wait_send())
            pl.when(place.x == k % 2)(lambda k=k: pass_on(shard, k, 1, spot, place.beside).wait_send())
            if t < lines - 1:
                shard = 2 * spot + place.column
                pl.when(spot > place.line)(lambda k=k: pass_on(shard, k, 2, spot, place.above).wait_send())
                pl.when(spot < place.line)(lambda k=k: pass_on(shard, k, 3, spot, place.below).wait_send())


def reduce_grads_remote(grads, count):
    lines = count // 2
    grads = tuple(g.reshape(count, g.shape[0] // count, g.shape[1]) for g in grads)
    a_shape, gu_shape, d_shape = (g.shape[1:] for g in grads)
    halves = ((a_shape[0], a_shape[1] // 2), (gu_shape[0], FF), (d_shape[0] // 2, d_shape[1]))
    return pl.pallas_call(
        partial(sum_kernel, lines),
        out_shape=tuple(jax.ShapeDtypeStruct(g.shape[1:], BF16) for g in grads),
        in_specs=vmem(3),
        out_specs=tuple(vmem(3)),
        scratch_shapes=[pltpu.VMEM((count,) + h, BF16) for h in halves]
        + [pltpu.VMEM((5, lines) + h, BF16) for h in halves]
        + [
            pltpu.SemaphoreType.DMA((count, PARTS)),
            pltpu.SemaphoreType.DMA((4, lines, PARTS)),
            pltpu.SemaphoreType.DMA((2, PARTS)),
            pltpu.SemaphoreType.DMA((count, PARTS)),
            pltpu.SemaphoreType.DMA((4, lines, PARTS)),
            pltpu.SemaphoreType.DMA((2, PARTS)),
        ],
        compiler_params=pltpu.CompilerParams(
            collective_id=3, has_side_effects=True, vmem_limit_bytes=60 << 20
        ),
        name="sum_grads",
    )(*grads)


def own_kernels():
    return lax.axis_size("fsdp") == 8 and lax.axis_size("dp") == 4


def gather_weights(weights, gains):
    if not own_kernels():
        return tuple(gather_rows_xla(s) for s in pack(*weights, gains))
    full = gather_weights_remote(weights, gains, lax.axis_size("fsdp"))
    return tuple(f.reshape(f.shape[0] * f.shape[1], f.shape[2]) for f in full)


def gather_keyval(keyval):
    if not own_kernels():
        return lax.all_gather(keyval, "dp", axis=0, tiled=True)
    return gather_keyval_remote(keyval)


def reduce_keyval(dkv):
    if not own_kernels():
        return lax.psum_scatter(dkv, "dp", scatter_dimension=0, tiled=True)
    return reduce_keyval_remote(dkv)


def reduce_grads(grads):
    if not own_kernels():
        return tuple(reduce_rows_xla(g) for g in grads)
    return reduce_grads_remote(grads, lax.axis_size("fsdp"))


WIDE_AT, TALL_AT = (2, 5), 3
SQUARE_AT, NARROW_AT = (0, 7), (6, 1)
NARROW = 256


def by_core(pair, core):
    return pair[0] + (pair[1] - pair[0]) * core


def greet_plane(place, count):
    barrier = pltpu.get_barrier_semaphore()
    pl.semaphore_signal(barrier, inc=1, device_id=place.sibling, device_id_type=pl.DeviceIdType.MESH)
    for step in range(1, count):
        f = lax.rem(place.f + step, count)
        for core in range(2):
            pl.semaphore_signal(
                barrier, inc=1, device_id=(f, 2 * place.x + core), device_id_type=pl.DeviceIdType.MESH
            )
    pl.semaphore_wait(barrier, 2 * count - 1)


def newton_schulz(x_s, low_s, gram_s, gram_low_s, poly_s):
    size, width = x_s.shape
    cuts = [(at, min(256, size - at)) for at in range(0, size, 256)]

    @pl.loop(0, NS_STEPS)
    def _(step):
        shift = jnp.where(step >= NS_STEPS - 2, 1.0, 0.0)
        for at, wide in cuts:
            gram = dot_nt(low_s[...], low_s[at : at + wide, :])
            row = lax.broadcasted_iota(jnp.int32, (size, wide), 0)
            column = lax.broadcasted_iota(jnp.int32, (size, wide), 1) + at
            gram = gram - jnp.where(row == column, shift, 0.0)
            gram_s[:, at : at + wide] = gram
            gram_low_s[:, at : at + wide] = gram.astype(BF16)
        for at, wide in cuts:
            square = dot(gram_low_s[...], gram_low_s[:, at : at + wide])
            poly = (COEF_B + 2.0 * COEF_C * shift) * gram_s[:, at : at + wide] + COEF_C * square
            poly_s[:, at : at + wide] = poly.astype(BF16)
        keep = COEF_A + COEF_B * shift + COEF_C * shift * shift
        for at in range(0, width, 256):
            lanes = slice(at, at + 256)
            new = keep * x_s[:, lanes] + dot(poly_s[...], low_s[:, lanes])
            x_s[:, lanes] = new
            low_s[:, lanes] = new.astype(BF16)


def muon_kernel(
    count, a_ref, gu_ref, d_ref, mq_ref, mkv_ref, mo_ref, mgu_ref, md_ref,
    sq_out, nk_out, gu_out, d_out,
    my_gu, my_sq, my_nk, my_d, wide_s, sq_s, nk_s, tall_s, x_s, low_s, gram_s, gram_low_s, poly_s,
    in_send, in_recv, own_sem, out_send, out_recv, pair_send, pair_recv,
):
    place = Place(count // 2)
    greet_plane(place, count)
    rows, tall = my_gu.shape[0], my_d.shape[0]

    def moment(momentum, grad):
        return (MOMENTUM_DECAY * momentum + grad.astype(F32)).astype(BF16)

    my_nk[...] = jnp.zeros_like(my_nk)

    def moments_of(core, m_square):
        my_gu[...] = moment(mgu_ref[:, core, :], gu_ref[:, core * FF : core * FF + FF])
        at = core * O_AT
        my_sq[...] = moment(m_square[...], a_ref[:, at : at + QW])
        my_nk[:, :KVW] = moment(mkv_ref[:, core, :], a_ref[:, at + QW : at + HALF])
        part = slice(core * tall, (core + 1) * tall)
        my_d[...] = moment(md_ref[part, :], d_ref[part, :])

    pl.when(place.core == 0)(lambda: moments_of(0, mq_ref))
    pl.when(place.core == 1)(lambda: moments_of(1, mo_ref))

    tall_rows = pl.ds(pl.multiple_of(place.core * tall, 16), tall)
    wide_at, sq_at, nk_at = (by_core(p, place.core) for p in (WIDE_AT, SQUARE_AT, NARROW_AT))
    tall_core = 2 * place.x
    routes = (
        (my_gu, wide_s.at[place.f], wide_at, place.d),
        (my_d, tall_s.at[place.f, tall_rows], TALL_AT, tall_core),
        (my_sq, sq_s.at[place.f], sq_at, place.d),
        (my_nk, nk_s.at[place.f], nk_at, place.d),
    )

    def each_route(far, near):
        for i, (source, target, f, d) in enumerate(routes):
            here = (place.f == f) & (place.d == d)
            recv = in_recv.at[i, place.f] if i != 1 else in_recv.at[i, place.f + count * place.core]
            pl.when(jnp.logical_not(here))(
                lambda i=i, source=source, target=target, f=f, d=d, recv=recv: far(
                    remote(source, target, in_send.at[i], recv, (f, d))
                )
            )
            pl.when(here)(
                lambda i=i, source=source, target=target: near(
                    pltpu.make_async_copy(source, target, own_sem.at[i])
                )
            )

    each_route(lambda copy: copy.start(), lambda copy: copy.start())
    each_route(lambda copy: copy.wait_send(), lambda copy: copy.wait())

    def received(i, slot_of):
        for step in range(1, count):
            f = lax.rem(place.f + step, count)
            target = slot_of(f)
            remote(target, target, in_send.at[i], in_recv.at[i, f], place.sibling).wait_recv()

    def received_tall():
        for step in range(count):
            f = lax.rem(place.f + step, count)
            for core in range(2):
                if step == 0 and core == 0:
                    continue
                target = tall_s.at[f, pl.ds(core * tall, tall)]
                remote(target, target, in_send.at[1], in_recv.at[1, f + count * core], place.sibling).wait_recv()

    def scaled():
        total = jnp.zeros((1, 1), F32)
        for at in range(0, FF, 256):
            part = x_s[:, at : at + 256]
            total = total + jnp.sum(jnp.sum(part * part, axis=0, keepdims=True), axis=1, keepdims=True)
        factor = 1.0 / (jnp.sqrt(total) + 1e-07)
        for at in range(0, FF, 256):
            part = x_s[:, at : at + 256] * factor
            x_s[:, at : at + 256] = part
            low_s[:, at : at + 256] = part.astype(BF16)

    is_wide, is_square, is_narrow = (place.f == at for at in (wide_at, sq_at, nk_at))
    is_tall = (place.f == TALL_AT) & (place.core == 0)
    is_small = is_square | is_narrow

    @pl.when(is_wide)
    def _():
        received(0, lambda f: wide_s.at[f])
        for f in range(count):
            x_s[f * rows : (f + 1) * rows, :] = wide_s[f].astype(F32)

    @pl.when(is_tall)
    def _():
        received_tall()
        for f in range(0, count, 2):
            pair = jnp.concatenate([tall_s[f], tall_s[f + 1]], axis=0).astype(F32)
            x_s[:, 2 * f * tall : 2 * (f + 2) * tall] = pair.T

    @pl.when(is_small)
    def _():
        x_s[...] = jnp.zeros_like(x_s)

    @pl.when(is_square)
    def _():
        received(2, lambda f: sq_s.at[f])
        for f in range(count):
            x_s[f * rows : (f + 1) * rows, :QW] = sq_s[f].astype(F32)

    @pl.when(is_narrow)
    def _():
        received(3, lambda f: nk_s.at[f])
        for f in range(count):
            x_s[f * rows : (f + 1) * rows, :NARROW] = nk_s[f].astype(F32)

    @pl.when(is_wide | is_tall | is_small)
    def _():
        scaled()
        newton_schulz(x_s, low_s, gram_s, gram_low_s, poly_s)

    rate = MUON_RATE * math.sqrt(FF)
    small_rate = MUON_RATE * math.sqrt(D)

    def back(i, f, core):
        source = (
            wide_s.at[f], tall_s.at[f, pl.ds(core * tall, tall)] if i == 1 else None, sq_s.at[f], nk_s.at[f],
        )[i]
        return source, landing(i, core), (f, 2 * place.x + core)

    def landing(i, core):
        if i == 1:
            start = core * tall if isinstance(core, int) else pl.multiple_of(core * tall, 16)
            return d_out.at[pl.ds(start, tall)]
        return (gu_out, None, sq_out, nk_out)[i].at[core]

    def give(i, cores, act):
        for step in range(count):
            f = lax.rem(place.f + step, count)
            for n, core in enumerate(cores):
                source, target, device = back(i, f, core)
                if step == 0 and n == 0:
                    copy = pltpu.make_async_copy(source, target, own_sem.at[i])
                    act(copy, True)
                else:
                    slot = f + count * n
                    act(remote(source, target, out_send.at[i, slot], out_recv.at[i], device), False)

    def given(i, cores):
        give(i, cores, lambda copy, own: copy.start())
        give(i, cores, lambda copy, own: copy.wait() if own else copy.wait_send())

    @pl.when(is_wide)
    def _():
        for f in range(count):
            wide_s[f] = (x_s[f * rows : (f + 1) * rows, :] * rate).astype(BF16)
        given(0, (place.core,))

    @pl.when(is_tall)
    def _():
        for f in range(0, count, 2):
            pair = (x_s[:, 2 * f * tall : 2 * (f + 2) * tall] * rate).T
            tall_s[f] = pair[: 2 * tall].astype(BF16)
            tall_s[f + 1] = pair[2 * tall :].astype(BF16)
        given(1, (0, 1))

    @pl.when(is_square)
    def _():
        for f in range(count):
            sq_s[f] = (x_s[f * rows : (f + 1) * rows, :QW] * small_rate).astype(BF16)
        given(2, (place.core,))

    @pl.when(is_narrow)
    def _():
        for f in range(count):
            nk_s[f] = (x_s[f * rows : (f + 1) * rows, :NARROW] * small_rate).astype(BF16)
        given(3, (place.core,))

    makers = (is_wide, is_tall, is_square, is_narrow)

    def hand_over(i, core):
        target = landing(i, core)
        return remote(target, target, pair_send.at[i], pair_recv.at[i], place.sibling)

    for i in (2, 3, 1, 0):
        target = landing(i, place.core)

        def take(i=i, target=target):
            remote(target, target, pair_send.at[i], out_recv.at[i], place.sibling).wait_recv()

        pl.when(jnp.logical_not(makers[i]))(take)
        hand_over(i, place.core).start()
    for i in range(4):
        hand_over(i, 1 - place.core).wait_recv()
        hand_over(i, place.core).wait_send()


def muon_remote(grads, momenta, count):
    rows, tall = grads[0].shape[0], grads[2].shape[0] // 2
    pieces = ((rows, FF), (rows, QW), (rows, NARROW), (tall, D))
    return pl.pallas_call(
        partial(muon_kernel, count),
        out_shape=(
            jax.ShapeDtypeStruct((2, rows, QW), BF16),
            jax.ShapeDtypeStruct((2, rows, NARROW), BF16),
            jax.ShapeDtypeStruct((2, rows, FF), BF16),
            jax.ShapeDtypeStruct((2 * tall, D), BF16),
        ),
        in_specs=vmem(8),
        out_specs=tuple(vmem(4)),
        scratch_shapes=[pltpu.VMEM(p, BF16) for p in pieces]
        + [pltpu.VMEM((count,) + p, BF16) for p in pieces[:3]]
        + [
            pltpu.VMEM((count, 2 * tall, D), BF16),
            pltpu.VMEM((D, FF), F32),
            pltpu.VMEM((D, FF), BF16),
            pltpu.VMEM((D, D), F32),
            pltpu.VMEM((D, D), BF16),
            pltpu.VMEM((D, D), BF16),
            pltpu.SemaphoreType.DMA((4,)),
            pltpu.SemaphoreType.DMA((4, 2 * count)),
            pltpu.SemaphoreType.DMA((4,)),
            pltpu.SemaphoreType.DMA((4, 2 * count)),
            pltpu.SemaphoreType.DMA((4,)),
            pltpu.SemaphoreType.DMA((4,)),
            pltpu.SemaphoreType.DMA((4,)),
        ],
        compiler_params=pltpu.CompilerParams(
            collective_id=4, has_side_effects=True, vmem_limit_bytes=56 << 20
        ),
        name="muon",
    )(*grads, *momenta)


def outputs_kernel(
    gain_rate, a_ref, gu_ref, d_ref, sq_ref, nk_ref, ugu_ref, ud_ref,
    gains_ref, gainm_ref, wq_ref, wkv_ref, wo_ref, wgu_ref, wd_ref,
    mq_ref, mkv_ref, mo_ref, mgu_ref, md_ref,
    gg_ref, gm_ref, gv_ref, qg_ref, qm_ref, qn_ref, kvg_ref, kvm_ref, kvn_ref,
    og_ref, om_ref, on_ref, gug_ref, gum_ref, gun_ref, dg_ref, dm_ref, dn_ref,
):
    rows = a_ref.shape[0]

    def write(grad, momentum, weight, update, outs, index):
        grad = grad.astype(F32)
        outs[0][index] = grad
        outs[1][index] = MOMENTUM_DECAY * momentum[index] + grad
        outs[2][index] = weight[index] - update.astype(F32)

    every = (slice(None), slice(None))
    write(a_ref[:, :QW], mq_ref, wq_ref, sq_ref[0], (qg_ref, qm_ref, qn_ref), every)
    write(a_ref[:, O_AT : O_AT + QW], mo_ref, wo_ref, sq_ref[1], (og_ref, om_ref, on_ref), every)
    write(d_ref[...], md_ref, wd_ref, ud_ref[...], (dg_ref, dm_ref, dn_ref), every)
    for side in range(2):
        index = (slice(None), side, slice(None))
        at = side * O_AT + QW
        write(a_ref[:, at : at + KVW], mkv_ref, wkv_ref, nk_ref[side, :, :KVW], (kvg_ref, kvm_ref, kvn_ref), index)
        write(gu_ref[:, side * FF : side * FF + FF], mgu_ref, wgu_ref, ugu_ref[side], (gug_ref, gum_ref, gun_ref), index)
    gain = jnp.where(
        lane_index(rows) == 0, a_ref[:, HALF:O_AT].astype(F32), a_ref[:, O_AT + HALF :].astype(F32)
    )[:, :2]
    moments = GAIN_DECAY * gainm_ref[...] + gain
    gg_ref[...] = gain
    gm_ref[...] = moments
    gv_ref[...] = gains_ref[...] - gain_rate * moments


def write_outputs(gain_rate, grads, updates, gains, gain_momentum, weights, momenta):
    shapes = [jax.ShapeDtypeStruct(gains.shape, F32)] * 3
    for w in weights:
        shapes += [jax.ShapeDtypeStruct(w.shape, F32)] * 3
    return pl.pallas_call(
        partial(outputs_kernel, gain_rate),
        out_shape=tuple(shapes),
        in_specs=vmem(19),
        out_specs=tuple(vmem(18)),
        compiler_params=pltpu.CompilerParams(vmem_limit_bytes=56 << 20),
        name="outputs",
    )(*grads, *updates, gains, gain_momentum, *weights, *momenta)


def muon_updates(grads, momenta):
    if own_kernels():
        return muon_remote(grads, momenta, lax.axis_size("fsdp"))
    packed, gateup, down = (g.astype(F32) for g in grads)
    m_query, m_keyval, m_out, m_gateup, m_down = momenta

    def moment(momentum, grad):
        return MOMENTUM_DECAY * momentum + grad

    steps = muon_exchange(
        [
            moment(m_query, packed[:, :QW]),
            moment(m_keyval[:, 0], packed[:, QW:HALF]),
            moment(m_keyval[:, 1], packed[:, O_AT + QW : O_AT + HALF]),
            moment(m_out, packed[:, O_AT : O_AT + QW]),
            moment(m_gateup[:, 0], gateup[:, :FF]),
            moment(m_gateup[:, 1], gateup[:, FF:]),
            moment(m_down, down),
        ]
    )
    return (
        jnp.stack([steps[0], steps[3]]).astype(BF16),
        jnp.pad(jnp.stack(steps[1:3]), ((0, 0), (0, 0), (0, NARROW - KVW))).astype(BF16),
        jnp.stack(steps[4:6]).astype(BF16),
        steps[6].astype(BF16),
    )


def local(
    tokens, cotangent, lengths, assignment, norm_gains, gain_momentum, w_query, w_keyval, w_out,
    w_gateup, w_down, m_query, m_keyval, m_out, m_gateup, m_down,
):
    slots = tokens.shape[0] // BLK
    gain_rate = GAIN_SCALE / math.sqrt(assignment.shape[1] * BLK * 3 // 4 * lax.axis_size("fsdp"))
    meta = block_meta(lengths[0], assignment[0], lax.axis_index("dp") * slots, slots)
    inner, outer = rope_constants()
    weights = (w_query, w_keyval, w_out, w_gateup, w_down)
    momenta = (m_query, m_keyval, m_out, m_gateup, m_down)
    packed, gateup, down = gather_weights(weights, norm_gains)
    queries, keyval = project(meta, tokens, packed, inner, outer)
    group_kv = gather_keyval(keyval)
    act, gres, gb, low, gq, dkv, d_gateup, d_down, gain = layer(
        meta, tokens, cotangent, queries, group_kv, packed, gateup, down, inner, outer
    )
    dkv = reduce_keyval(dkv)
    input_grad, d_packed = finish(
        meta, tokens, packed, gq, dkv, gres, gb, low, gain, inner, outer
    )
    grads = reduce_grads((d_packed, d_gateup, d_down))
    updates = muon_updates(grads, momenta)
    return (act, input_grad) + tuple(
        write_outputs(gain_rate, grads, updates, norm_gains, gain_momentum, weights, momenta)
    )


def solution(mesh):
    rows = P(("fsdp", "dp"), None)
    two, three = P("fsdp", None), P("fsdp", None, None)
    return jax.shard_map(
        local,
        mesh=mesh,
        in_specs=(rows, rows, two, two, two, two, two, three, two, three, two, two, three, two, three, two),
        out_specs=(rows, rows) + (two,) * 6 + (three,) * 3 + (two,) * 3 + (three,) * 3 + (two,) * 3,
        check_vma=False,
    )
```

```python
from functools import partial
import math

import jax
import jax.numpy as jnp
import numpy as np
from jax import lax
from jax.experimental import pallas as pl
from jax.experimental.pallas import tpu as pltpu
from jax.sharding import PartitionSpec as P

D = 576
HEADS = 9
KVH = 3
HD = 64
FF = 1536
BLK = 128
SEQS_G = 3
NS_STEPS = 5
QW = 576
KVW = 192
LONGEST = 12

EPS = 1e-05
THETA = 100000.0
MOMENTUM_DECAY = 0.95
GAIN_DECAY = 0.9
MUON_RATE = 0.03
GAIN_SCALE = 0.4
COEF_A = 3.4445
COEF_B = -4.775
COEF_C = 2.0315
SCALE = 1.0 / math.sqrt(HD)
HALF = 768
WIDE_A = 2 * (HALF + 128)
O_AT = HALF + 128
STEP = 256
F32, BF16 = jnp.float32, jnp.bfloat16


def vmem(count=1):
    return [pl.BlockSpec(memory_space=pltpu.VMEM)] * count


def dot(a, b):
    return lax.dot_general(a, b, (((1,), (0,)), ((), ())), preferred_element_type=F32)


def dot_nt(a, b):
    return lax.dot_general(a, b, (((1,), (1,)), ((), ())), preferred_element_type=F32)


def dot_tn(a, b):
    return lax.dot_general(a, b, (((0,), (0,)), ((), ())), preferred_element_type=F32)


META = 4 + LONGEST


def block_meta(lengths, assignment, first_slot, slots, meta):
    entries = assignment.shape[1]
    starts, sizes = [jnp.int32(0)], []
    for k in range(SEQS_G):
        sizes.append((lengths[0, k] + (BLK - 1)) // BLK)
        starts.append(starts[-1] + sizes[-1])

    @pl.loop(0, slots)
    def _(slot):
        mine = first_slot + slot

        def look(e, found):
            return jnp.where(assignment[0, e] == mine, e, found)

        entry = lax.fori_loop(0, entries, look, jnp.int32(0))
        first, size = entry, jnp.int32(0)
        for k in range(SEQS_G):
            inside = (entry >= starts[k]) & (entry < starts[k + 1])
            first = jnp.where(inside, starts[k], first)
            size = jnp.where(inside, lengths[0, k], size)
        place = entry - first
        meta[slot, 0] = place
        meta[slot, 1] = jnp.clip(size - place * BLK, 0, BLK)
        meta[slot, 2] = place // 2 + 1
        meta[slot, 3] = entry
        for step in range(LONGEST):
            key = assignment[0, jnp.minimum(first + step, entry)]
            meta[slot, 4 + step] = key


def rope_constants():
    freq = np.exp(np.arange(HD // 2, dtype=np.float64) * (-2.0 * math.log(THETA) / HD))
    lanes = np.tile(freq, 4)
    inner = np.arange(BLK)[:, None] * lanes[None, :]
    outer = BLK * np.arange(16)[:, None] * lanes[None, :]
    turned = inner.T[: HD // 2]
    steps = np.broadcast_to((BLK * np.arange(LONGEST))[:, None, None] * freq[None, :, None], (LONGEST, HD // 2, BLK))
    return tuple(
        np.stack([np.cos(angle), np.sin(angle)]).astype(np.float32)
        for angle in (inner, outer, turned, steps)
    )


def lane_index(rows):
    return lax.broadcasted_iota(jnp.int32, (rows, 128), 1)


def rope_tables(meta, slot, inner_ref, outer_ref):
    place, live = meta[slot, 0], meta[slot, 1]
    co, so = outer_ref[0, pl.ds(place, 1), :], outer_ref[1, pl.ds(place, 1), :]
    ci, si = inner_ref[0], inner_ref[1]
    lane = lane_index(BLK)
    row = lax.broadcasted_iota(jnp.int32, (BLK, 128), 0)
    turned = (row < live) & (lane < HD)
    cosine = jnp.where(turned, co * ci - so * si, 1.0)
    sine = jnp.where(turned, so * ci + co * si, 0.0)
    return cosine, jnp.where(lane < HD // 2, sine, 0.0), jnp.where(lane < HD // 2, 0.0, sine)


def rope(tile, tables):
    cosine, sine_low, sine_high = tables
    return (
        tile * cosine - pltpu.roll(tile, 128 - HD // 2, 1) * sine_low
        + pltpu.roll(tile, HD // 2, 1) * sine_high
    )


def rope_back(tile, tables):
    cosine, sine_low, sine_high = tables
    return (
        tile * cosine + pltpu.roll(tile, 128 - HD // 2, 1) * sine_low
        - pltpu.roll(tile, HD // 2, 1) * sine_high
    )


def swap(tile):
    return pltpu.roll(tile, HD, 1)


def gain_row(packed_ref, at):
    return packed_ref[:, at : at + 128].astype(F32).T[0:1, :]


def project_rows(meta, i, x_ref, wa_ref, gain, inner_ref, outer_ref, q_ref, kv_ref):
    low_lane = lane_index(BLK) < HD
    x = x_ref[i * STEP : (i + 1) * STEP, :].astype(F32)
    inv = lax.rsqrt(jnp.mean(x * x, axis=1, keepdims=True) + EPS)
    normed = (x * inv * gain).astype(BF16)
    qk = dot(normed, wa_ref[:, :HALF])
    ov = dot(normed, wa_ref[:, O_AT + 512 : O_AT + HALF])
    for b in range(STEP // BLK):
        tables = rope_tables(meta, i * (STEP // BLK) + b, inner_ref, outer_ref)
        rows = slice(i * STEP + b * BLK, i * STEP + (b + 1) * BLK)
        part = slice(b * BLK, (b + 1) * BLK)
        tiles = [qk[part, 128 * t : 128 * t + 128] for t in range(6)]
        for head in range(HEADS):
            tile = tiles[head // 2]
            tile = jnp.where(low_lane, swap(tile) if head % 2 else tile, 0.0)
            q_ref[rows, 128 * head : 128 * head + 128] = (rope(tile, tables) * SCALE).astype(BF16)
        values = [ov[part, :128], ov[part, 128:]]
        pairs = (
            (swap(tiles[4]), values[0]),
            (tiles[5], swap(values[1])),
            (swap(tiles[5]), values[1]),
        )
        for h in range(KVH):
            tile = jnp.where(low_lane, *pairs[h])
            kv_ref[rows, 128 * h : 128 * h + 128] = rope(tile, tables).astype(BF16)


def chunk_bias(meta, slot, chunk):
    key = lax.broadcasted_iota(jnp.int32, (2 * BLK, BLK), 0) + chunk * (2 * BLK)
    query = lax.broadcasted_iota(jnp.int32, (2 * BLK, BLK), 1) + meta[slot, 0] * BLK
    live_end = meta[slot, 0] * BLK + meta[slot, 1]
    allowed = (key <= query) & ((query < live_end) | (key == query))
    bias = jnp.where(allowed, 0.0, -1e30)
    return jnp.concatenate([bias] * (HEADS // KVH), axis=1)


def key_tile(kv_ref, meta, slot, chunk, h):
    lanes = slice(128 * h, 128 * h + 128)
    one = pl.ds(pl.multiple_of(meta[slot, 4 + 2 * chunk] * BLK, BLK), BLK)
    two = pl.ds(pl.multiple_of(meta[slot, 5 + 2 * chunk] * BLK, BLK), BLK)
    return jnp.concatenate([kv_ref[one, lanes], kv_ref[two, lanes]], axis=0)


def stacked(ref, rows, h):
    at = 128 * (HEADS // KVH) * h
    return jnp.concatenate(
        [ref[rows, at + 128 * j : at + 128 * j + 128] for j in range(HEADS // KVH)], axis=0
    )


def attention_forward(meta, q_ref, kv_ref, low_ref, lowt_ref, mixed_s, lse_s, peak_s, accum_s):
    group = HEADS // KVH
    low_key = lane_index(2 * BLK) < HD

    @pl.loop(0, q_ref.shape[0] // BLK)
    def _(slot):
        rows = pl.ds(pl.multiple_of(slot * BLK, BLK), BLK)
        peak_s[...] = jnp.full_like(peak_s, -1e30)
        accum_s[...] = jnp.zeros_like(accum_s)

        @pl.loop(0, meta[slot, 2])
        def _(chunk):
            bias = chunk_bias(meta, slot, chunk)
            for h in range(KVH):
                tile = key_tile(kv_ref, meta, slot, chunk, h)
                scores = dot_nt(tile, stacked(q_ref, rows, h)) + bias
                old = peak_s[h, 0:1, :]
                new = jnp.maximum(old, jnp.max(scores, axis=0, keepdims=True))
                probs = jnp.exp(scores - new).astype(BF16)
                ones = jnp.where(low_key, jnp.ones_like(tile), tile)
                accum_s[h] = accum_s[h] * jnp.exp(old - new) + dot_tn(ones, probs)
                peak_s[h, 0:1, :] = new

        for h in range(KVH):
            total = accum_s[h, 0:1, :]
            lse_s[slot, h, 0:1, :] = peak_s[h, 0:1, :] + jnp.log(total)
            mixed = accum_s[h, HD:, :] / total
            for j in range(group):
                head = h * group + j
                mixed_s[slot, HD * head : HD * head + HD, :] = mixed[:, BLK * j : BLK * j + BLK]
        lowt_ref[:, rows] = mixed_s[slot].astype(BF16)
        low_ref[rows, :] = mixed_s[slot].T.astype(BF16)


def feed_forward(
    meta, x_ref, cot_ref, wa_ref, wgu_ref, wd_ref, actt_ref, gres_ref, gb_ref, gain_ref,
    low_s, mixed_s, do_s, delta_s, second_s, second_t_s, grad_gu_s, hidden_s, gm_s,
):
    group = HEADS // KVH
    gain = gain_row(wa_ref, O_AT + HALF)
    high_lane = lane_index(BLK) >= HD
    gain_ref[...] = jnp.zeros_like(gain_ref)
    w_out = wa_ref[:, O_AT : O_AT + QW]
    rows_all = x_ref.shape[0]
    blocks = STEP // BLK

    def living(i):
        row = lax.broadcasted_iota(jnp.int32, (BLK, 1), 0)
        return jnp.concatenate([(row < meta[i * blocks + b, 1]).astype(F32) for b in range(blocks)], axis=0)

    def normalized(i):
        residual = gres_ref[i * STEP : (i + 1) * STEP, :]
        inv = lax.rsqrt(jnp.mean(residual * residual, axis=1, keepdims=True) + EPS)
        return residual * inv, inv

    for i in range(rows_all // STEP):
        rows = slice(i * STEP, (i + 1) * STEP)
        gres_ref[rows, :] = x_ref[rows, :].astype(F32) + dot(low_s[rows, :], w_out)
        second = (normalized(i)[0] * gain).astype(BF16)
        second_s[rows, :] = second
        second_t_s[:, rows] = second.T
        gm_s[rows, :] = (cot_ref[rows, :].astype(F32) * living(i)).astype(BF16)

    width = 256

    @pl.loop(0, FF // width)
    def _(c):
        at = pl.multiple_of(c * width, width)
        here, there = pl.ds(at, width), pl.ds(pl.multiple_of(FF + at, width), width)
        gate, up = dot(second_s[...], wgu_ref[:, here]), dot(second_s[...], wgu_ref[:, there])
        grad_hidden = dot_nt(gm_s[...], wd_ref[here, :])
        sigma = jax.nn.sigmoid(gate)
        swish = gate * sigma
        hidden_s[:, here] = (swish * up).astype(BF16)
        grad_gu_s[:, there] = (grad_hidden * swish).astype(BF16)
        grad_gu_s[:, here] = (grad_hidden * up * (sigma * (1.0 + gate * (1.0 - sigma)))).astype(BF16)

    for i in range(rows_all // STEP):
        rows = slice(i * STEP, (i + 1) * STEP)
        actt_ref[:, rows] = (gres_ref[rows, :] + dot(hidden_s[rows, :], wd_ref[...])).T.astype(BF16)
        norm, inv = normalized(i)
        grad_second = dot_nt(grad_gu_s[rows, :], wgu_ref[...])
        grad_final = cot_ref[rows, :].astype(F32) * living(i)
        scaled = grad_second * gain
        grad_res = grad_final + inv * (scaled - norm * jnp.mean(scaled * norm, axis=1, keepdims=True))
        gres_ref[rows, :] = grad_res
        grad_branch = grad_res.astype(BF16)
        gb_ref[rows, :QW] = grad_branch
        gb_ref[rows, QW:] = jnp.zeros((STEP, 128 - HD), BF16)
        gain_ref[0:1, :] += jnp.sum(grad_second * norm, axis=0, keepdims=True)
        grad_att = dot_nt(grad_branch, w_out).astype(BF16).astype(F32)
        for b in range(blocks):
            slot = i * blocks + b
            here = slice(i * STEP + b * BLK, i * STEP + (b + 1) * BLK)
            part = slice(b * BLK, (b + 1) * BLK)
            product = grad_att[part, :].T * mixed_s[slot]
            for head in range(HEADS):
                at = 128 * (head // 2)
                if head == HEADS - 1:
                    tile = jnp.concatenate([grad_att[part, at : at + HD]] * 2, axis=1)
                else:
                    tile = grad_att[part, at : at + 128]
                    tile = tile if head % 2 else swap(tile)
                tile = jnp.where(high_lane, tile, 0.0).astype(BF16)
                do_s[here, 128 * head : 128 * head + 128] = tile
                h, j = head // group, head % group
                delta_s[slot, h, 0:1, BLK * j : BLK * j + BLK] = jnp.sum(
                    product[HD * head : HD * head + HD, :], axis=0, keepdims=True
                )


def weight_grads(dgu_ref, dd_ref, second_t_s, grad_gu_s, hidden_s, gm_s):
    width = 512

    @pl.loop(0, 2 * FF // width)
    def _(c):
        here = pl.ds(pl.multiple_of(c * width, width), width)
        dgu_ref[:, here] = dot(second_t_s[...], grad_gu_s[:, here]).astype(BF16)

    @pl.loop(0, FF // width)
    def _(c):
        here = pl.ds(pl.multiple_of(c * width, width), width)
        dd_ref[here, :] = dot_tn(hidden_s[:, here], gm_s[...]).astype(BF16)


def attention_backward(meta, q_ref, kv_ref, turned_ref, steps_ref, do_s, lse_s, delta_s, gq_ref, dkv_s, dq_s):
    group = HEADS // KVH
    tall = group * BLK
    dkv_s[...] = jnp.zeros_like(dkv_s)

    @pl.loop(0, q_ref.shape[0] // BLK)
    def _(slot):
        rows = pl.ds(pl.multiple_of(slot * BLK, BLK), BLK)
        dq_s[...] = jnp.zeros_like(dq_s)

        @pl.loop(0, jnp.where(meta[slot, 1] > 0, meta[slot, 2], 0))
        def _(chunk):
            bias = chunk_bias(meta, slot, chunk)
            one = pl.ds(pl.multiple_of(meta[slot, 4 + 2 * chunk] * BLK, BLK), BLK)
            two = pl.ds(pl.multiple_of(meta[slot, 5 + 2 * chunk] * BLK, BLK), BLK)
            for h in range(KVH):
                lanes = slice(128 * h, 128 * h + 128)
                tile = key_tile(kv_ref, meta, slot, chunk, h)
                both = jnp.concatenate([stacked(q_ref, rows, h), stacked(do_s, rows, h)], axis=0)
                products = dot_nt(tile, both)
                probs = jnp.exp(products[:, :tall] + (bias - lse_s[slot, h, 0:1, :]))
                grads = (probs * (products[:, tall:] - delta_s[slot, h, 0:1, :])).astype(BF16)
                dq_s[h] += dot_tn(tile, grads)
                sides = jnp.concatenate([grads, probs.astype(BF16)], axis=1)
                terms = dot(sides, both)
                dkv_s[one, lanes] += terms[:BLK]
                dkv_s[two, lanes] += terms[BLK:]

        place = meta[slot, 0]
        co, so, ci, si = steps_ref[0, place], steps_ref[1, place], turned_ref[0], turned_ref[1]
        turned = lax.broadcasted_iota(jnp.int32, (HD // 2, BLK), 1) < meta[slot, 1]
        cosine = jnp.where(turned, co * ci - so * si, 1.0) * SCALE
        sine = jnp.where(turned, so * ci + co * si, 0.0) * SCALE
        parts = []
        for h in range(KVH):
            for j in range(group):
                one = dq_s[h, : HD // 2, BLK * j : BLK * j + BLK]
                two = dq_s[h, HD // 2 : HD, BLK * j : BLK * j + BLK]
                parts += [one * cosine + two * sine, two * cosine - one * sine]
        gq_ref[rows, :QW] = jnp.concatenate(parts, axis=0).T.astype(BF16)
        gq_ref[rows, QW:] = jnp.zeros((BLK, HD), BF16)


def layer_kernel(
    meta, x_ref, cot_ref, q_ref, kv_ref, wa_ref, gu_hbm, d_hbm, turned_ref, steps_ref,
    actt_ref, gres_ref, gb_ref, lowt_ref, gq_ref, dkv_ref, gain_ref, dgu_hbm, dd_hbm,
    mixed_s, lse_s, delta_s, peak_s, accum_s, do_s, second_s, second_t_s, grad_gu_s, hidden_s, gm_s, dkv_s, low_s,
    wgu_s, wd_s, dgu_s, dd_s, sems,
):
    loads = [
        pltpu.make_async_copy(gu_hbm, wgu_s, sems.at[0]), pltpu.make_async_copy(d_hbm, wd_s, sems.at[1]),
    ]
    stores = [
        pltpu.make_async_copy(dgu_s, dgu_hbm, sems.at[2]), pltpu.make_async_copy(dd_s, dd_hbm, sems.at[3]),
    ]
    for copy in loads:
        copy.start()
    attention_forward(meta, q_ref, kv_ref, low_s, lowt_ref, mixed_s, lse_s, peak_s, accum_s)
    for copy in loads:
        copy.wait()
    feed_forward(
        meta, x_ref, cot_ref, wa_ref, wgu_s, wd_s, actt_ref, gres_ref, gb_ref, gain_ref,
        low_s, mixed_s, do_s, delta_s, second_s, second_t_s, grad_gu_s, hidden_s, gm_s,
    )
    weight_grads(dgu_s, dd_s, second_t_s, grad_gu_s, hidden_s, gm_s)
    for copy in stores:
        copy.start()
    attention_backward(
        meta, q_ref, kv_ref, turned_ref, steps_ref, do_s, lse_s, delta_s, gq_ref, dkv_s, accum_s
    )
    dkv_ref[...] = dkv_s[...].astype(BF16)
    for copy in stores:
        copy.wait()


VMEM_LIMIT = 62 << 20


def layer(meta, tokens, cotangent, queries, keyval, packed, gateup, down, turned, steps):
    rows, slots, group = tokens.shape[0], tokens.shape[0] // BLK, HEADS // KVH
    keys = keyval.shape[0]
    anywhere = pl.BlockSpec(memory_space=pl.ANY)
    return pl.pallas_call(
        layer_kernel,
        out_shape=(
            jax.ShapeDtypeStruct((D, rows), BF16),
            jax.ShapeDtypeStruct((rows, D), F32),
            jax.ShapeDtypeStruct((rows, QW + HD), BF16),
            jax.ShapeDtypeStruct((QW, rows), BF16),
            jax.ShapeDtypeStruct((rows, QW + HD), BF16),
            jax.ShapeDtypeStruct((keys, 2 * KVW), BF16),
            jax.ShapeDtypeStruct((8, D), F32),
            jax.ShapeDtypeStruct((D, 2 * FF), BF16),
            jax.ShapeDtypeStruct((FF, D), BF16),
        ),
        in_specs=[pl.BlockSpec(memory_space=pltpu.SMEM)] + vmem(5) + [anywhere] * 2 + vmem(2),
        out_specs=tuple(vmem(7)) + (anywhere,) * 2,
        scratch_shapes=[
            pltpu.VMEM((slots, QW, BLK), F32),
            pltpu.VMEM((slots, KVH, 8, group * BLK), F32),
            pltpu.VMEM((slots, KVH, 8, group * BLK), F32),
            pltpu.VMEM((KVH, 8, group * BLK), F32),
            pltpu.VMEM((KVH, BLK, group * BLK), F32),
            pltpu.VMEM((rows, 128 * HEADS), BF16),
            pltpu.VMEM((rows, D), BF16),
            pltpu.VMEM((D, rows), BF16),
            pltpu.VMEM((rows, 2 * FF), BF16),
            pltpu.VMEM((rows, FF), BF16),
            pltpu.VMEM((rows, D), BF16),
            pltpu.VMEM((keys, 2 * KVW), F32),
            pltpu.VMEM((rows, QW), BF16),
            pltpu.VMEM((D, 2 * FF), BF16),
            pltpu.VMEM((FF, D), BF16),
            pltpu.VMEM((D, 2 * FF), BF16),
            pltpu.VMEM((FF, D), BF16),
            pltpu.SemaphoreType.DMA((4,)),
        ],
        compiler_params=pltpu.CompilerParams(vmem_limit_bytes=VMEM_LIMIT),
        name="layer",
    )(meta, tokens, cotangent, queries, keyval, packed, gateup, down, turned, steps)


def input_grad_rows(
    meta, i, x_ref, wa_ref, gain, gq_ref, dkv_ref, gres_ref, inner_ref, outer_ref, int_ref, normed_s, first_s, values_s
):
    low_lane = lane_index(BLK) < HD
    rows = slice(i * STEP, (i + 1) * STEP)
    x = x_ref[rows, :].astype(F32)
    inv = lax.rsqrt(jnp.mean(x * x, axis=1, keepdims=True) + EPS)
    norm = x * inv
    normed_s[:, rows] = (norm * gain).astype(BF16).T
    first_s[rows, :512] = gq_ref[rows, :512]
    for b in range(STEP // BLK):
        here = slice(i * STEP + b * BLK, i * STEP + (b + 1) * BLK)
        tables = rope_tables(meta, i * (STEP // BLK) + b, inner_ref, outer_ref)
        tiles = [
            rope_back(dkv_ref[here, 128 * h : 128 * h + 128].astype(F32), tables) for h in range(KVH)
        ]
        last = gq_ref[here, 512:640].astype(F32)
        first_s[here, 512:640] = jnp.where(low_lane, last, swap(tiles[0])).astype(BF16)
        first_s[here, 640:768] = jnp.where(low_lane, tiles[1], swap(tiles[2])).astype(BF16)
        values_s[here, :128] = jnp.where(low_lane, 0.0, tiles[0]).astype(BF16)
        values_s[here, 128:] = jnp.where(low_lane, swap(tiles[1]), tiles[2]).astype(BF16)
    grad_normed = dot_nt(first_s[rows, :], wa_ref[:, :HALF]) + dot_nt(
        values_s[rows, :], wa_ref[:, O_AT + 512 : O_AT + HALF]
    )
    scaled = grad_normed * gain
    grad = gres_ref[rows, :] + inv * (scaled - norm * jnp.mean(scaled * norm, axis=1, keepdims=True))
    int_ref[:, rows] = grad.T
    return jnp.sum(grad_normed * norm, axis=0, keepdims=True)


def packed_grads(da_ref, normed_s, first_s, values_s, lowt_ref, gb_ref, gains, gain_ref):
    shards, rows = da_ref.shape[:2]

    def put(at, value):
        for f in range(shards):
            part = value[f * rows : (f + 1) * rows]
            da_ref[f, :, at : at + value.shape[1]] = part.astype(BF16)

    for c in range(0, HALF, 256):
        put(c, dot(normed_s[...], first_s[:, c : c + 256]))
    for c in range(0, 512, 256):
        put(O_AT + c, dot(lowt_ref[...], gb_ref[:, c : c + 256]))
    put(O_AT + 512, dot(lowt_ref[...], gb_ref[:, 512:640]) + dot(normed_s[...], values_s[:, :128]))
    put(O_AT + 640, dot(normed_s[...], values_s[:, 128:]))
    put(HALF, jnp.broadcast_to(gains, (128, D)).T)
    put(O_AT + HALF, jnp.broadcast_to(gain_ref[0:1, :], (128, D)).T)


def finish_kernel(
    meta, x_ref, wa_ref, gq_ref, dkv_ref, gres_ref, gb_ref, lowt_ref, gain_ref, inner_ref, outer_ref,
    int_ref, da_ref, normed_s, first_s, values_s,
):
    gain = gain_row(wa_ref, HALF)
    gains = jnp.zeros((1, D), F32)
    for i in range(x_ref.shape[0] // STEP):
        gains = gains + input_grad_rows(
            meta, i, x_ref, wa_ref, gain, gq_ref, dkv_ref, gres_ref, inner_ref, outer_ref, int_ref,
            normed_s, first_s, values_s,
        )
    packed_grads(da_ref, normed_s, first_s, values_s, lowt_ref, gb_ref, gains, gain_ref)


def finish_scratch(rows):
    return [pltpu.VMEM((D, rows), BF16), pltpu.VMEM((rows, HALF), BF16), pltpu.VMEM((rows, 256), BF16)]


def finish(meta, tokens, packed, gq, dkv, gres, gb, lowt, gain, inner, outer):
    rows = tokens.shape[0]
    input_grad, d_packed = pl.pallas_call(
        finish_kernel,
        out_shape=(
            jax.ShapeDtypeStruct((D, rows), F32),
            jax.ShapeDtypeStruct((1, D, WIDE_A), BF16),
        ),
        in_specs=[pl.BlockSpec(memory_space=pltpu.SMEM)] + vmem(10),
        out_specs=tuple(vmem(2)),
        scratch_shapes=finish_scratch(rows),
        compiler_params=pltpu.CompilerParams(vmem_limit_bytes=VMEM_LIMIT),
        name="finish",
    )(meta, tokens, packed, gq, dkv, gres, gb, lowt, gain, inner, outer)
    return input_grad, d_packed[0]


def pack(w_query, w_keyval, w_out, w_gateup, w_down, norm_gains):
    rows = w_query.shape[0]
    spread = [jnp.broadcast_to(norm_gains[:, g : g + 1], (rows, 128)) for g in range(2)]
    packed = jnp.concatenate(
        [w_query, w_keyval[:, 0], spread[0], w_out, w_keyval[:, 1], spread[1]], axis=1
    )
    return packed.astype(BF16), w_gateup.reshape(rows, 2 * FF).astype(BF16), w_down.astype(BF16)


def for_sending(value):
    return jax.tree.map(lambda a: a.astype(jnp.bfloat16) if a.dtype == jnp.float32 else a, value)


def orthogonal(matrix):
    flipped = matrix.shape[0] > matrix.shape[1]
    iterate = matrix.T if flipped else matrix
    iterate = iterate / (jnp.sqrt(jnp.sum(iterate * iterate)) + 1e-07)
    for turn in range(NS_STEPS):
        gram_matrix = jnp.dot(iterate, iterate.T, precision=lax.Precision.HIGHEST)
        polynomial = COEF_B * gram_matrix + COEF_C * jnp.dot(
            gram_matrix, gram_matrix, precision=lax.Precision.HIGHEST
        )
        iterate = COEF_A * iterate + jnp.dot(polynomial, iterate, precision=lax.Precision.HIGHEST)
    return iterate.T if flipped else iterate


def muon_step(matrix):
    return MUON_RATE * math.sqrt(max(matrix.shape[0], matrix.shape[1])) * orthogonal(matrix)


def owner_branch(matrix_rows, matrix_cols, widest, received):
    group_size = received.shape[0]
    shard_size = matrix_rows * matrix_cols // group_size
    full_matrix = received[:, :shard_size].reshape(matrix_rows, matrix_cols)
    update_rows = muon_step(full_matrix).reshape(group_size, shard_size)
    return jnp.pad(update_rows, ((0, 0), (0, widest - shard_size)))


def zero_branch(received):
    return jnp.zeros_like(received)


def muon_exchange(pieces):
    fsdp_size, fsdp_index = lax.axis_size("fsdp"), lax.axis_index("fsdp")
    flat_sizes = [piece.size for piece in pieces]
    widest = max(flat_sizes)
    padded = [jnp.pad(piece.reshape(-1), (0, widest - piece.size)) for piece in pieces]
    outgoing = jnp.stack(padded + [jnp.zeros((widest,), F32)] * (fsdp_size - len(pieces)))
    received = lax.all_to_all(
        outgoing.astype(BF16), "fsdp", split_axis=0, concat_axis=0, tiled=True
    ).astype(F32)
    branches = [
        partial(owner_branch, piece.shape[0] * fsdp_size, piece.shape[1], widest)
        for piece in pieces
    ] + [zero_branch]
    update_rows = lax.switch(jnp.minimum(fsdp_index, len(pieces)), branches, received)
    returned = lax.all_to_all(
        update_rows.astype(BF16), "fsdp", split_axis=0, concat_axis=0, tiled=True
    ).astype(F32)
    return [returned[m, : flat_sizes[m]].reshape(pieces[m].shape) for m in range(len(pieces))]


def gather_rows_xla(shard):
    return lax.all_gather(shard, "fsdp", axis=0, tiled=True)


def reduce_rows_xla(grads):
    return lax.psum(lax.psum_scatter(grads, "fsdp", scatter_dimension=0, tiled=True), "dp")


class Place:
    def __init__(self, lines):
        self.f, self.d = lax.axis_index("fsdp"), lax.axis_index("dp")
        self.line, self.column = self.f // 2, self.f % 2
        self.x, self.core = self.d // 2, self.d % 2
        self.lines = lines
        self.sibling = (self.f, self.d + 1 - 2 * self.core)
        self.across = (self.f, self.core + 2 * (1 - self.x))
        self.beside = (self.f + 1 - 2 * self.column, self.d)
        self.above = (self.f + 2, self.d)
        self.below = (self.f - 2, self.d)


def remote(source, target, send_sem, recv_sem, device):
    return pltpu.make_async_remote_copy(
        src_ref=source, dst_ref=target, send_sem=send_sem, recv_sem=recv_sem,
        device_id=device, device_id_type=pl.DeviceIdType.MESH,
    )


def greet(place, chips=True, between=lambda: None):
    barrier = pltpu.get_barrier_semaphore()

    def signal(device):
        pl.semaphore_signal(barrier, inc=1, device_id=device, device_id_type=pl.DeviceIdType.MESH)

    signal(place.sibling)
    signal(place.across)
    if not chips:
        between()
        pl.semaphore_wait(barrier, 2)
        return
    signal(place.beside)
    pl.when(place.line > 0)(lambda: signal(place.below))
    pl.when(place.line < place.lines - 1)(lambda: signal(place.above))
    between()
    ends = (place.line == 0).astype(jnp.int32) + (place.line == place.lines - 1).astype(jnp.int32)
    pl.semaphore_wait(barrier, 5 - ends)


PARTS = 4


def half_parts(packed, gateup, down, core):
    tall = down.shape[0] // 2
    at = core * FF
    return (
        None if packed is None else packed.at[:, pl.ds(pl.multiple_of(core * O_AT, 128), O_AT)],
        gateup.at[:, pl.ds(pl.multiple_of(at, 128), FF // 2)],
        gateup.at[:, pl.ds(pl.multiple_of(at + FF // 2, 128), FF // 2)],
        down.at[pl.ds(pl.multiple_of(core * tall, 16), tall), :],
    )


SPLIT = (False, True, True, False)


def start_kernel(
    lines, lengths, assignment, xt_ref, cott_ref, gains_ref, wq_ref, wkv_ref, wo_ref, wgu_ref, wd_ref,
    inner_ref, outer_ref,
    meta, x_ref, cot_ref, q_ref, wa_ref, kv_out, gu_out, d_out,
    a_s, gu_s, d_s, a_out, kv_s,
    own_sem, in_sem, pair_sem, up_sem, down_sem, side_sem, cross_sem, mate_sem,
    kv_in, kv_pair, kv_cross, kv_mate,
):
    place = Place(lines)
    shard_rows = a_s.shape[0]
    own = [
        pltpu.make_async_copy(source, target.at[place.f], own_sem.at[i])
        for i, (source, target) in enumerate(((a_s, a_out), (gu_s, gu_out), (d_s, d_out)))
    ]

    def pack_first():
        gains = jnp.broadcast_to(gains_ref[...][:, None, :], (2, 128, shard_rows))
        for side, w_ref in enumerate((wq_ref, wo_ref)):
            at = side * O_AT
            a_s[:, at : at + QW] = w_ref[...].astype(BF16)
            a_s[:, at + QW : at + HALF] = wkv_ref[:, side, :].astype(BF16)
            a_s[:, at + HALF : at + O_AT] = gains[side].T.astype(BF16)
        for side in range(2):
            gu_s[:, side * FF : side * FF + FF] = wgu_ref[:, side, :].astype(BF16)
        d_s[...] = wd_ref[...].astype(BF16)

    greet(place, True, pack_first)

    def full(shard, core):
        return half_parts(a_out.at[shard], gu_out.at[shard], d_out.at[shard], core)

    mine = half_parts(a_s, gu_s, d_s, place.core)

    def send(shard, k, sems, device, recv, source=None):
        target = full(shard, place.core)[k]
        return remote(target if source is None else source, target, sems.at[shard, k], recv.at[shard, k], device)

    def to_pair(shard, k):
        return send(shard, k, mate_sem, place.sibling, pair_sem)

    def if_sideways(k, run):
        if SPLIT[k]:
            pl.when(place.x == k % 2)(run)
        else:
            run()

    def on_z(t, k, action):
        for sign in (-1, 1) if t else (0,):
            shard = place.f + 2 * sign * t
            there = place.line + sign * t

            def go(shard=shard, sign=sign):
                source = None if sign else mine[k]
                if sign:
                    action(None, shard)
                if sign <= 0:
                    pl.when(place.line < lines - 1)(
                        lambda: action(send(shard, k, up_sem, place.above, in_sem, source))
                    )
                if sign >= 0:
                    pl.when(place.line > 0)(
                        lambda: action(send(shard, k, down_sem, place.below, in_sem, source))
                    )
                if_sideways(k, lambda: action(send(shard, k, side_sem, place.beside, in_sem, source)))
                if sign:
                    action(to_pair(shard, k))

            if sign:
                pl.when((there >= 0) & (there < lines))(go)
            else:
                go()

    def at_distance(base, t, run):
        if t == 0:
            run(base)
            return
        for sign in (-1, 1):
            there = place.line + sign * t
            pl.when((there >= 0) & (there < lines))(lambda sign=sign: run(base + 2 * sign * t))

    def on_side(t, k, action):
        def run(shard):
            action(None, shard)
            if SPLIT[k]:
                action(send(shard, k, cross_sem, place.across, in_sem))
            action(to_pair(shard, k))

        if_sideways(k, lambda: at_distance(place.beside[0], t, run))

    def on_cross(t, k, action):
        def run(shard):
            action(None, shard)
            action(to_pair(shard, k))

        if SPLIT[k]:
            pl.when(place.x != k % 2)(lambda: at_distance(place.beside[0], t, run))

    def start(k):
        def action(copy, shard=None):
            if copy is None:
                send(shard, k, up_sem, place.sibling, in_sem).wait_recv()
            else:
                copy.start()

        return action

    def finish_send(copy, shard=None):
        if copy is not None:
            copy.wait_send()

    def from_pair(k):
        def got(shard):
            target = full(shard, 1 - place.core)[k]
            remote(target, target, mate_sem.at[shard, k], pair_sem.at[shard, k], place.sibling).wait_recv()

        for t in range(lines):
            at_distance(place.beside[0], t, got)
            if t > 0:
                at_distance(place.f, t, got)

    on_z(0, 0, start(0))
    on_z(0, 1, start(1))
    for copy in own:
        copy.start()
    block_meta(lengths, assignment, place.d * (x_ref.shape[0] // BLK), x_ref.shape[0] // BLK, meta)
    for i in range(x_ref.shape[0] // STEP):
        rows = slice(i * STEP, (i + 1) * STEP)
        x_ref[rows, :] = xt_ref[:, rows].T
        cot_ref[rows, :] = cott_ref[:, rows].T
    for t in range(1, lines + 1):
        if t < lines:
            on_z(t, 0, start(0))
        if t < PARTS - 1:
            on_z(0, t + 1, start(t + 1))
        on_side(t - 1, 0, start(0))
    own[0].wait()
    from_pair(0)
    for f in range(0, 2 * lines, 2):
        wa_ref[f * shard_rows : (f + 2) * shard_rows, :] = jnp.concatenate([a_out[f], a_out[f + 1]], axis=0)
    later = []
    for t in range(lines + 2):
        for k in range(1, PARTS):
            if 0 < t < lines:
                later.append((on_z, t, k))
            if 0 <= t - 1 < lines:
                later.append((on_side, t - 1, k))
            if 0 <= t - 2 < lines:
                later.append((on_cross, t - 2, k))

    def rest(count):
        for go, t, k in later[:count]:
            go(t, k, start(k))
        del later[:count]

    def kv_rows(i):
        return pl.ds(i * STEP, STEP)

    def kv_send(i, device, sems, recv):
        return remote(kv_s.at[kv_rows(i)], kv_out.at[place.d, kv_rows(i)], sems.at[i], recv.at[i], device)

    def kv_pass(i):
        here = kv_out.at[place.across[1], kv_rows(i)]
        return remote(here, here, kv_mate.at[1, i], kv_pair.at[1, i], place.sibling)

    steps = x_ref.shape[0] // STEP
    gain = gain_row(wa_ref, HALF)
    rest(PARTS - 1)
    for i in range(steps):
        project_rows(meta, i, x_ref, wa_ref, gain, inner_ref, outer_ref, q_ref, kv_s)
        kv_send(i, place.across, kv_cross, kv_in).start()
        kv_send(i, place.sibling, kv_mate.at[0], kv_pair.at[0]).start()
        rest(PARTS)
    own_kv = pltpu.make_async_copy(kv_s, kv_out.at[place.d], own_sem.at[3])
    own_kv.start()
    for i in range(steps):
        rest(2 * (PARTS - 1))
        kv_send(i, place.across, kv_cross, kv_in).wait_recv()
        kv_pass(i).start()
    rest(len(later))
    for k in range(PARTS):
        if k > 0:
            from_pair(k)
        for t in range(lines):
            on_z(t, k, finish_send)
            on_side(t, k, finish_send)
            on_cross(t, k, finish_send)
    for i in range(steps):
        kv_send(i, place.sibling, kv_mate.at[0], kv_pair.at[0]).wait()
        kv_send(i, place.across, kv_cross, kv_in).wait_send()
        kv_pass(i).wait()
    for copy in own[1:] + [own_kv]:
        copy.wait()


def start_remote(lengths, assignment, tokens, cotangent, gains, weights, inner, outer, count):
    rows = tokens.shape[0]
    shard_rows, tall, steps = weights[0].shape[0], weights[4].shape[0], rows // STEP
    smem, anywhere = pl.BlockSpec(memory_space=pltpu.SMEM), pl.BlockSpec(memory_space=pl.ANY)
    shapes = ((shard_rows, WIDE_A), (shard_rows, 2 * FF), (tall, D))
    sems = pltpu.SemaphoreType.DMA((count, PARTS))
    meta, x, cot, queries, packed, keyval, gateup, down = pl.pallas_call(
        partial(start_kernel, count // 2),
        out_shape=(
            jax.ShapeDtypeStruct((rows // BLK, META), jnp.int32),
            jax.ShapeDtypeStruct((rows, D), BF16),
            jax.ShapeDtypeStruct((rows, D), BF16),
            jax.ShapeDtypeStruct((rows, 128 * HEADS), BF16),
            jax.ShapeDtypeStruct((D, WIDE_A), BF16),
            jax.ShapeDtypeStruct((4, rows, 2 * KVW), BF16),
            jax.ShapeDtypeStruct((count,) + shapes[1], BF16),
            jax.ShapeDtypeStruct((count,) + shapes[2], BF16),
        ),
        in_specs=[smem] * 2 + vmem(10),
        out_specs=(smem,) + tuple(vmem(4)) + (anywhere,) * 3,
        scratch_shapes=[pltpu.VMEM(s, BF16) for s in shapes]
        + [pltpu.VMEM((count,) + shapes[0], BF16), pltpu.VMEM((rows, 2 * KVW), BF16)]
        + [pltpu.SemaphoreType.DMA((4,))]
        + [sems] * 7
        + [
            pltpu.SemaphoreType.DMA((steps,)),
            pltpu.SemaphoreType.DMA((2, steps)),
            pltpu.SemaphoreType.DMA((steps,)),
            pltpu.SemaphoreType.DMA((2, steps)),
        ],
        compiler_params=pltpu.CompilerParams(
            collective_id=0, has_side_effects=True, vmem_limit_bytes=VMEM_LIMIT
        ),
        name="gather_and_project",
    )(lengths, assignment, tokens.T, cotangent.T, gains.T, *weights, inner, outer)
    return (
        meta, x, cot, queries, packed, keyval.reshape(4 * rows, 2 * KVW),
        gateup.reshape(D, 2 * FF), down.reshape(FF, D),
    )


def start_kernel_plain(
    lengths, assignment, x_ref, wa_ref, inner_ref, outer_ref, meta, q_ref, kv_ref
):
    slots = x_ref.shape[0] // BLK
    block_meta(lengths, assignment, lax.axis_index("dp") * slots, slots, meta)
    gain = gain_row(wa_ref, HALF)
    for i in range(x_ref.shape[0] // STEP):
        project_rows(meta, i, x_ref, wa_ref, gain, inner_ref, outer_ref, q_ref, kv_ref)


def start_xla(lengths, assignment, tokens, cotangent, gains, weights, inner, outer):
    packed, gateup, down = (gather_rows_xla(s) for s in pack(*weights, gains))
    rows = tokens.shape[0]
    smem = pl.BlockSpec(memory_space=pltpu.SMEM)
    meta, queries, keyval = pl.pallas_call(
        start_kernel_plain,
        out_shape=(
            jax.ShapeDtypeStruct((rows // BLK, META), jnp.int32),
            jax.ShapeDtypeStruct((rows, 128 * HEADS), BF16),
            jax.ShapeDtypeStruct((rows, 2 * KVW), BF16),
        ),
        in_specs=[smem] * 2 + vmem(4),
        out_specs=(smem,) + tuple(vmem(2)),
        compiler_params=pltpu.CompilerParams(vmem_limit_bytes=VMEM_LIMIT),
        name="project",
    )(lengths, assignment, tokens, packed, inner, outer)
    keyval = lax.all_gather(keyval, "dp", axis=0, tiled=True)
    return meta, tokens, cotangent, queries, packed, keyval, gateup, down


def visit_order(lines):
    return [sorted(range(lines), key=lambda other: (-abs(other - line), -other)) for line in range(lines)]


def reduce_kernel(
    lines, meta, x_ref, wa_ref, gq_ref, dkv_ref, gres_ref, gb_ref, lowt_ref, gain_ref, inner_ref, outer_ref,
    gu_hbm, d_hbm,
    int_ref, a_out, gu_out, d_out,
    normed_s, first_s, values_s, kv_s, kv_pair_s, kv_far_s, kv_cross_s,
    da_s, gu_s, d_s, a_pair, gu_pair, d_pair, a_in, gu_in, d_in,
    load_sem, kv_pair, kv_cross, kv_pair_send, kv_cross_send,
    pair_recv, recv, last_recv, pair_send, send, last_send,
):
    place = Place(lines)
    half = FF // 2
    steps = x_ref.shape[0] // STEP
    order_table = visit_order(lines)

    def own_load(shard, k):
        source = half_parts(None, gu_hbm.at[shard], d_hbm.at[shard], place.core)[k]
        return pltpu.make_async_copy(source, pieces(shard)[k], load_sem.at[shard, k - 1])

    def pieces(shard):
        at = pl.multiple_of(place.core * O_AT, 128)
        return (
            da_s.at[shard, :, pl.ds(at, O_AT)], gu_s.at[shard, :, pl.ds(0, half)],
            gu_s.at[shard, :, pl.ds(half, half)], d_s.at[shard],
        )

    def mate(shard):
        return (
            a_pair.at[shard], gu_pair.at[shard, :, pl.ds(0, half)], gu_pair.at[shard, :, pl.ds(half, half)],
            d_pair.at[shard],
        )

    def inbox(way, spot):
        return (
            a_in.at[way, spot], gu_in.at[way, spot, :, pl.ds(0, half)],
            gu_in.at[way, spot, :, pl.ds(half, half)], d_in.at[way, spot],
        )

    def order(t):
        spot = jnp.int32(0)
        for line in range(lines):
            spot = spot + order_table[line][t] * (place.line == line).astype(jnp.int32)
        return spot

    def to_pair(shard, k):
        there = 1 - place.core
        if k == 0:
            source = da_s.at[shard, :, pl.ds(pl.multiple_of(there * O_AT, 128), O_AT)]
        else:
            source = half_parts(None, gu_hbm.at[shard], d_hbm.at[shard], there)[k]
        return remote(source, mate(shard)[k], pair_send.at[shard, k], pair_recv.at[shard, k], place.sibling)

    def pass_on(shard, k, way, spot, device):
        return remote(
            mate(shard)[k], inbox(way, spot)[k], send.at[way, spot, k], recv.at[way, spot, k], device
        )

    def arrived(k, way, spot):
        target = inbox(way, spot)[k]
        remote(target, target, send.at[way, spot, k], recv.at[way, spot, k], place.sibling).wait_recv()

    def local_ready(shard, k):
        to_pair(shard, k).wait_recv()
        if k > 0:
            own_load(shard, k).wait()

    def total(shard, k, spot, ways):
        value = pieces(shard)[k][...].astype(F32) + mate(shard)[k][...].astype(F32)
        for way in ways:
            value = value + inbox(way, spot)[k][...].astype(F32)
        mate(shard)[k][...] = value.astype(BF16)

    def on_plane(k, run, other=None):
        if not SPLIT[k]:
            run(False)
            return
        pl.when(place.x == k % 2)(lambda: run(True))
        if other is not None:
            pl.when(place.x != k % 2)(other)

    def stage_pair(t, k):
        spot = order(t)
        shard = 2 * spot + 1 - place.column
        local_ready(shard, k)

        def away():
            total(shard, k, spot, ())
            pass_on(shard, k, 0, spot, place.across).start()

        if SPLIT[k]:
            pl.when(place.x != k % 2)(away)
        else:
            total(shard, k, spot, ())
            pass_on(shard, k, 1, spot, place.beside).start()

    def stage_side(t, k):
        spot = order(t)
        shard = 2 * spot + 1 - place.column

        def go():
            arrived(k, 0, spot)
            total(shard, k, spot, (0,))
            pass_on(shard, k, 1, spot, place.beside).start()

        if SPLIT[k]:
            pl.when(place.x == k % 2)(go)

    def stage_line(t, k):
        spot = order(t)
        shard = 2 * spot + place.column
        local_ready(shard, k)
        if SPLIT[k]:
            pl.when(place.x == k % 2)(lambda: arrived(k, 1, spot))
        else:
            arrived(k, 1, spot)

        def summed(ways):
            for way in ways:
                arrived(k, way, spot)
            if SPLIT[k]:
                pl.when(place.x == k % 2)(lambda: total(shard, k, spot, (1,) + ways))
                pl.when(place.x != k % 2)(lambda: total(shard, k, spot, ways))
            else:
                total(shard, k, spot, (1,) + ways)

        below, above = place.line > 0, place.line < lines - 1

        if t < lines - 1:

            @pl.when(spot > place.line)
            def _():
                pl.when(below)(lambda: summed((2,)))
                pl.when(jnp.logical_not(below))(lambda: summed(()))
                pass_on(shard, k, 2, spot, place.above).start()

            @pl.when(spot < place.line)
            def _():
                pl.when(above)(lambda: summed((3,)))
                pl.when(jnp.logical_not(above))(lambda: summed(()))
                pass_on(shard, k, 3, spot, place.below).start()

        else:
            pl.when(below & above)(lambda: summed((2, 3)))
            pl.when(jnp.logical_not(below))(lambda: summed((3,)))
            pl.when(jnp.logical_not(above))(lambda: summed((2,)))
            last(k).start()

    def last(k):
        return remote(
            mate(place.f)[k], inbox(4, 0)[k], last_send.at[0, k], last_recv.at[0, k], place.across
        )

    def share(k, core):
        target = half_parts(a_out, gu_out, d_out, core)[k]
        return remote(target, target, last_send.at[1, k], last_recv.at[1, k], place.sibling)

    def stage_last(k):
        last(k).wait_recv()
        target = half_parts(a_out, gu_out, d_out, place.core)[k]
        target[...] = added(mate(place.f)[k][...], inbox(4, 0)[k][...]).astype(BF16)
        share(k, place.core).start()

    def every(act, ks):
        for t in range(lines):
            for column in (1 - place.column, place.column):
                for k in ks:
                    act(2 * order(t) + column, k)

    early = (1, 2, 3)
    targets = ((1 - place.core) + 2 * (1 - place.x), (1 - place.core) + 2 * place.x)

    def kv_rows(i):
        return pl.ds(i * STEP, STEP)

    def kv_to_pair(w, i):
        return remote(
            dkv_ref.at[targets[w], kv_rows(i)], kv_pair_s.at[w, kv_rows(i)], kv_pair_send.at[w, i],
            kv_pair.at[w, i], place.sibling,
        )

    def kv_across(i):
        return remote(
            kv_far_s.at[kv_rows(i)], kv_cross_s.at[kv_rows(i)], kv_cross_send.at[i], kv_cross.at[i], place.across
        )

    greet(place, True, lambda: every(lambda shard, k: own_load(shard, k).start(), early))
    for w in range(2):
        for i in range(steps):
            kv_to_pair(w, i).start()
    every(lambda shard, k: to_pair(shard, k).start(), early)
    for i in range(steps):
        kv_to_pair(0, i).wait_recv()
        kv_far_s[kv_rows(i)] = added(dkv_ref[place.across[1], kv_rows(i)], kv_pair_s[0, kv_rows(i)]).astype(BF16)
        kv_across(i).start()
    gain = gain_row(wa_ref, HALF)
    events = []
    for t in range(lines + 2):
        for k in early:
            if t < lines:
                events.append((stage_pair, t, k))
            if 0 <= t - 1 < lines:
                events.append((stage_side, t - 1, k))
            if 0 <= t - 2 < lines:
                events.append((stage_line, t - 2, k))

    def go_on(count):
        for stage, t, k in events[:count]:
            stage(t, k)
        del events[:count]

    go_on(12)
    gains = jnp.zeros((1, D), F32)
    for i in range(steps):
        kv_to_pair(1, i).wait_recv()
        kv_across(i).wait_recv()
        mine = added(dkv_ref[place.d, kv_rows(i)], kv_pair_s[1, kv_rows(i)])
        kv_s[kv_rows(i)] = (mine + kv_cross_s[kv_rows(i)].astype(F32)).astype(BF16)
        gains = gains + input_grad_rows(
            meta, i, x_ref, wa_ref, gain, gq_ref, kv_s, gres_ref, inner_ref, outer_ref, int_ref,
            normed_s, first_s, values_s,
        )
        go_on(3)
    packed_grads(da_s, normed_s, first_s, values_s, lowt_ref, gb_ref, gains, gain_ref)
    every(lambda shard, k: to_pair(shard, k).start(), (0,))
    go_on(6)
    for t in range(lines):
        stage_pair(t, 0)
        go_on(3)
    go_on(len(events))
    for t in range(lines):
        stage_line(t, 0)
        if t < len(early):
            stage_last(early[t])
    stage_last(0)
    for k in range(PARTS):
        share(k, 1 - place.core).wait_recv()
        share(k, place.core).wait_send()
        last(k).wait_send()
    every(lambda shard, k: to_pair(shard, k).wait_send(), range(PARTS))
    for i in range(steps):
        kv_to_pair(0, i).wait_send()
        kv_to_pair(1, i).wait_send()
        kv_across(i).wait_send()
    for t in range(lines):
        spot = order(t)
        for k in range(PARTS):
            other, own = 2 * spot + 1 - place.column, 2 * spot + place.column
            on_plane(
                k,
                lambda split: pass_on(other, k, 1, spot, place.beside).wait_send(),
                lambda: pass_on(other, k, 0, spot, place.across).wait_send(),
            )
            if t < lines - 1:
                pl.when(spot > place.line)(lambda: pass_on(own, k, 2, spot, place.above).wait_send())
                pl.when(spot < place.line)(lambda: pass_on(own, k, 3, spot, place.below).wait_send())


def added(one, two):
    return one.astype(F32) + two.astype(F32)


def reduce_remote(meta, x, packed, gq, dkv, gres, gb, lowt, gain, inner, outer, d_gateup, d_down, count):
    lines, rows = count // 2, x.shape[0]
    shard_rows, tall = D // count, FF // count
    steps, width = rows // STEP, dkv.shape[1]
    halves = ((shard_rows, O_AT), (shard_rows, FF), (tall // 2, D))
    anywhere = pl.BlockSpec(memory_space=pl.ANY)
    dma = pltpu.SemaphoreType.DMA
    outs = pl.pallas_call(
        partial(reduce_kernel, lines),
        out_shape=(
            jax.ShapeDtypeStruct((D, rows), F32),
            jax.ShapeDtypeStruct((shard_rows, WIDE_A), BF16),
            jax.ShapeDtypeStruct((shard_rows, 2 * FF), BF16),
            jax.ShapeDtypeStruct((tall, D), BF16),
        ),
        in_specs=[pl.BlockSpec(memory_space=pltpu.SMEM)] + vmem(10) + [anywhere] * 2,
        out_specs=tuple(vmem(4)),
        scratch_shapes=finish_scratch(rows)
        + [pltpu.VMEM((rows, width), BF16), pltpu.VMEM((2, rows, width), BF16)]
        + [pltpu.VMEM((rows, width), BF16)] * 2
        + [pltpu.VMEM((count, shard_rows, WIDE_A), BF16)]
        + [pltpu.VMEM((count,) + h, BF16) for h in halves[1:] + halves]
        + [pltpu.VMEM((5, lines) + h, BF16) for h in halves]
        + [
            dma((count, PARTS - 1)), dma((2, steps)), dma((steps,)), dma((2, steps)), dma((steps,)),
            dma((count, PARTS)), dma((4, lines, PARTS)), dma((2, PARTS)),
            dma((count, PARTS)), dma((4, lines, PARTS)), dma((2, PARTS)),
        ],
        compiler_params=pltpu.CompilerParams(
            collective_id=3, has_side_effects=True, vmem_limit_bytes=VMEM_LIMIT
        ),
        name="finish_and_reduce",
    )(
        meta, x, packed, gq, dkv.reshape(4, rows, width), gres, gb, lowt, gain, inner, outer,
        d_gateup.reshape(count, shard_rows, 2 * FF), d_down.reshape(count, tall, D),
    )
    return outs[0], outs[1:]


def own_kernels():
    return lax.axis_size("fsdp") == 8 and lax.axis_size("dp") == 4


def begin(*given):
    return start_remote(*given, lax.axis_size("fsdp")) if own_kernels() else start_xla(*given)


def reduce_gradients(meta, x, packed, gq, dkv, gres, gb, lowt, gain, inner, outer, d_gateup, d_down):
    if own_kernels():
        return reduce_remote(
            meta, x, packed, gq, dkv, gres, gb, lowt, gain, inner, outer, d_gateup, d_down,
            lax.axis_size("fsdp"),
        )
    dkv = lax.psum_scatter(dkv, "dp", scatter_dimension=0, tiled=True)
    input_grad, d_packed = finish(meta, x, packed, gq, dkv, gres, gb, lowt, gain, inner, outer)
    return input_grad, tuple(reduce_rows_xla(g) for g in (d_packed, d_gateup, d_down))


WIDE_AT, TALL_AT = (2, 5), 3
SQUARE_AT, NARROW_AT = (0, 7), (6, 1)
NARROW = 256


def by_core(pair, core):
    return pair[0] + (pair[1] - pair[0]) * core


def greet_plane(place, count):
    barrier = pltpu.get_barrier_semaphore()
    pl.semaphore_signal(barrier, inc=1, device_id=place.sibling, device_id_type=pl.DeviceIdType.MESH)
    for step in range(1, count):
        f = lax.rem(place.f + step, count)
        for core in range(2):
            pl.semaphore_signal(
                barrier, inc=1, device_id=(f, 2 * place.x + core), device_id_type=pl.DeviceIdType.MESH
            )
    pl.semaphore_wait(barrier, 2 * count - 1)


def newton_schulz(x_s, low_s, gram_s, gram_low_s, poly_s):
    size, width = x_s.shape
    cuts = [(at, min(256, size - at)) for at in range(0, size, 256)]

    @pl.loop(0, NS_STEPS)
    def _(step):
        shift = jnp.where(step >= NS_STEPS - 2, 1.0, 0.0)
        for at, wide in cuts:
            gram = dot_nt(low_s[...], low_s[at : at + wide, :])
            row = lax.broadcasted_iota(jnp.int32, (size, wide), 0)
            column = lax.broadcasted_iota(jnp.int32, (size, wide), 1) + at
            gram = gram - jnp.where(row == column, shift, 0.0)
            gram_s[:, at : at + wide] = gram
            gram_low_s[:, at : at + wide] = gram.astype(BF16)
        for at, wide in cuts:
            square = dot(gram_low_s[...], gram_low_s[:, at : at + wide])
            poly = (COEF_B + 2.0 * COEF_C * shift) * gram_s[:, at : at + wide] + COEF_C * square
            poly_s[:, at : at + wide] = poly.astype(BF16)
        keep = COEF_A + COEF_B * shift + COEF_C * shift * shift
        for at in range(0, width, 256):
            lanes = slice(at, at + 256)
            new = keep * x_s[:, lanes] + dot(poly_s[...], low_s[:, lanes])
            x_s[:, lanes] = new
            low_s[:, lanes] = new.astype(BF16)


def muon_kernel(
    count, a_ref, gu_ref, d_ref, mq_ref, mkv_ref, mo_ref, mgu_ref, md_ref,
    sq_out, nk_out, gu_out, d_out,
    my_gu, my_sq, my_nk, my_d, wide_s, sq_s, nk_s, tall_s, x_s, low_s, gram_s, gram_low_s, poly_s,
    in_send, in_recv, own_sem, out_send, out_recv, pair_send, pair_recv,
):
    place = Place(count // 2)
    greet_plane(place, count)
    rows, tall = my_gu.shape[0], my_d.shape[0]

    def moment(momentum, grad):
        return (MOMENTUM_DECAY * momentum + grad.astype(F32)).astype(BF16)

    my_nk[...] = jnp.zeros_like(my_nk)

    def moments_of(core, m_square):
        my_gu[...] = moment(mgu_ref[:, core, :], gu_ref[:, core * FF : core * FF + FF])
        at = core * O_AT
        my_sq[...] = moment(m_square[...], a_ref[:, at : at + QW])
        my_nk[:, :KVW] = moment(mkv_ref[:, core, :], a_ref[:, at + QW : at + HALF])
        part = slice(core * tall, (core + 1) * tall)
        my_d[...] = moment(md_ref[part, :], d_ref[part, :])

    pl.when(place.core == 0)(lambda: moments_of(0, mq_ref))
    pl.when(place.core == 1)(lambda: moments_of(1, mo_ref))

    tall_rows = pl.ds(pl.multiple_of(place.core * tall, 16), tall)
    wide_at, sq_at, nk_at = (by_core(p, place.core) for p in (WIDE_AT, SQUARE_AT, NARROW_AT))
    tall_core = 2 * place.x
    routes = (
        (my_gu, wide_s.at[place.f], wide_at, place.d),
        (my_d, tall_s.at[place.f, tall_rows], TALL_AT, tall_core),
        (my_sq, sq_s.at[place.f], sq_at, place.d),
        (my_nk, nk_s.at[place.f], nk_at, place.d),
    )

    def each_route(far, near):
        for i, (source, target, f, d) in enumerate(routes):
            here = (place.f == f) & (place.d == d)
            recv = in_recv.at[i, place.f] if i != 1 else in_recv.at[i, place.f + count * place.core]
            pl.when(jnp.logical_not(here))(
                lambda i=i, source=source, target=target, f=f, d=d, recv=recv: far(
                    remote(source, target, in_send.at[i], recv, (f, d))
                )
            )
            pl.when(here)(
                lambda i=i, source=source, target=target: near(
                    pltpu.make_async_copy(source, target, own_sem.at[i])
                )
            )

    each_route(lambda copy: copy.start(), lambda copy: copy.start())
    each_route(lambda copy: copy.wait_send(), lambda copy: copy.wait())

    def received(i, slot_of):
        for step in range(1, count):
            f = lax.rem(place.f + step, count)
            target = slot_of(f)
            remote(target, target, in_send.at[i], in_recv.at[i, f], place.sibling).wait_recv()

    def received_tall():
        for step in range(count):
            f = lax.rem(place.f + step, count)
            for core in range(2):
                if step == 0 and core == 0:
                    continue
                target = tall_s.at[f, pl.ds(core * tall, tall)]
                remote(target, target, in_send.at[1], in_recv.at[1, f + count * core], place.sibling).wait_recv()

    def scaled():
        total = jnp.zeros((1, 1), F32)
        for at in range(0, FF, 256):
            part = x_s[:, at : at + 256]
            total = total + jnp.sum(jnp.sum(part * part, axis=0, keepdims=True), axis=1, keepdims=True)
        factor = 1.0 / (jnp.sqrt(total) + 1e-07)
        for at in range(0, FF, 256):
            part = x_s[:, at : at + 256] * factor
            x_s[:, at : at + 256] = part
            low_s[:, at : at + 256] = part.astype(BF16)

    is_wide, is_square, is_narrow = (place.f == at for at in (wide_at, sq_at, nk_at))
    is_tall = (place.f == TALL_AT) & (place.core == 0)
    is_small = is_square | is_narrow

    @pl.when(is_wide)
    def _():
        received(0, lambda f: wide_s.at[f])
        for f in range(count):
            x_s[f * rows : (f + 1) * rows, :] = wide_s[f].astype(F32)

    @pl.when(is_tall)
    def _():
        received_tall()
        for f in range(0, count, 2):
            pair = jnp.concatenate([tall_s[f], tall_s[f + 1]], axis=0).astype(F32)
            x_s[:, 2 * f * tall : 2 * (f + 2) * tall] = pair.T

    @pl.when(is_small)
    def _():
        x_s[...] = jnp.zeros_like(x_s)

    @pl.when(is_square)
    def _():
        received(2, lambda f: sq_s.at[f])
        for f in range(count):
            x_s[f * rows : (f + 1) * rows, :QW] = sq_s[f].astype(F32)

    @pl.when(is_narrow)
    def _():
        received(3, lambda f: nk_s.at[f])
        for f in range(count):
            x_s[f * rows : (f + 1) * rows, :NARROW] = nk_s[f].astype(F32)

    @pl.when(is_wide | is_tall | is_small)
    def _():
        scaled()
        newton_schulz(x_s, low_s, gram_s, gram_low_s, poly_s)

    rate = MUON_RATE * math.sqrt(FF)
    small_rate = MUON_RATE * math.sqrt(D)

    def back(i, f, core):
        source = (
            wide_s.at[f], tall_s.at[f, pl.ds(core * tall, tall)] if i == 1 else None, sq_s.at[f], nk_s.at[f],
        )[i]
        return source, landing(i, core), (f, 2 * place.x + core)

    def landing(i, core):
        if i == 1:
            start = core * tall if isinstance(core, int) else pl.multiple_of(core * tall, 16)
            return d_out.at[pl.ds(start, tall)]
        return (gu_out, None, sq_out, nk_out)[i].at[core]

    def give(i, cores, act):
        for step in range(count):
            f = lax.rem(place.f + step, count)
            for n, core in enumerate(cores):
                source, target, device = back(i, f, core)
                if step == 0 and n == 0:
                    copy = pltpu.make_async_copy(source, target, own_sem.at[i])
                    act(copy, True)
                else:
                    slot = f + count * n
                    act(remote(source, target, out_send.at[i, slot], out_recv.at[i], device), False)

    def given(i, cores):
        give(i, cores, lambda copy, own: copy.start())
        give(i, cores, lambda copy, own: copy.wait() if own else copy.wait_send())

    @pl.when(is_wide)
    def _():
        for f in range(count):
            wide_s[f] = (x_s[f * rows : (f + 1) * rows, :] * rate).astype(BF16)
        given(0, (place.core,))

    @pl.when(is_tall)
    def _():
        for f in range(0, count, 2):
            pair = (x_s[:, 2 * f * tall : 2 * (f + 2) * tall] * rate).T
            tall_s[f] = pair[: 2 * tall].astype(BF16)
            tall_s[f + 1] = pair[2 * tall :].astype(BF16)
        given(1, (0, 1))

    @pl.when(is_square)
    def _():
        for f in range(count):
            sq_s[f] = (x_s[f * rows : (f + 1) * rows, :QW] * small_rate).astype(BF16)
        given(2, (place.core,))

    @pl.when(is_narrow)
    def _():
        for f in range(count):
            nk_s[f] = (x_s[f * rows : (f + 1) * rows, :NARROW] * small_rate).astype(BF16)
        given(3, (place.core,))

    makers = (is_wide, is_tall, is_square, is_narrow)

    def hand_over(i, core):
        target = landing(i, core)
        return remote(target, target, pair_send.at[i], pair_recv.at[i], place.sibling)

    for i in (2, 3, 1, 0):
        target = landing(i, place.core)

        def take(i=i, target=target):
            remote(target, target, pair_send.at[i], out_recv.at[i], place.sibling).wait_recv()

        pl.when(jnp.logical_not(makers[i]))(take)
        hand_over(i, place.core).start()
    for i in range(4):
        hand_over(i, 1 - place.core).wait_recv()
        hand_over(i, place.core).wait_send()


def muon_remote(grads, momenta, count):
    rows, tall = grads[0].shape[0], grads[2].shape[0] // 2
    pieces = ((rows, FF), (rows, QW), (rows, NARROW), (tall, D))
    return pl.pallas_call(
        partial(muon_kernel, count),
        out_shape=(
            jax.ShapeDtypeStruct((2, rows, QW), BF16),
            jax.ShapeDtypeStruct((2, rows, NARROW), BF16),
            jax.ShapeDtypeStruct((2, rows, FF), BF16),
            jax.ShapeDtypeStruct((2 * tall, D), BF16),
        ),
        in_specs=vmem(8),
        out_specs=tuple(vmem(4)),
        scratch_shapes=[pltpu.VMEM(p, BF16) for p in pieces]
        + [pltpu.VMEM((count,) + p, BF16) for p in pieces[:3]]
        + [
            pltpu.VMEM((count, 2 * tall, D), BF16),
            pltpu.VMEM((D, FF), F32),
            pltpu.VMEM((D, FF), BF16),
            pltpu.VMEM((D, D), F32),
            pltpu.VMEM((D, D), BF16),
            pltpu.VMEM((D, D), BF16),
            pltpu.SemaphoreType.DMA((4,)),
            pltpu.SemaphoreType.DMA((4, 2 * count)),
            pltpu.SemaphoreType.DMA((4,)),
            pltpu.SemaphoreType.DMA((4, 2 * count)),
            pltpu.SemaphoreType.DMA((4,)),
            pltpu.SemaphoreType.DMA((4,)),
            pltpu.SemaphoreType.DMA((4,)),
        ],
        compiler_params=pltpu.CompilerParams(
            collective_id=4, has_side_effects=True, vmem_limit_bytes=VMEM_LIMIT
        ),
        name="muon",
    )(*grads, *momenta)


def outputs_kernel(
    gain_rate, a_ref, gu_ref, d_ref, sq_ref, nk_ref, ugu_ref, ud_ref,
    gains_ref, gainm_ref, wq_ref, wkv_ref, wo_ref, wgu_ref, wd_ref,
    mq_ref, mkv_ref, mo_ref, mgu_ref, md_ref,
    gg_ref, gm_ref, gv_ref, qg_ref, qm_ref, qn_ref, kvg_ref, kvm_ref, kvn_ref,
    og_ref, om_ref, on_ref, gug_ref, gum_ref, gun_ref, dg_ref, dm_ref, dn_ref,
):
    def write(grad, momentum, weight, update, outs, index):
        grad = grad.astype(F32)
        outs[0][index] = grad
        outs[1][index] = MOMENTUM_DECAY * momentum[index] + grad
        outs[2][index] = weight[index] - update.astype(F32)

    every = (slice(None), slice(None))
    write(a_ref[:, :QW], mq_ref, wq_ref, sq_ref[0], (qg_ref, qm_ref, qn_ref), every)
    write(a_ref[:, O_AT : O_AT + QW], mo_ref, wo_ref, sq_ref[1], (og_ref, om_ref, on_ref), every)
    write(d_ref[...], md_ref, wd_ref, ud_ref[...], (dg_ref, dm_ref, dn_ref), every)
    for side in range(2):
        index = (slice(None), side, slice(None))
        at = side * O_AT + QW
        write(a_ref[:, at : at + KVW], mkv_ref, wkv_ref, nk_ref[side, :, :KVW], (kvg_ref, kvm_ref, kvn_ref), index)
        write(gu_ref[:, side * FF : side * FF + FF], mgu_ref, wgu_ref, ugu_ref[side], (gug_ref, gum_ref, gun_ref), index)
    gain = jnp.concatenate(
        [a_ref[:, at : at + 128].astype(F32).T[0:1, :] for at in (HALF, O_AT + HALF)], axis=0
    )
    moments = GAIN_DECAY * gainm_ref[...] + gain
    gg_ref[...] = gain
    gm_ref[...] = moments
    gv_ref[...] = gains_ref[...] - gain_rate * moments


def write_outputs(gain_rate, grads, updates, gains, gain_momentum, weights, momenta):
    shapes = [jax.ShapeDtypeStruct(gains.shape, F32)] * 3
    for w in weights:
        shapes += [jax.ShapeDtypeStruct(w.shape, F32)] * 3
    return pl.pallas_call(
        partial(outputs_kernel, gain_rate),
        out_shape=tuple(shapes),
        in_specs=vmem(19),
        out_specs=tuple(vmem(18)),
        compiler_params=pltpu.CompilerParams(vmem_limit_bytes=VMEM_LIMIT),
        name="outputs",
    )(*grads, *updates, gains, gain_momentum, *weights, *momenta)


def muon_updates(grads, momenta):
    if own_kernels():
        return muon_remote(grads, momenta, lax.axis_size("fsdp"))
    packed, gateup, down = (g.astype(F32) for g in grads)
    m_query, m_keyval, m_out, m_gateup, m_down = momenta

    def moment(momentum, grad):
        return MOMENTUM_DECAY * momentum + grad

    steps = muon_exchange(
        [
            moment(m_query, packed[:, :QW]),
            moment(m_keyval[:, 0], packed[:, QW:HALF]),
            moment(m_keyval[:, 1], packed[:, O_AT + QW : O_AT + HALF]),
            moment(m_out, packed[:, O_AT : O_AT + QW]),
            moment(m_gateup[:, 0], gateup[:, :FF]),
            moment(m_gateup[:, 1], gateup[:, FF:]),
            moment(m_down, down),
        ]
    )
    return (
        jnp.stack([steps[0], steps[3]]).astype(BF16),
        jnp.pad(jnp.stack(steps[1:3]), ((0, 0), (0, 0), (0, NARROW - KVW))).astype(BF16),
        jnp.stack(steps[4:6]).astype(BF16),
        steps[6].astype(BF16),
    )


def local(
    tokens, cotangent, lengths, assignment, norm_gains, gain_momentum, w_query, w_keyval, w_out,
    w_gateup, w_down, m_query, m_keyval, m_out, m_gateup, m_down,
):
    gain_rate = GAIN_SCALE / math.sqrt(assignment.shape[1] * BLK * 3 // 4 * lax.axis_size("fsdp"))
    inner, outer, turned, steps = rope_constants()
    weights = (w_query, w_keyval, w_out, w_gateup, w_down)
    momenta = (m_query, m_keyval, m_out, m_gateup, m_down)
    meta, x, cot, queries, packed, group_kv, gateup, down = begin(
        lengths, assignment, tokens, cotangent, norm_gains, weights, inner, outer
    )
    act, gres, gb, lowt, gq, dkv, gain, d_gateup, d_down = layer(
        meta, x, cot, queries, group_kv, packed, gateup, down, turned, steps
    )
    input_grad, grads = reduce_gradients(
        meta, x, packed, gq, dkv, gres, gb, lowt, gain, inner, outer, d_gateup, d_down
    )
    updates = muon_updates(grads, momenta)
    outs = write_outputs(gain_rate, grads, updates, norm_gains.T, gain_momentum.T, weights, momenta)
    return (act.T, input_grad.T) + tuple(g.T for g in outs[:3]) + tuple(outs[3:])


def solution(mesh):
    rows = P(("fsdp", "dp"), None)
    two, three = P("fsdp", None), P("fsdp", None, None)
    return jax.shard_map(
        local,
        mesh=mesh,
        in_specs=(rows, rows, two, two, two, two, two, three, two, three, two, two, three, two, three, two),
        out_specs=(rows, rows) + (two,) * 6 + (three,) * 3 + (two,) * 3 + (three,) * 3 + (two,) * 3,
        check_vma=False,
    )
```

```python
from functools import partial
import math

import jax
import jax.numpy as jnp
import numpy as np
from jax import lax
from jax.experimental import pallas as pl
from jax.experimental.pallas import tpu as pltpu
from jax.sharding import PartitionSpec as P

D = 576
HEADS = 9
KVH = 3
HD = 64
FF = 1536
BLK = 128
SEQS_G = 3
NS_STEPS = 5
QW = 576
KVW = 192
LONGEST = 12

EPS = 1e-05
THETA = 100000.0
MOMENTUM_DECAY = 0.95
GAIN_DECAY = 0.9
MUON_RATE = 0.03
GAIN_SCALE = 0.4
COEF_A = 3.4445
COEF_B = -4.775
COEF_C = 2.0315
SCALE = 1.0 / math.sqrt(HD)
HALF = 768
WIDE_A = 2 * (HALF + 128)
O_AT = HALF + 128
STEP = 256
F32, BF16 = jnp.float32, jnp.bfloat16


def vmem(count=1):
    return [pl.BlockSpec(memory_space=pltpu.VMEM)] * count


def dot(a, b):
    return lax.dot_general(a, b, (((1,), (0,)), ((), ())), preferred_element_type=F32)


def dot_nt(a, b):
    return lax.dot_general(a, b, (((1,), (1,)), ((), ())), preferred_element_type=F32)


def dot_tn(a, b):
    return lax.dot_general(a, b, (((0,), (0,)), ((), ())), preferred_element_type=F32)


META = 4 + LONGEST


def block_meta(lengths, assignment, first_slot, slots, meta):
    entries = assignment.shape[1]
    starts, sizes = [jnp.int32(0)], []
    for k in range(SEQS_G):
        sizes.append((lengths[0, k] + (BLK - 1)) // BLK)
        starts.append(starts[-1] + sizes[-1])

    @pl.loop(0, slots)
    def _(slot):
        mine = first_slot + slot

        def look(e, found):
            return jnp.where(assignment[0, e] == mine, e, found)

        entry = lax.fori_loop(0, entries, look, jnp.int32(0))
        first, size = entry, jnp.int32(0)
        for k in range(SEQS_G):
            inside = (entry >= starts[k]) & (entry < starts[k + 1])
            first = jnp.where(inside, starts[k], first)
            size = jnp.where(inside, lengths[0, k], size)
        place = entry - first
        meta[slot, 0] = place
        meta[slot, 1] = jnp.clip(size - place * BLK, 0, BLK)
        meta[slot, 2] = place // 2 + 1
        meta[slot, 3] = entry
        for step in range(LONGEST):
            key = assignment[0, jnp.minimum(first + step, entry)]
            meta[slot, 4 + step] = key


def rope_constants():
    freq = np.exp(np.arange(HD // 2, dtype=np.float64) * (-2.0 * math.log(THETA) / HD))
    lanes = np.tile(freq, 4)
    inner = np.arange(BLK)[:, None] * lanes[None, :]
    outer = BLK * np.arange(16)[:, None] * lanes[None, :]
    turned = inner.T[: HD // 2]
    steps = np.broadcast_to((BLK * np.arange(LONGEST))[:, None, None] * freq[None, :, None], (LONGEST, HD // 2, BLK))
    return tuple(
        np.stack([np.cos(angle), np.sin(angle)]).astype(np.float32)
        for angle in (inner, outer, turned, steps)
    )


def lane_index(rows):
    return lax.broadcasted_iota(jnp.int32, (rows, 128), 1)


def rope_tables(meta, slot, inner_ref, outer_ref):
    place, live = meta[slot, 0], meta[slot, 1]
    co, so = outer_ref[0, pl.ds(place, 1), :], outer_ref[1, pl.ds(place, 1), :]
    ci, si = inner_ref[0], inner_ref[1]
    lane = lane_index(BLK)
    row = lax.broadcasted_iota(jnp.int32, (BLK, 128), 0)
    turned = (row < live) & (lane < HD)
    cosine = jnp.where(turned, co * ci - so * si, 1.0)
    sine = jnp.where(turned, so * ci + co * si, 0.0)
    return cosine, jnp.where(lane < HD // 2, sine, 0.0), jnp.where(lane < HD // 2, 0.0, sine)


def rope(tile, tables):
    cosine, sine_low, sine_high = tables
    return (
        tile * cosine - pltpu.roll(tile, 128 - HD // 2, 1) * sine_low
        + pltpu.roll(tile, HD // 2, 1) * sine_high
    )


def rope_back(tile, tables):
    cosine, sine_low, sine_high = tables
    return (
        tile * cosine + pltpu.roll(tile, 128 - HD // 2, 1) * sine_low
        - pltpu.roll(tile, HD // 2, 1) * sine_high
    )


def swap(tile):
    return pltpu.roll(tile, HD, 1)


def gain_row(packed_ref, at):
    return packed_ref[:, at : at + 128].astype(F32).T[0:1, :]


def project_rows(meta, i, x_ref, wa_ref, gain, inner_ref, outer_ref, q_ref, kv_ref):
    low_lane = lane_index(BLK) < HD
    x = x_ref[i * STEP : (i + 1) * STEP, :].astype(F32)
    inv = lax.rsqrt(jnp.mean(x * x, axis=1, keepdims=True) + EPS)
    normed = (x * inv * gain).astype(BF16)
    qk = dot(normed, wa_ref[:, :HALF])
    ov = dot(normed, wa_ref[:, O_AT + 512 : O_AT + HALF])
    for b in range(STEP // BLK):
        tables = rope_tables(meta, i * (STEP // BLK) + b, inner_ref, outer_ref)
        rows = slice(i * STEP + b * BLK, i * STEP + (b + 1) * BLK)
        part = slice(b * BLK, (b + 1) * BLK)
        tiles = [qk[part, 128 * t : 128 * t + 128] for t in range(6)]
        for head in range(HEADS):
            tile = tiles[head // 2]
            tile = jnp.where(low_lane, swap(tile) if head % 2 else tile, 0.0)
            q_ref[rows, 128 * head : 128 * head + 128] = (rope(tile, tables) * SCALE).astype(BF16)
        values = [ov[part, :128], ov[part, 128:]]
        pairs = (
            (swap(tiles[4]), values[0]),
            (tiles[5], swap(values[1])),
            (swap(tiles[5]), values[1]),
        )
        for h in range(KVH):
            tile = jnp.where(low_lane, *pairs[h])
            kv_ref[rows, 128 * h : 128 * h + 128] = rope(tile, tables).astype(BF16)


def chunk_bias(meta, slot, chunk):
    key = lax.broadcasted_iota(jnp.int32, (2 * BLK, BLK), 0) + chunk * (2 * BLK)
    query = lax.broadcasted_iota(jnp.int32, (2 * BLK, BLK), 1) + meta[slot, 0] * BLK
    live_end = meta[slot, 0] * BLK + meta[slot, 1]
    allowed = (key <= query) & ((query < live_end) | (key == query))
    bias = jnp.where(allowed, 0.0, -1e30)
    return jnp.concatenate([bias] * (HEADS // KVH), axis=1)


def chunk_blocks(meta, slot, chunk):
    return meta[slot, 4 + 2 * chunk], meta[slot, 5 + 2 * chunk]


def key_tile(kv_ref, blocks, h):
    lanes = slice(128 * h, 128 * h + 128)
    rows = [pl.ds(pl.multiple_of(block * BLK, BLK), BLK) for block in blocks]
    return jnp.concatenate([kv_ref[r, lanes] for r in rows], axis=0)


def turned_tile(kv_t_s, blocks, h):
    return jnp.concatenate([kv_t_s[block, h] for block in blocks], axis=1)


def stacked(ref, rows, h):
    at = 128 * (HEADS // KVH) * h
    return jnp.concatenate(
        [ref[rows, at + 128 * j : at + 128 * j + 128] for j in range(HEADS // KVH)], axis=0
    )


def turn_keys(kv_ref, kv_t_s):
    @pl.loop(0, kv_t_s.shape[0])
    def _(block):
        rows = pl.ds(pl.multiple_of(block * BLK, BLK), BLK)
        for h in range(KVH):
            kv_t_s[block, h] = kv_ref[rows, 128 * h : 128 * h + 128].T


def over_chunks(meta, slot, count, visit):
    open_chunks = jnp.where(meta[slot, 1] == BLK, count - 1, 0)

    @pl.loop(0, open_chunks)
    def _(chunk):
        visit(chunk, None)

    @pl.loop(open_chunks, count)
    def _(chunk):
        visit(chunk, chunk_bias(meta, slot, chunk))


def attention_forward(meta, q_ref, kv_ref, kv_t_s, q_t_s, low_ref, lowt_ref, mixed_s, lse_s, peak_s, accum_s):
    group = HEADS // KVH
    turn_keys(kv_ref, kv_t_s)

    @pl.loop(0, q_ref.shape[0] // BLK)
    def _(slot):
        rows = pl.ds(pl.multiple_of(slot * BLK, BLK), BLK)
        peak_s[...] = jnp.full_like(peak_s, -1e30)
        accum_s[...] = jnp.zeros_like(accum_s)
        key_row = lax.broadcasted_iota(jnp.int32, (BLK, 2 * BLK), 0) < HD
        for head in range(HEADS):
            h, j = head // group, head % group
            q_t_s[slot, h, :, BLK * j : BLK * j + BLK] = q_ref[rows, 128 * head : 128 * head + 128].T

        def visit(chunk, bias):
            blocks = chunk_blocks(meta, slot, chunk)
            for h in range(KVH):
                scores = dot(key_tile(kv_ref, blocks, h), q_t_s[slot, h])
                scores = scores if bias is None else scores + bias
                old = peak_s[h, 0:1, :]
                new = jnp.maximum(old, jnp.max(scores, axis=0, keepdims=True))
                probs = jnp.exp(scores - new).astype(BF16)
                tile = turned_tile(kv_t_s, blocks, h)
                ones = jnp.where(key_row, jnp.ones_like(tile), tile)
                accum_s[h] = accum_s[h] * jnp.exp(old - new) + dot(ones, probs)
                peak_s[h, 0:1, :] = new

        over_chunks(meta, slot, meta[slot, 2], visit)

        for h in range(KVH):
            total = accum_s[h, 0:1, :]
            lse_s[slot, h, 0:1, :] = peak_s[h, 0:1, :] + jnp.log(total)
            mixed = accum_s[h, HD:, :] / total
            for j in range(group):
                head = h * group + j
                mixed_s[slot, HD * head : HD * head + HD, :] = mixed[:, BLK * j : BLK * j + BLK]
        lowt_ref[:, rows] = mixed_s[slot].astype(BF16)
        low_ref[rows, :] = mixed_s[slot].T.astype(BF16)


def feed_forward(
    meta, x_ref, cot_ref, wa_ref, wgu_ref, wd_ref, actt_ref, gres_ref, gb_ref, gain_ref,
    low_s, mixed_s, do_s, do_t_s, delta_s, second_s, second_t_s, grad_gu_s, hidden_s, gm_s, wide_s,
):
    group = HEADS // KVH
    gain = gain_row(wa_ref, O_AT + HALF)
    high_lane = lane_index(BLK) >= HD
    gain_ref[...] = jnp.zeros_like(gain_ref)
    w_out = wa_ref[:, O_AT : O_AT + QW]
    rows_all = x_ref.shape[0]
    blocks = STEP // BLK

    def living(i):
        row = lax.broadcasted_iota(jnp.int32, (BLK, 1), 0)
        return jnp.concatenate([(row < meta[i * blocks + b, 1]).astype(F32) for b in range(blocks)], axis=0)

    def normalized(i):
        residual = gres_ref[i * STEP : (i + 1) * STEP, :]
        inv = lax.rsqrt(jnp.mean(residual * residual, axis=1, keepdims=True) + EPS)
        return residual * inv, inv

    for i in range(rows_all // STEP):
        rows = slice(i * STEP, (i + 1) * STEP)
        gres_ref[rows, :] = x_ref[rows, :].astype(F32) + dot(low_s[rows, :], w_out)
        second = (normalized(i)[0] * gain).astype(BF16)
        second_s[rows, :] = second
        second_t_s[:, rows] = second.T
        gm_s[rows, :] = (cot_ref[rows, :].astype(F32) * living(i)).astype(BF16)

    width = 256

    @pl.loop(0, FF // width)
    def _(c):
        at = pl.multiple_of(c * width, width)
        here, there = pl.ds(at, width), pl.ds(pl.multiple_of(FF + at, width), width)
        gate, up = dot(second_s[...], wgu_ref[:, here]), dot(second_s[...], wgu_ref[:, there])
        grad_hidden = dot_nt(gm_s[...], wd_ref[here, :])
        sigma = jax.nn.sigmoid(gate)
        swish = gate * sigma
        hidden_s[:, here] = (swish * up).astype(BF16)
        grad_gu_s[:, there] = (grad_hidden * swish).astype(BF16)
        grad_gu_s[:, here] = (grad_hidden * up * (sigma * (1.0 + gate * (1.0 - sigma)))).astype(BF16)

    cuts = [(at, min(256, D - at)) for at in range(0, D, 256)]
    for at, wide in cuts:
        wide_s[:, at : at + wide] = dot_nt(grad_gu_s[...], wgu_ref[at : at + wide, :])
    for i in range(rows_all // STEP):
        rows = slice(i * STEP, (i + 1) * STEP)
        out = gres_ref[rows, :] + dot(hidden_s[rows, :], wd_ref[...])
        actt_ref[:, rows] = out.astype(BF16).T
        norm, inv = normalized(i)
        grad_second = wide_s[rows, :]
        grad_final = cot_ref[rows, :].astype(F32) * living(i)
        scaled = grad_second * gain
        grad_res = grad_final + inv * (scaled - norm * jnp.mean(scaled * norm, axis=1, keepdims=True))
        gres_ref[rows, :] = grad_res
        grad_branch = grad_res.astype(BF16)
        gb_ref[rows, :QW] = grad_branch
        gb_ref[rows, QW:] = jnp.zeros((STEP, 128 - HD), BF16)
        gain_ref[0:1, :] += jnp.sum(grad_second * norm, axis=0, keepdims=True)
    for at, wide in cuts:
        wide_s[:, at : at + wide] = dot_nt(gb_ref[:, :QW], w_out[at : at + wide, :])
    for i in range(rows_all // STEP):
        grad_att_low = wide_s[i * STEP : (i + 1) * STEP, :].astype(BF16)
        grad_att_t = grad_att_low.T
        grad_att = grad_att_low.astype(F32)
        for b in range(blocks):
            slot = i * blocks + b
            here = slice(i * STEP + b * BLK, i * STEP + (b + 1) * BLK)
            part = slice(b * BLK, (b + 1) * BLK)
            do_t_s[slot] = grad_att_t[:, part]
            product = grad_att_t[:, part].astype(F32) * mixed_s[slot]
            for head in range(HEADS):
                at = 128 * (head // 2)
                if head == HEADS - 1:
                    tile = jnp.concatenate([grad_att[part, at : at + HD]] * 2, axis=1)
                else:
                    tile = grad_att[part, at : at + 128]
                    tile = tile if head % 2 else swap(tile)
                tile = jnp.where(high_lane, tile, 0.0).astype(BF16)
                do_s[here, 128 * head : 128 * head + 128] = tile
                h, j = head // group, head % group
                delta_s[slot, h, 0:1, BLK * j : BLK * j + BLK] = jnp.sum(
                    product[HD * head : HD * head + HD, :], axis=0, keepdims=True
                )


def weight_grads(dgu_ref, dd_ref, second_t_s, grad_gu_s, hidden_s, gm_s):
    width = 512

    @pl.loop(0, 2 * FF // width)
    def _(c):
        here = pl.ds(pl.multiple_of(c * width, width), width)
        dgu_ref[:, here] = dot(second_t_s[...], grad_gu_s[:, here]).astype(BF16)

    @pl.loop(0, FF // width)
    def _(c):
        here = pl.ds(pl.multiple_of(c * width, width), width)
        dd_ref[here, :] = dot_tn(hidden_s[:, here], gm_s[...]).astype(BF16)


def in_parts(row):
    parts, rest = [], row
    for _ in range(3):
        parts.append(rest.astype(BF16).astype(F32))
        rest = rest - parts[-1]
    index = lax.broadcasted_iota(jnp.int32, (16, row.shape[1]), 0)
    table = jnp.zeros(index.shape, F32)
    for i, part in enumerate(parts):
        table = jnp.where(index == i, part, table)
    return table.astype(BF16)


def attention_backward(
    meta, q_ref, kv_ref, kv_t_s, q_t_s, turned_ref, steps_ref, do_s, do_t_s, lse_s, delta_s, gq_ref, dkv_s, dq_s,
    both_s, both_t_s,
):
    group = HEADS // KVH
    tall = group * BLK
    dkv_s[...] = jnp.zeros_like(dkv_s)
    both_t_s[...] = jnp.zeros_like(both_t_s)

    @pl.loop(0, q_ref.shape[0] // BLK)
    def _(slot):
        rows = pl.ds(pl.multiple_of(slot * BLK, BLK), BLK)
        dq_s[...] = jnp.zeros_like(dq_s)
        ones = jnp.where(lane_index(2 * BLK) < 3, 1.0, 0.0).astype(BF16)
        for h in range(KVH):
            both_s[h, :tall] = stacked(q_ref, rows, h)
            both_s[h, tall:] = stacked(do_s, rows, h)
            both_t_s[h, :BLK, :tall] = q_t_s[slot, h]
            for j in range(group):
                head = h * group + j
                both_t_s[h, HD:BLK, tall + BLK * j : tall + BLK * j + BLK] = do_t_s[slot, HD * head : HD * head + HD]
            both_t_s[h, BLK : BLK + 16, :tall] = in_parts(-lse_s[slot, h, 0:1, :])
            both_t_s[h, BLK : BLK + 16, tall:] = in_parts(-delta_s[slot, h, 0:1, :])

        def visit(chunk, bias):
            blocks = chunk_blocks(meta, slot, chunk)
            one, two = (pl.ds(pl.multiple_of(block * BLK, BLK), BLK) for block in blocks)
            for h in range(KVH):
                lanes = slice(128 * h, 128 * h + 128)
                wide = jnp.concatenate([key_tile(kv_ref, blocks, h), ones], axis=1)
                products = dot(wide, both_t_s[h])
                scores = products[:, :tall]
                probs = jnp.exp(scores if bias is None else scores + bias)
                grads = (probs * products[:, tall:]).astype(BF16)
                dq_s[h] += dot(turned_tile(kv_t_s, blocks, h), grads)
                sides = jnp.concatenate([grads, probs.astype(BF16)], axis=1)
                terms = dot(sides, both_s[h])
                dkv_s[one, lanes] += terms[:BLK]
                dkv_s[two, lanes] += terms[BLK:]

        over_chunks(meta, slot, jnp.where(meta[slot, 1] > 0, meta[slot, 2], 0), visit)

        place = meta[slot, 0]
        co, so, ci, si = steps_ref[0, place], steps_ref[1, place], turned_ref[0], turned_ref[1]
        turned = lax.broadcasted_iota(jnp.int32, (HD // 2, BLK), 1) < meta[slot, 1]
        cosine = jnp.where(turned, co * ci - so * si, 1.0) * SCALE
        sine = jnp.where(turned, so * ci + co * si, 0.0) * SCALE
        parts = []
        for h in range(KVH):
            for j in range(group):
                one = dq_s[h, : HD // 2, BLK * j : BLK * j + BLK]
                two = dq_s[h, HD // 2 : HD, BLK * j : BLK * j + BLK]
                parts += [one * cosine + two * sine, two * cosine - one * sine]
        gq_ref[rows, :QW] = jnp.concatenate(parts, axis=0).T.astype(BF16)
        gq_ref[rows, QW:] = jnp.zeros((BLK, HD), BF16)


def layer_kernel(
    meta, q_ref, kv_ref, turned_ref, steps_ref, x_hbm, cot_hbm, wa_hbm, gu_hbm, d_hbm,
    gq_ref, dkv_ref, gain_ref, lowt_hbm, actt_hbm, gres_hbm, gb_hbm, dgu_hbm, dd_hbm,
    mixed_s, lse_s, delta_s, peak_s, accum_s, do_s, second_s, second_t_s, grad_gu_s, hidden_s, gm_s, dkv_s, low_s,
    both_s, both_t_s, kv_t_s, q_t_s, do_t_s, wide_s, x_s, cot_s, wa_s, wgu_s, wd_s, lowt_s, actt_s, gres_s, gb_s, dgu_s, dd_s, load_sem, store_sem,
):
    loads = [
        pltpu.make_async_copy(source, target, load_sem.at[i])
        for i, (source, target) in enumerate(
            ((x_hbm, x_s), (wa_hbm, wa_s), (cot_hbm, cot_s), (gu_hbm, wgu_s), (d_hbm, wd_s))
        )
    ]
    stores = [
        pltpu.make_async_copy(source, target, store_sem.at[i])
        for i, (source, target) in enumerate(
            (
                (lowt_s, lowt_hbm), (actt_s, actt_hbm), (gres_s, gres_hbm), (gb_s, gb_hbm),
                (dgu_s, dgu_hbm), (dd_s, dd_hbm),
            )
        )
    ]
    for copy in loads:
        copy.start()
    attention_forward(meta, q_ref, kv_ref, kv_t_s, q_t_s, low_s, lowt_s, mixed_s, lse_s, peak_s, accum_s)
    stores[0].start()
    for copy in loads:
        copy.wait()
    feed_forward(
        meta, x_s, cot_s, wa_s, wgu_s, wd_s, actt_s, gres_s, gb_s, gain_ref,
        low_s, mixed_s, do_s, do_t_s, delta_s, second_s, second_t_s, grad_gu_s, hidden_s, gm_s, wide_s,
    )
    for copy in stores[1:4]:
        copy.start()
    weight_grads(dgu_s, dd_s, second_t_s, grad_gu_s, hidden_s, gm_s)
    for copy in stores[4:]:
        copy.start()
    attention_backward(
        meta, q_ref, kv_ref, kv_t_s, q_t_s, turned_ref, steps_ref, do_s, do_t_s, lse_s, delta_s, gq_ref, dkv_s,
        accum_s, both_s, both_t_s,
    )
    dkv_ref[...] = dkv_s[...].astype(BF16)
    for copy in stores:
        copy.wait()


VMEM_LIMIT = 62 << 20


def layer(meta, tokens, cotangent, queries, keyval, packed, gateup, down, turned, steps):
    rows, slots, group = tokens.shape[0], tokens.shape[0] // BLK, HEADS // KVH
    keys = keyval.shape[0]
    anywhere = pl.BlockSpec(memory_space=pl.ANY)
    results = [((QW, rows), BF16), ((D, rows), BF16), ((rows, D), F32), ((rows, QW + HD), BF16)]
    results += [((D, 2 * FF), BF16), ((FF, D), BF16)]
    return pl.pallas_call(
        layer_kernel,
        out_shape=(
            jax.ShapeDtypeStruct((rows, QW + HD), BF16),
            jax.ShapeDtypeStruct((keys, 2 * KVW), BF16),
            jax.ShapeDtypeStruct((8, D), F32),
        )
        + tuple(jax.ShapeDtypeStruct(*r) for r in results),
        in_specs=[pl.BlockSpec(memory_space=pltpu.SMEM)] + vmem(4) + [anywhere] * 5,
        out_specs=tuple(vmem(3)) + (anywhere,) * 6,
        scratch_shapes=[
            pltpu.VMEM((slots, QW, BLK), F32),
            pltpu.VMEM((slots, KVH, 8, group * BLK), F32),
            pltpu.VMEM((slots, KVH, 8, group * BLK), F32),
            pltpu.VMEM((KVH, 8, group * BLK), F32),
            pltpu.VMEM((KVH, BLK, group * BLK), F32),
            pltpu.VMEM((rows, 128 * HEADS), BF16),
            pltpu.VMEM((rows, D), BF16),
            pltpu.VMEM((D, rows), BF16),
            pltpu.VMEM((rows, 2 * FF), BF16),
            pltpu.VMEM((rows, FF), BF16),
            pltpu.VMEM((rows, D), BF16),
            pltpu.VMEM((keys, 2 * KVW), F32),
            pltpu.VMEM((rows, QW), BF16),
            pltpu.VMEM((KVH, 2 * group * BLK, 128), BF16),
            pltpu.VMEM((KVH, 256, 2 * group * BLK), BF16),
            pltpu.VMEM((keys // BLK, KVH, BLK, BLK), BF16),
            pltpu.VMEM((slots, KVH, BLK, group * BLK), BF16),
            pltpu.VMEM((slots, QW, BLK), BF16),
            pltpu.VMEM((rows, D), F32),
            pltpu.VMEM((rows, D), BF16),
            pltpu.VMEM((rows, D), BF16),
            pltpu.VMEM((D, WIDE_A), BF16),
            pltpu.VMEM((D, 2 * FF), BF16),
            pltpu.VMEM((FF, D), BF16),
        ]
        + [pltpu.VMEM(*r) for r in results]
        + [pltpu.SemaphoreType.DMA((5,)), pltpu.SemaphoreType.DMA((6,))],
        compiler_params=pltpu.CompilerParams(vmem_limit_bytes=VMEM_LIMIT),
        name="layer",
    )(meta, queries, keyval, turned, steps, tokens, cotangent, packed, gateup, down)


def input_grad_rows(
    meta, i, x_ref, wa_ref, gain, gq_ref, dkv_ref, gres_ref, inner_ref, outer_ref, int_ref, normed_s, first_s, values_s
):
    low_lane = lane_index(BLK) < HD
    rows = slice(i * STEP, (i + 1) * STEP)
    x = x_ref[rows, :].astype(F32)
    inv = lax.rsqrt(jnp.mean(x * x, axis=1, keepdims=True) + EPS)
    norm = x * inv
    normed_s[:, rows] = (norm * gain).astype(BF16).T
    first_s[rows, :512] = gq_ref[rows, :512]
    for b in range(STEP // BLK):
        here = slice(i * STEP + b * BLK, i * STEP + (b + 1) * BLK)
        tables = rope_tables(meta, i * (STEP // BLK) + b, inner_ref, outer_ref)
        tiles = [
            rope_back(dkv_ref[here, 128 * h : 128 * h + 128].astype(F32), tables) for h in range(KVH)
        ]
        last = gq_ref[here, 512:640].astype(F32)
        first_s[here, 512:640] = jnp.where(low_lane, last, swap(tiles[0])).astype(BF16)
        first_s[here, 640:768] = jnp.where(low_lane, tiles[1], swap(tiles[2])).astype(BF16)
        values_s[here, :128] = jnp.where(low_lane, 0.0, tiles[0]).astype(BF16)
        values_s[here, 128:] = jnp.where(low_lane, swap(tiles[1]), tiles[2]).astype(BF16)
    grad_normed = dot_nt(first_s[rows, :], wa_ref[:, :HALF]) + dot_nt(
        values_s[rows, :], wa_ref[:, O_AT + 512 : O_AT + HALF]
    )
    scaled = grad_normed * gain
    grad = gres_ref[rows, :] + inv * (scaled - norm * jnp.mean(scaled * norm, axis=1, keepdims=True))
    int_ref[:, rows] = grad.T
    return jnp.sum(grad_normed * norm, axis=0, keepdims=True)


def put_rows(da_ref, at, value):
    shards, rows = da_ref.shape[:2]
    for f in range(shards):
        da_ref[f, :, at : at + value.shape[1]] = value[f * rows : (f + 1) * rows].astype(BF16)


def out_grads(da_ref, lowt_ref, gb_ref):
    for c in range(0, 512, 256):
        put_rows(da_ref, O_AT + c, dot(lowt_ref[...], gb_ref[:, c : c + 256]))


def packed_grads(da_ref, normed_s, first_s, values_s, lowt_ref, gb_ref, gains, gain_ref):
    for c in range(0, HALF, 256):
        put_rows(da_ref, c, dot(normed_s[...], first_s[:, c : c + 256]))
    both = dot(lowt_ref[...], gb_ref[:, 512:640]) + dot(normed_s[...], values_s[:, :128])
    put_rows(da_ref, O_AT + 512, both)
    put_rows(da_ref, O_AT + 640, dot(normed_s[...], values_s[:, 128:]))
    put_rows(da_ref, HALF, jnp.broadcast_to(gains, (128, D)).T)
    put_rows(da_ref, O_AT + HALF, jnp.broadcast_to(gain_ref[0:1, :], (128, D)).T)


def finish_kernel(
    meta, x_ref, wa_ref, gq_ref, dkv_ref, gres_ref, gb_ref, lowt_ref, gain_ref, inner_ref, outer_ref,
    int_ref, da_ref, normed_s, first_s, values_s,
):
    gain = gain_row(wa_ref, HALF)
    gains = jnp.zeros((1, D), F32)
    for i in range(x_ref.shape[0] // STEP):
        gains = gains + input_grad_rows(
            meta, i, x_ref, wa_ref, gain, gq_ref, dkv_ref, gres_ref, inner_ref, outer_ref, int_ref,
            normed_s, first_s, values_s,
        )
    out_grads(da_ref, lowt_ref, gb_ref)
    packed_grads(da_ref, normed_s, first_s, values_s, lowt_ref, gb_ref, gains, gain_ref)


def finish_scratch(rows):
    return [pltpu.VMEM((D, rows), BF16), pltpu.VMEM((rows, HALF), BF16), pltpu.VMEM((rows, 256), BF16)]


def finish(meta, tokens, packed, gq, dkv, gres, gb, lowt, gain, inner, outer):
    rows = tokens.shape[0]
    input_grad, d_packed = pl.pallas_call(
        finish_kernel,
        out_shape=(
            jax.ShapeDtypeStruct((D, rows), F32),
            jax.ShapeDtypeStruct((1, D, WIDE_A), BF16),
        ),
        in_specs=[pl.BlockSpec(memory_space=pltpu.SMEM)] + vmem(10),
        out_specs=tuple(vmem(2)),
        scratch_shapes=finish_scratch(rows),
        compiler_params=pltpu.CompilerParams(vmem_limit_bytes=VMEM_LIMIT),
        name="finish",
    )(meta, tokens, packed, gq, dkv, gres, gb, lowt, gain, inner, outer)
    return input_grad, d_packed[0]


def pack(w_query, w_keyval, w_out, w_gateup, w_down, norm_gains):
    rows = w_query.shape[0]
    spread = [jnp.broadcast_to(norm_gains[:, g : g + 1], (rows, 128)) for g in range(2)]
    packed = jnp.concatenate(
        [w_query, w_keyval[:, 0], spread[0], w_out, w_keyval[:, 1], spread[1]], axis=1
    )
    return packed.astype(BF16), w_gateup.reshape(rows, 2 * FF).astype(BF16), w_down.astype(BF16)


def for_sending(value):
    return jax.tree.map(lambda a: a.astype(jnp.bfloat16) if a.dtype == jnp.float32 else a, value)


def orthogonal(matrix):
    flipped = matrix.shape[0] > matrix.shape[1]
    iterate = matrix.T if flipped else matrix
    iterate = iterate / (jnp.sqrt(jnp.sum(iterate * iterate)) + 1e-07)
    for turn in range(NS_STEPS):
        gram_matrix = jnp.dot(iterate, iterate.T, precision=lax.Precision.HIGHEST)
        polynomial = COEF_B * gram_matrix + COEF_C * jnp.dot(
            gram_matrix, gram_matrix, precision=lax.Precision.HIGHEST
        )
        iterate = COEF_A * iterate + jnp.dot(polynomial, iterate, precision=lax.Precision.HIGHEST)
    return iterate.T if flipped else iterate


def muon_step(matrix):
    return MUON_RATE * math.sqrt(max(matrix.shape[0], matrix.shape[1])) * orthogonal(matrix)


def owner_branch(matrix_rows, matrix_cols, widest, received):
    group_size = received.shape[0]
    shard_size = matrix_rows * matrix_cols // group_size
    full_matrix = received[:, :shard_size].reshape(matrix_rows, matrix_cols)
    update_rows = muon_step(full_matrix).reshape(group_size, shard_size)
    return jnp.pad(update_rows, ((0, 0), (0, widest - shard_size)))


def zero_branch(received):
    return jnp.zeros_like(received)


def muon_exchange(pieces):
    fsdp_size, fsdp_index = lax.axis_size("fsdp"), lax.axis_index("fsdp")
    flat_sizes = [piece.size for piece in pieces]
    widest = max(flat_sizes)
    padded = [jnp.pad(piece.reshape(-1), (0, widest - piece.size)) for piece in pieces]
    outgoing = jnp.stack(padded + [jnp.zeros((widest,), F32)] * (fsdp_size - len(pieces)))
    received = lax.all_to_all(
        outgoing.astype(BF16), "fsdp", split_axis=0, concat_axis=0, tiled=True
    ).astype(F32)
    branches = [
        partial(owner_branch, piece.shape[0] * fsdp_size, piece.shape[1], widest)
        for piece in pieces
    ] + [zero_branch]
    update_rows = lax.switch(jnp.minimum(fsdp_index, len(pieces)), branches, received)
    returned = lax.all_to_all(
        update_rows.astype(BF16), "fsdp", split_axis=0, concat_axis=0, tiled=True
    ).astype(F32)
    return [returned[m, : flat_sizes[m]].reshape(pieces[m].shape) for m in range(len(pieces))]


def gather_rows_xla(shard):
    return lax.all_gather(shard, "fsdp", axis=0, tiled=True)


def reduce_rows_xla(grads):
    return lax.psum(lax.psum_scatter(grads, "fsdp", scatter_dimension=0, tiled=True), "dp")


START_SPLIT = (False, True, True, False)
REDUCE_SPLIT = (False, True, False, False)
START_ORDER = (
    ("z", 0, 0), ("z", 1, 0), ("z", 2, 0), ("prep",), ("side", 0, 0), ("z", 3, 0), ("z", 0, 1), ("z", 0, 2),
    ("side", 1, 0), ("side", 2, 0), ("z", 1, 1), ("side", 3, 0), ("z", 1, 2), ("side", 0, 2), ("side", 0, 1),
    ("wa",), ("side", 1, 2), ("side", 1, 1), ("proj", 0), ("z", 0, 3), ("z", 2, 2), ("z", 2, 1), ("proj", 1),
    ("side", 2, 2), ("cross", 0, 2), ("z", 1, 3), ("z", 3, 2), ("side", 3, 2), ("side", 2, 1), ("proj", 2),
    ("z", 3, 1), ("z", 2, 3), ("cross", 1, 2), ("z", 3, 3), ("side", 2, 3), ("side", 0, 3), ("side", 1, 3),
    ("side", 3, 1), ("cross", 0, 1), ("cross", 1, 1), ("kvpass", 0), ("cross", 3, 2), ("side", 3, 3),
    ("cross", 2, 2), ("cross", 2, 1), ("kvpass", 1), ("kvpass", 2), ("cross", 3, 1),
)
REDUCE_ORDER = (
    ("pp", 0, 0), ("pp", 1, 0), ("pp", 3, 0), ("P", 0, 3), ("P", 0, 2), ("P", 0, 1), ("pp", 1, 1),
    ("kvp", 0), ("pp", 0, 1), ("P", 1, 3), ("P", 1, 1), ("kvp", 1), ("P", 3, 2), ("pp", 2, 0), ("kvx",),
    ("S", 0, 1), ("Z", 0, 3), ("Z", 1, 3), ("S", 1, 1), ("P", 2, 3), ("pp", 3, 1), ("P", 2, 2), ("Z", 0, 2),
    ("da1",), ("pp", 2, 1), ("fin", 0), ("Z", 0, 1), ("P", 2, 1), ("fin", 1), ("Z", 1, 1), ("P", 1, 2),
    ("fin", 2), ("Z", 2, 3), ("P", 3, 3), ("da2",), ("S", 2, 1), ("P", 3, 1), ("pp0",), ("Z", 1, 2),
    ("Z", 2, 2), ("S", 3, 1), ("P", 0, 0), ("P", 1, 0), ("Z", 3, 3), ("Z", 2, 1), ("Z", 3, 2), ("P", 2, 0),
    ("Z", 0, 0), ("Z", 3, 1), ("F", 3), ("P", 3, 0), ("Z", 1, 0), ("Z", 2, 0), ("F", 2), ("F", 1),
    ("Z", 3, 0), ("F", 0),
)


WIDE_AT, TALL_AT = (2, 5), 3
SQUARE_AT, NARROW_AT = (0, 7), (6, 1)
NARROW = 256


def by_core(pair, core):
    return pair[0] + (pair[1] - pair[0]) * core


def newton_schulz(x_s, low_s, gram_s, gram_low_s, poly_s, factor):
    size, width = x_s.shape
    cuts = [(at, min(256, size - at)) for at in range(0, size, 256)]

    @pl.loop(0, NS_STEPS)
    def _(step):
        shift = jnp.where(step >= NS_STEPS - 2, 1.0, 0.0)
        first = jnp.where(step == 0, factor, 1.0)
        for at, wide in cuts:
            gram = dot_nt(low_s[...], low_s[at : at + wide, :]) * (first * first)
            row = lax.broadcasted_iota(jnp.int32, (size, wide), 0)
            column = lax.broadcasted_iota(jnp.int32, (size, wide), 1) + at
            gram = gram - jnp.where(row == column, shift, 0.0)
            gram_s[:, at : at + wide] = gram
            gram_low_s[:, at : at + wide] = gram.astype(BF16)
        for at, wide in cuts:
            square = dot(gram_low_s[...], gram_low_s[:, at : at + wide])
            poly = (COEF_B + 2.0 * COEF_C * shift) * gram_s[:, at : at + wide] + COEF_C * square
            poly_s[:, at : at + wide] = (poly * first).astype(BF16)
        keep = (COEF_A + COEF_B * shift + COEF_C * shift * shift) * first
        for at in range(0, width, 256):
            lanes = slice(at, at + 256)
            new = keep * x_s[:, lanes] + dot(poly_s[...], low_s[:, lanes])
            x_s[:, lanes] = new
            low_s[:, lanes] = new.astype(BF16)


def muon_part(
    place, a_ref, gu_ref, d_ref, mq_ref, mkv_ref, mo_ref, mgu_ref, md_ref,
    sq_out, nk_out, gu_out, d_out,
    my_gu, my_sq, my_nk, my_d, wide_s, sq_s, nk_s, tall_s, x_s, low_s, gram_s, gram_low_s, poly_s,
    in_send, in_recv, own_sem, out_send, out_recv, pair_send, pair_recv,
):
    count = 2 * place.lines
    rows, tall = my_gu.shape[0], my_d.shape[0]

    def moment(momentum, grad):
        return (MOMENTUM_DECAY * momentum + grad.astype(F32)).astype(BF16)

    my_nk[...] = jnp.zeros_like(my_nk)

    def moments_of(core, m_square):
        my_gu[...] = moment(mgu_ref[:, core, :], gu_ref[:, core * FF : core * FF + FF])
        at = core * O_AT
        my_sq[...] = moment(m_square[...], a_ref[:, at : at + QW])
        my_nk[:, :KVW] = moment(mkv_ref[:, core, :], a_ref[:, at + QW : at + HALF])
        part = slice(core * tall, (core + 1) * tall)
        my_d[...] = moment(md_ref[part, :], d_ref[part, :])

    pl.when(place.core == 0)(lambda: moments_of(0, mq_ref))
    pl.when(place.core == 1)(lambda: moments_of(1, mo_ref))

    tall_rows = pl.ds(pl.multiple_of(place.core * tall, 16), tall)
    wide_at, sq_at, nk_at = (by_core(p, place.core) for p in (WIDE_AT, SQUARE_AT, NARROW_AT))
    tall_core = 2 * place.x
    routes = (
        (my_gu, wide_s.at[place.f], wide_at, place.d),
        (my_d, tall_s.at[place.f, tall_rows], TALL_AT, tall_core),
        (my_sq, sq_s.at[place.f], sq_at, place.d),
        (my_nk, nk_s.at[place.f], nk_at, place.d),
    )

    def each_route(far, near):
        for i, (source, target, f, d) in enumerate(routes):
            here = (place.f == f) & (place.d == d)
            recv = in_recv.at[i, place.f] if i != 1 else in_recv.at[i, place.f + count * place.core]
            pl.when(jnp.logical_not(here))(
                lambda i=i, source=source, target=target, f=f, d=d, recv=recv: far(
                    remote(source, target, in_send.at[i], recv, (f, d))
                )
            )
            pl.when(here)(
                lambda i=i, source=source, target=target: near(
                    pltpu.make_async_copy(source, target, own_sem.at[i])
                )
            )

    each_route(lambda copy: copy.start(), lambda copy: copy.start())
    each_route(lambda copy: copy.wait_send(), lambda copy: copy.wait())

    def received(i, slot_of):
        for step in range(1, count):
            f = lax.rem(place.f + step, count)
            target = slot_of(f)
            remote(target, target, in_send.at[i], in_recv.at[i, f], place.sibling).wait_recv()

    def received_tall():
        for step in range(count):
            f = lax.rem(place.f + step, count)
            for core in range(2):
                if step == 0 and core == 0:
                    continue
                target = tall_s.at[f, pl.ds(core * tall, tall)]
                remote(target, target, in_send.at[1], in_recv.at[1, f + count * core], place.sibling).wait_recv()

    def scale_of():
        total = jnp.zeros((1, 1), F32)
        for at in range(0, FF, 256):
            part = x_s[:, at : at + 256]
            total = total + jnp.sum(jnp.sum(part * part, axis=0, keepdims=True), axis=1, keepdims=True)
            low_s[:, at : at + 256] = part.astype(BF16)
        return 1.0 / (jnp.sqrt(total) + 1e-07)

    is_wide, is_square, is_narrow = (place.f == at for at in (wide_at, sq_at, nk_at))
    is_tall = (place.f == TALL_AT) & (place.core == 0)
    is_small = is_square | is_narrow

    @pl.when(is_wide)
    def _():
        received(0, lambda f: wide_s.at[f])
        for f in range(count):
            x_s[f * rows : (f + 1) * rows, :] = wide_s[f].astype(F32)

    @pl.when(is_tall)
    def _():
        received_tall()
        for f in range(0, count, 2):
            pair = jnp.concatenate([tall_s[f], tall_s[f + 1]], axis=0).astype(F32)
            x_s[:, 2 * f * tall : 2 * (f + 2) * tall] = pair.T

    @pl.when(is_small)
    def _():
        x_s[...] = jnp.zeros_like(x_s)

    @pl.when(is_square)
    def _():
        received(2, lambda f: sq_s.at[f])
        for f in range(count):
            x_s[f * rows : (f + 1) * rows, :QW] = sq_s[f].astype(F32)

    @pl.when(is_narrow)
    def _():
        received(3, lambda f: nk_s.at[f])
        for f in range(count):
            x_s[f * rows : (f + 1) * rows, :NARROW] = nk_s[f].astype(F32)

    @pl.when(is_wide | is_tall | is_small)
    def _():
        newton_schulz(x_s, low_s, gram_s, gram_low_s, poly_s, scale_of())

    rate = MUON_RATE * math.sqrt(FF)
    small_rate = MUON_RATE * math.sqrt(D)

    def back(i, f, core):
        source = (
            wide_s.at[f], tall_s.at[f, pl.ds(core * tall, tall)] if i == 1 else None, sq_s.at[f], nk_s.at[f],
        )[i]
        return source, landing(i, core), (f, 2 * place.x + core)

    def landing(i, core):
        if i == 1:
            start = core * tall if isinstance(core, int) else pl.multiple_of(core * tall, 16)
            return d_out.at[pl.ds(start, tall)]
        return (gu_out, None, sq_out, nk_out)[i].at[core]

    def give(i, cores, act):
        for step in range(count):
            f = lax.rem(place.f + step, count)
            for n, core in enumerate(cores):
                source, target, device = back(i, f, core)
                if step == 0 and n == 0:
                    copy = pltpu.make_async_copy(source, target, own_sem.at[i])
                    act(copy, True)
                else:
                    slot = f + count * n
                    act(remote(source, target, out_send.at[i, slot], out_recv.at[i], device), False)

    def given(i, cores):
        give(i, cores, lambda copy, own: copy.start())
        give(i, cores, lambda copy, own: copy.wait() if own else copy.wait_send())

    @pl.when(is_wide)
    def _():
        for f in range(count):
            wide_s[f] = (x_s[f * rows : (f + 1) * rows, :] * rate).astype(BF16)
        given(0, (place.core,))

    @pl.when(is_tall)
    def _():
        for f in range(0, count, 2):
            pair = (x_s[:, 2 * f * tall : 2 * (f + 2) * tall] * rate).T
            tall_s[f] = pair[: 2 * tall].astype(BF16)
            tall_s[f + 1] = pair[2 * tall :].astype(BF16)
        given(1, (0, 1))

    @pl.when(is_square)
    def _():
        for f in range(count):
            sq_s[f] = (x_s[f * rows : (f + 1) * rows, :QW] * small_rate).astype(BF16)
        given(2, (place.core,))

    @pl.when(is_narrow)
    def _():
        for f in range(count):
            nk_s[f] = (x_s[f * rows : (f + 1) * rows, :NARROW] * small_rate).astype(BF16)
        given(3, (place.core,))

    makers = (is_wide, is_tall, is_square, is_narrow)

    def hand_over(i, core):
        target = landing(i, core)
        return remote(target, target, pair_send.at[i], pair_recv.at[i], place.sibling)

    for i in (2, 3, 1, 0):
        target = landing(i, place.core)

        def take(i=i, target=target):
            remote(target, target, pair_send.at[i], out_recv.at[i], place.sibling).wait_recv()

        pl.when(jnp.logical_not(makers[i]))(take)
        hand_over(i, place.core).start()
    for i in range(4):
        hand_over(i, 1 - place.core).wait_recv()
        hand_over(i, place.core).wait_send()


def muon_scratch(count, rows, tall):
    pieces = ((rows, FF), (rows, QW), (rows, NARROW), (tall, D))
    dma = pltpu.SemaphoreType.DMA
    return (
        [pltpu.VMEM(p, BF16) for p in pieces]
        + [pltpu.VMEM((count,) + p, BF16) for p in pieces[:3]]
        + [
            pltpu.VMEM((count, 2 * tall, D), BF16), pltpu.VMEM((D, FF), F32), pltpu.VMEM((D, FF), BF16),
            pltpu.VMEM((D, D), F32), pltpu.VMEM((D, D), BF16), pltpu.VMEM((D, D), BF16),
            dma((4,)), dma((4, 2 * count)), dma((4,)), dma((4, 2 * count)), dma((4,)), dma((4,)), dma((4,)),
        ]
    )


def outputs_kernel(gain_rate, a_ref, gu_ref, d_ref, sq_ref, nk_ref, ugu_ref, ud_ref, gains_ref, gainm_ref, *refs):
    given, (gg_ref, gm_ref, gv_ref), results = refs[:10], refs[10:13], refs[13:28]
    held, made, (load_sem, store_sem) = refs[28:38], refs[38:53], refs[53:]
    loads = [pltpu.make_async_copy(given[i], held[i], load_sem.at[i]) for i in range(10)]
    stores = [pltpu.make_async_copy(made[i], results[i], store_sem.at[i]) for i in range(15)]
    order = (3, 4, 0, 2, 1)
    for i in order:
        loads[5 + i].start()
        loads[i].start()
    gain = jnp.concatenate(
        [a_ref[:, at : at + 128].astype(F32).T[0:1, :] for at in (HALF, O_AT + HALF)], axis=0
    )
    moments = GAIN_DECAY * gainm_ref[...] + gain
    gg_ref[...] = gain
    gm_ref[...] = moments
    gv_ref[...] = gains_ref[...] - gain_rate * moments

    def write(i, grad, update, index=(slice(None), slice(None))):
        grad = grad.astype(F32)
        made[3 * i][index] = grad
        made[3 * i + 1][index] = MOMENTUM_DECAY * held[5 + i][index] + grad
        made[3 * i + 2][index] = held[i][index] - update.astype(F32)

    for i in order:
        loads[5 + i].wait()
        loads[i].wait()
        for side in range(2) if i in (1, 3) else ():
            index = (slice(None), side, slice(None))
            at = side * O_AT + QW
            if i == 1:
                write(1, a_ref[:, at : at + KVW], nk_ref[side, :, :KVW], index)
            else:
                write(3, gu_ref[:, side * FF : side * FF + FF], ugu_ref[side], index)
        if i == 0:
            write(0, a_ref[:, :QW], sq_ref[0])
        elif i == 2:
            write(2, a_ref[:, O_AT : O_AT + QW], sq_ref[1])
        elif i == 4:
            write(4, d_ref[...], ud_ref[...])
        for j in range(3):
            stores[3 * i + j].start()
    for copy in stores:
        copy.wait()


def write_outputs(gain_rate, grads, updates, gains, gain_momentum, weights, momenta):
    outs = [jax.ShapeDtypeStruct(w.shape, F32) for w in weights for _ in range(3)]
    anywhere = pl.BlockSpec(memory_space=pl.ANY)
    return pl.pallas_call(
        partial(outputs_kernel, gain_rate),
        out_shape=(jax.ShapeDtypeStruct(gains.shape, F32),) * 3 + tuple(outs),
        in_specs=vmem(9) + [anywhere] * 10,
        out_specs=tuple(vmem(3)) + (anywhere,) * 15,
        scratch_shapes=[pltpu.VMEM(w.shape, F32) for w in weights + momenta]
        + [pltpu.VMEM(o.shape, F32) for o in outs]
        + [pltpu.SemaphoreType.DMA((10,)), pltpu.SemaphoreType.DMA((15,))],
        compiler_params=pltpu.CompilerParams(vmem_limit_bytes=VMEM_LIMIT),
        name="outputs",
    )(*grads, *updates, gains, gain_momentum, *weights, *momenta)


class Place:
    def __init__(self, lines):
        self.f, self.d = lax.axis_index("fsdp"), lax.axis_index("dp")
        self.line, self.column = self.f // 2, self.f % 2
        self.x, self.core = self.d // 2, self.d % 2
        self.lines = lines
        self.sibling = (self.f, self.d + 1 - 2 * self.core)
        self.across = (self.f, self.core + 2 * (1 - self.x))
        self.beside = (self.f + 1 - 2 * self.column, self.d)
        self.above = (self.f + 2, self.d)
        self.below = (self.f - 2, self.d)


def remote(source, target, send_sem, recv_sem, device):
    return pltpu.make_async_remote_copy(
        src_ref=source, dst_ref=target, send_sem=send_sem, recv_sem=recv_sem,
        device_id=device, device_id_type=pl.DeviceIdType.MESH,
    )


def greet(place, between, plane=False):
    barrier = pltpu.get_barrier_semaphore()

    def signal(device):
        pl.semaphore_signal(barrier, inc=1, device_id=device, device_id_type=pl.DeviceIdType.MESH)

    signal(place.sibling)
    signal(place.across)
    if plane:
        count = 2 * place.lines
        for step in range(1, count):
            f = lax.rem(place.f + step, count)
            for core in range(2):
                signal((f, 2 * place.x + core))
        between()
        pl.semaphore_wait(barrier, 2 * count)
        return
    signal(place.beside)
    pl.when(place.line > 0)(lambda: signal(place.below))
    pl.when(place.line < place.lines - 1)(lambda: signal(place.above))
    between()
    ends = (place.line == 0).astype(jnp.int32) + (place.line == place.lines - 1).astype(jnp.int32)
    pl.semaphore_wait(barrier, 5 - ends)


PARTS = 4


def half_parts(packed, gateup, down, core):
    tall = down.shape[0] // 2
    at = core * FF
    return (
        None if packed is None else packed.at[:, pl.ds(pl.multiple_of(core * O_AT, 128), O_AT)],
        gateup.at[:, pl.ds(pl.multiple_of(at, 128), FF // 2)],
        gateup.at[:, pl.ds(pl.multiple_of(at + FF // 2, 128), FF // 2)],
        down.at[pl.ds(pl.multiple_of(core * tall, 16), tall), :],
    )


def start_kernel(
    lines, lengths, assignment, xt_ref, cott_ref, gains_ref, wq_ref, wkv_ref, wo_ref, wgu_ref, wd_ref,
    inner_ref, outer_ref,
    meta, x_ref, cot_ref, q_ref, wa_ref, kv_out, gu_out, d_out,
    a_s, gu_s, d_s, a_out, kv_s,
    own_sem, in_sem, pair_sem, up_sem, down_sem, side_sem, cross_sem, mate_sem,
    kv_in, kv_pair, kv_cross, kv_mate,
):
    place = Place(lines)
    shard_rows = a_s.shape[0]
    own = [
        pltpu.make_async_copy(source, target.at[place.f], own_sem.at[i])
        for i, (source, target) in enumerate(((a_s, a_out), (gu_s, gu_out), (d_s, d_out)))
    ]

    def pack_first():
        gains = jnp.broadcast_to(gains_ref[...][:, None, :], (2, 128, shard_rows))
        for side, w_ref in enumerate((wq_ref, wo_ref)):
            at = side * O_AT
            a_s[:, at : at + QW] = w_ref[...].astype(BF16)
            a_s[:, at + QW : at + HALF] = wkv_ref[:, side, :].astype(BF16)
            a_s[:, at + HALF : at + O_AT] = gains[side].T.astype(BF16)
        for side in range(2):
            gu_s[:, side * FF : side * FF + FF] = wgu_ref[:, side, :].astype(BF16)
        d_s[...] = wd_ref[...].astype(BF16)

    greet(place, pack_first)

    def full(shard, core):
        return half_parts(a_out.at[shard], gu_out.at[shard], d_out.at[shard], core)

    mine = half_parts(a_s, gu_s, d_s, place.core)

    def send(shard, k, sems, device, recv, source=None):
        target = full(shard, place.core)[k]
        return remote(target if source is None else source, target, sems.at[shard, k], recv.at[shard, k], device)

    def to_pair(shard, k):
        return send(shard, k, mate_sem, place.sibling, pair_sem)

    def if_sideways(k, run):
        if START_SPLIT[k]:
            pl.when(place.x == k % 2)(run)
        else:
            run()

    def on_z(t, k, action):
        for sign in (-1, 1) if t else (0,):
            shard = place.f + 2 * sign * t
            there = place.line + sign * t

            def go(shard=shard, sign=sign):
                source = None if sign else mine[k]
                if sign:
                    action(None, shard)
                if sign <= 0:
                    pl.when(place.line < lines - 1)(
                        lambda: action(send(shard, k, up_sem, place.above, in_sem, source))
                    )
                if sign >= 0:
                    pl.when(place.line > 0)(
                        lambda: action(send(shard, k, down_sem, place.below, in_sem, source))
                    )
                if_sideways(k, lambda: action(send(shard, k, side_sem, place.beside, in_sem, source)))
                if sign:
                    action(to_pair(shard, k))

            if sign:
                pl.when((there >= 0) & (there < lines))(go)
            else:
                go()

    def at_distance(base, t, run):
        if t == 0:
            run(base)
            return
        for sign in (-1, 1):
            there = place.line + sign * t
            pl.when((there >= 0) & (there < lines))(lambda sign=sign: run(base + 2 * sign * t))

    def on_side(t, k, action):
        def run(shard):
            action(None, shard)
            if START_SPLIT[k]:
                action(send(shard, k, cross_sem, place.across, in_sem))
            action(to_pair(shard, k))

        if_sideways(k, lambda: at_distance(place.beside[0], t, run))

    def on_cross(t, k, action):
        def run(shard):
            action(None, shard)
            action(to_pair(shard, k))

        if START_SPLIT[k]:
            pl.when(place.x != k % 2)(lambda: at_distance(place.beside[0], t, run))

    def start(k):
        def action(copy, shard=None):
            if copy is None:
                send(shard, k, up_sem, place.sibling, in_sem).wait_recv()
            else:
                copy.start()

        return action

    def finish_send(copy, shard=None):
        if copy is not None:
            copy.wait_send()

    def from_pair(k):
        def got(shard):
            target = full(shard, 1 - place.core)[k]
            remote(target, target, mate_sem.at[shard, k], pair_sem.at[shard, k], place.sibling).wait_recv()

        for t in range(lines):
            at_distance(place.beside[0], t, got)
            if t > 0:
                at_distance(place.f, t, got)

    def kv_rows(i):
        return pl.ds(i * STEP, STEP)

    def kv_send(i, device, sems, recv):
        return remote(kv_s.at[kv_rows(i)], kv_out.at[place.d, kv_rows(i)], sems.at[i], recv.at[i], device)

    def kv_pass(i):
        here = kv_out.at[place.across[1], kv_rows(i)]
        return remote(here, here, kv_mate.at[1, i], kv_pair.at[1, i], place.sibling)

    steps = x_ref.shape[0] // STEP
    slots = x_ref.shape[0] // BLK
    own_kv = pltpu.make_async_copy(kv_s, kv_out.at[place.d], own_sem.at[3])

    def prepare():
        for copy in own:
            copy.start()
        block_meta(lengths, assignment, place.d * slots, slots, meta)
        for i in range(steps):
            rows = slice(i * STEP, (i + 1) * STEP)
            x_ref[rows, :] = xt_ref[:, rows].T
            cot_ref[rows, :] = cott_ref[:, rows].T

    def unpack():
        own[0].wait()
        from_pair(0)
        for f in range(0, 2 * lines, 2):
            wa_ref[f * shard_rows : (f + 2) * shard_rows, :] = jnp.concatenate([a_out[f], a_out[f + 1]], axis=0)

    def project(i):
        gain = gain_row(wa_ref, HALF)
        project_rows(meta, i, x_ref, wa_ref, gain, inner_ref, outer_ref, q_ref, kv_s)
        kv_send(i, place.across, kv_cross, kv_in).start()
        kv_send(i, place.sibling, kv_mate.at[0], kv_pair.at[0]).start()

    def hand_on(i):
        kv_send(i, place.across, kv_cross, kv_in).wait_recv()
        kv_pass(i).start()

    for event, *which in START_ORDER:
        if event == "z":
            on_z(*which, start(which[1]))
        elif event == "side":
            on_side(*which, start(which[1]))
        elif event == "cross":
            on_cross(*which, start(which[1]))
        else:
            {"prep": prepare, "wa": unpack, "proj": project, "kvpass": hand_on}[event](*which)
    own_kv.start()
    for k in range(PARTS):
        if k > 0:
            from_pair(k)
        for t in range(lines):
            on_z(t, k, finish_send)
            on_side(t, k, finish_send)
            on_cross(t, k, finish_send)
    for i in range(steps):
        kv_send(i, place.sibling, kv_mate.at[0], kv_pair.at[0]).wait()
        kv_send(i, place.across, kv_cross, kv_in).wait_send()
        kv_pass(i).wait()
    for copy in own[1:] + [own_kv]:
        copy.wait()


def start_remote(lengths, assignment, tokens, cotangent, gains, weights, inner, outer, count):
    rows = tokens.shape[0]
    shard_rows, tall, steps = weights[0].shape[0], weights[4].shape[0], rows // STEP
    smem, anywhere = pl.BlockSpec(memory_space=pltpu.SMEM), pl.BlockSpec(memory_space=pl.ANY)
    shapes = ((shard_rows, WIDE_A), (shard_rows, 2 * FF), (tall, D))
    sems = pltpu.SemaphoreType.DMA((count, PARTS))
    meta, x, cot, queries, packed, keyval, gateup, down = pl.pallas_call(
        partial(start_kernel, count // 2),
        out_shape=(
            jax.ShapeDtypeStruct((rows // BLK, META), jnp.int32),
            jax.ShapeDtypeStruct((rows, D), BF16),
            jax.ShapeDtypeStruct((rows, D), BF16),
            jax.ShapeDtypeStruct((rows, 128 * HEADS), BF16),
            jax.ShapeDtypeStruct((D, WIDE_A), BF16),
            jax.ShapeDtypeStruct((4, rows, 2 * KVW), BF16),
            jax.ShapeDtypeStruct((count,) + shapes[1], BF16),
            jax.ShapeDtypeStruct((count,) + shapes[2], BF16),
        ),
        in_specs=[smem] * 2 + vmem(10),
        out_specs=(smem,) + tuple(vmem(4)) + (anywhere,) * 3,
        scratch_shapes=[pltpu.VMEM(s, BF16) for s in shapes]
        + [pltpu.VMEM((count,) + shapes[0], BF16), pltpu.VMEM((rows, 2 * KVW), BF16)]
        + [pltpu.SemaphoreType.DMA((4,))]
        + [sems] * 7
        + [
            pltpu.SemaphoreType.DMA((steps,)),
            pltpu.SemaphoreType.DMA((2, steps)),
            pltpu.SemaphoreType.DMA((steps,)),
            pltpu.SemaphoreType.DMA((2, steps)),
        ],
        compiler_params=pltpu.CompilerParams(
            collective_id=0, has_side_effects=True, vmem_limit_bytes=VMEM_LIMIT
        ),
        name="gather_and_project",
    )(lengths, assignment, tokens.T, cotangent.T, gains.T, *weights, inner, outer)
    return (
        meta, x, cot, queries, packed, keyval.reshape(4 * rows, 2 * KVW),
        gateup.reshape(D, 2 * FF), down.reshape(FF, D),
    )


def start_kernel_plain(
    lengths, assignment, x_ref, wa_ref, inner_ref, outer_ref, meta, q_ref, kv_ref
):
    slots = x_ref.shape[0] // BLK
    block_meta(lengths, assignment, lax.axis_index("dp") * slots, slots, meta)
    gain = gain_row(wa_ref, HALF)
    for i in range(x_ref.shape[0] // STEP):
        project_rows(meta, i, x_ref, wa_ref, gain, inner_ref, outer_ref, q_ref, kv_ref)


def start_xla(lengths, assignment, tokens, cotangent, gains, weights, inner, outer):
    packed, gateup, down = (gather_rows_xla(s) for s in pack(*weights, gains))
    rows = tokens.shape[0]
    smem = pl.BlockSpec(memory_space=pltpu.SMEM)
    meta, queries, keyval = pl.pallas_call(
        start_kernel_plain,
        out_shape=(
            jax.ShapeDtypeStruct((rows // BLK, META), jnp.int32),
            jax.ShapeDtypeStruct((rows, 128 * HEADS), BF16),
            jax.ShapeDtypeStruct((rows, 2 * KVW), BF16),
        ),
        in_specs=[smem] * 2 + vmem(4),
        out_specs=(smem,) + tuple(vmem(2)),
        compiler_params=pltpu.CompilerParams(vmem_limit_bytes=VMEM_LIMIT),
        name="project",
    )(lengths, assignment, tokens, packed, inner, outer)
    keyval = lax.all_gather(keyval, "dp", axis=0, tiled=True)
    return meta, tokens, cotangent, queries, packed, keyval, gateup, down


def visit_order(lines):
    return [sorted(range(lines), key=lambda other: (-abs(other - line), -other)) for line in range(lines)]


def reduce_kernel(
    lines, meta, x_ref, wa_ref, gq_ref, dkv_ref, gres_ref, gb_ref, lowt_ref, gain_ref, inner_ref, outer_ref,
    mq_ref, mkv_ref, mo_ref, mgu_ref, md_ref, gu_hbm, d_hbm,
    int_ref, a_out, gu_out, d_out, sq_out, nk_out, ugu_out, ud_out,
    normed_s, first_s, values_s, kv_s, kv_pair_s, kv_far_s, kv_cross_s,
    da_s, gu_s, d_s, a_pair, gu_pair, d_pair, a_in, gu_in, d_in,
    load_sem, kv_pair, kv_cross, kv_pair_send, kv_cross_send,
    pair_recv, recv, last_recv, pair_send, send, last_send, *muon_s
):
    place = Place(lines)
    half = FF // 2
    steps = x_ref.shape[0] // STEP
    order_table = visit_order(lines)

    def own_load(shard, k):
        source = half_parts(None, gu_hbm.at[shard], d_hbm.at[shard], place.core)[k]
        return pltpu.make_async_copy(source, pieces(shard)[k], load_sem.at[shard, k - 1])

    def pieces(shard):
        at = pl.multiple_of(place.core * O_AT, 128)
        return (
            da_s.at[shard, :, pl.ds(at, O_AT)], gu_s.at[shard, :, pl.ds(0, half)],
            gu_s.at[shard, :, pl.ds(half, half)], d_s.at[shard],
        )

    def mate(shard):
        return (
            a_pair.at[shard], gu_pair.at[shard, :, pl.ds(0, half)], gu_pair.at[shard, :, pl.ds(half, half)],
            d_pair.at[shard],
        )

    def inbox(way, spot):
        return (
            a_in.at[way, spot], gu_in.at[way, spot, :, pl.ds(0, half)],
            gu_in.at[way, spot, :, pl.ds(half, half)], d_in.at[way, spot],
        )

    def order(t):
        spot = jnp.int32(0)
        for line in range(lines):
            spot = spot + order_table[line][t] * (place.line == line).astype(jnp.int32)
        return spot

    def to_pair(shard, k):
        there = 1 - place.core
        if k == 0:
            source = da_s.at[shard, :, pl.ds(pl.multiple_of(there * O_AT, 128), O_AT)]
        else:
            source = half_parts(None, gu_hbm.at[shard], d_hbm.at[shard], there)[k]
        return remote(source, mate(shard)[k], pair_send.at[shard, k], pair_recv.at[shard, k], place.sibling)

    def pass_on(shard, k, way, spot, device):
        return remote(
            mate(shard)[k], inbox(way, spot)[k], send.at[way, spot, k], recv.at[way, spot, k], device
        )

    def arrived(k, way, spot):
        target = inbox(way, spot)[k]
        remote(target, target, send.at[way, spot, k], recv.at[way, spot, k], place.sibling).wait_recv()

    def local_ready(shard, k):
        to_pair(shard, k).wait_recv()
        if k > 0:
            own_load(shard, k).wait()

    def total(shard, k, spot, ways):
        value = pieces(shard)[k][...].astype(F32) + mate(shard)[k][...].astype(F32)
        for way in ways:
            value = value + inbox(way, spot)[k][...].astype(F32)
        mate(shard)[k][...] = value.astype(BF16)

    def on_plane(k, run, other=None):
        if not REDUCE_SPLIT[k]:
            run(False)
            return
        pl.when(place.x == k % 2)(lambda: run(True))
        if other is not None:
            pl.when(place.x != k % 2)(other)

    def stage_pair(t, k):
        spot = order(t)
        shard = 2 * spot + 1 - place.column
        local_ready(shard, k)

        def away():
            total(shard, k, spot, ())
            pass_on(shard, k, 0, spot, place.across).start()

        if REDUCE_SPLIT[k]:
            pl.when(place.x != k % 2)(away)
        else:
            total(shard, k, spot, ())
            pass_on(shard, k, 1, spot, place.beside).start()

    def stage_side(t, k):
        spot = order(t)
        shard = 2 * spot + 1 - place.column

        def go():
            arrived(k, 0, spot)
            total(shard, k, spot, (0,))
            pass_on(shard, k, 1, spot, place.beside).start()

        if REDUCE_SPLIT[k]:
            pl.when(place.x == k % 2)(go)

    def stage_line(t, k):
        spot = order(t)
        shard = 2 * spot + place.column
        local_ready(shard, k)
        if REDUCE_SPLIT[k]:
            pl.when(place.x == k % 2)(lambda: arrived(k, 1, spot))
        else:
            arrived(k, 1, spot)

        def summed(ways):
            for way in ways:
                arrived(k, way, spot)
            if REDUCE_SPLIT[k]:
                pl.when(place.x == k % 2)(lambda: total(shard, k, spot, (1,) + ways))
                pl.when(place.x != k % 2)(lambda: total(shard, k, spot, ways))
            else:
                total(shard, k, spot, (1,) + ways)

        below, above = place.line > 0, place.line < lines - 1

        if t < lines - 1:

            @pl.when(spot > place.line)
            def _():
                pl.when(below)(lambda: summed((2,)))
                pl.when(jnp.logical_not(below))(lambda: summed(()))
                pass_on(shard, k, 2, spot, place.above).start()

            @pl.when(spot < place.line)
            def _():
                pl.when(above)(lambda: summed((3,)))
                pl.when(jnp.logical_not(above))(lambda: summed(()))
                pass_on(shard, k, 3, spot, place.below).start()

        else:
            pl.when(below & above)(lambda: summed((2, 3)))
            pl.when(jnp.logical_not(below))(lambda: summed((3,)))
            pl.when(jnp.logical_not(above))(lambda: summed((2,)))
            last(k).start()

    def last(k):
        return remote(
            mate(place.f)[k], inbox(4, 0)[k], last_send.at[0, k], last_recv.at[0, k], place.across
        )

    def share(k, core):
        target = half_parts(a_out, gu_out, d_out, core)[k]
        return remote(target, target, last_send.at[1, k], last_recv.at[1, k], place.sibling)

    def stage_last(k):
        last(k).wait_recv()
        target = half_parts(a_out, gu_out, d_out, place.core)[k]
        target[...] = added(mate(place.f)[k][...], inbox(4, 0)[k][...]).astype(BF16)
        share(k, place.core).start()

    def every(act, ks):
        for t in range(lines):
            for column in (1 - place.column, place.column):
                for k in ks:
                    act(2 * order(t) + column, k)

    early = (1, 2, 3)
    targets = ((1 - place.core) + 2 * (1 - place.x), (1 - place.core) + 2 * place.x)

    def kv_rows(i):
        return pl.ds(i * STEP, STEP)

    def kv_to_pair(w, i):
        return remote(
            dkv_ref.at[targets[w], kv_rows(i)], kv_pair_s.at[w, kv_rows(i)], kv_pair_send.at[w, i],
            kv_pair.at[w, i], place.sibling,
        )

    def kv_across(i):
        return remote(
            kv_far_s.at[kv_rows(i)], kv_cross_s.at[kv_rows(i)], kv_cross_send.at[i], kv_cross.at[i], place.across
        )

    greet(place, lambda: every(lambda shard, k: own_load(shard, k).start(), (3, 1, 2)), True)
    gain = gain_row(wa_ref, HALF)
    gains = [jnp.zeros((1, D), F32)]

    def send_pair(t, side):
        shard = 2 * order(t) + (place.column if side else 1 - place.column)
        for k in (3, 1, 2):
            to_pair(shard, k).start()

    def send_kv(w):
        for i in range(steps):
            kv_to_pair(w, i).start()

    def cross_kv():
        for i in range(steps):
            kv_to_pair(0, i).wait_recv()
            kv_far_s[kv_rows(i)] = added(dkv_ref[place.across[1], kv_rows(i)], kv_pair_s[0, kv_rows(i)]).astype(BF16)
            kv_across(i).start()

    def finish_rows(i):
        kv_to_pair(1, i).wait_recv()
        kv_across(i).wait_recv()
        mine = added(dkv_ref[place.d, kv_rows(i)], kv_pair_s[1, kv_rows(i)])
        kv_s[kv_rows(i)] = (mine + kv_cross_s[kv_rows(i)].astype(F32)).astype(BF16)
        gains[0] = gains[0] + input_grad_rows(
            meta, i, x_ref, wa_ref, gain, gq_ref, kv_s, gres_ref, inner_ref, outer_ref, int_ref,
            normed_s, first_s, values_s,
        )

    def attention_grads():
        packed_grads(da_s, normed_s, first_s, values_s, lowt_ref, gb_ref, gains[0], gain_ref)

    stages = {
        "pp": send_pair, "kvp": send_kv, "kvx": cross_kv, "fin": finish_rows,
        "da1": lambda: out_grads(da_s, lowt_ref, gb_ref), "da2": attention_grads,
        "pp0": lambda: every(lambda shard, k: to_pair(shard, k).start(), (0,)),
        "P": stage_pair, "S": stage_side, "Z": stage_line, "F": stage_last,
    }
    for event, *which in REDUCE_ORDER:
        stages[event](*which)
    muon_part(
        place, a_out, gu_out, d_out, mq_ref, mkv_ref, mo_ref, mgu_ref, md_ref,
        sq_out, nk_out, ugu_out, ud_out, *muon_s
    )
    for k in range(PARTS):
        share(k, 1 - place.core).wait_recv()
        share(k, place.core).wait_send()
        last(k).wait_send()
    every(lambda shard, k: to_pair(shard, k).wait_send(), range(PARTS))
    for i in range(steps):
        kv_to_pair(0, i).wait_send()
        kv_to_pair(1, i).wait_send()
        kv_across(i).wait_send()
    for t in range(lines):
        spot = order(t)
        for k in range(PARTS):
            other, own = 2 * spot + 1 - place.column, 2 * spot + place.column
            on_plane(
                k,
                lambda split: pass_on(other, k, 1, spot, place.beside).wait_send(),
                lambda: pass_on(other, k, 0, spot, place.across).wait_send(),
            )
            if t < lines - 1:
                pl.when(spot > place.line)(lambda: pass_on(own, k, 2, spot, place.above).wait_send())
                pl.when(spot < place.line)(lambda: pass_on(own, k, 3, spot, place.below).wait_send())


def added(one, two):
    return one.astype(F32) + two.astype(F32)


def reduce_remote(meta, x, packed, gq, dkv, gres, gb, lowt, gain, inner, outer, momenta, d_gateup, d_down, count):
    lines, rows = count // 2, x.shape[0]
    shard_rows, tall = D // count, FF // count
    steps, width = rows // STEP, dkv.shape[1]
    halves = ((shard_rows, O_AT), (shard_rows, FF), (tall // 2, D))
    anywhere = pl.BlockSpec(memory_space=pl.ANY)
    dma = pltpu.SemaphoreType.DMA
    outs = pl.pallas_call(
        partial(reduce_kernel, lines),
        out_shape=(
            jax.ShapeDtypeStruct((D, rows), F32),
            jax.ShapeDtypeStruct((shard_rows, WIDE_A), BF16),
            jax.ShapeDtypeStruct((shard_rows, 2 * FF), BF16),
            jax.ShapeDtypeStruct((tall, D), BF16),
            jax.ShapeDtypeStruct((2, shard_rows, QW), BF16),
            jax.ShapeDtypeStruct((2, shard_rows, NARROW), BF16),
            jax.ShapeDtypeStruct((2, shard_rows, FF), BF16),
            jax.ShapeDtypeStruct((tall, D), BF16),
        ),
        in_specs=[pl.BlockSpec(memory_space=pltpu.SMEM)] + vmem(15) + [anywhere] * 2,
        out_specs=tuple(vmem(8)),
        scratch_shapes=finish_scratch(rows)
        + [pltpu.VMEM((rows, width), BF16), pltpu.VMEM((2, rows, width), BF16)]
        + [pltpu.VMEM((rows, width), BF16)] * 2
        + [pltpu.VMEM((count, shard_rows, WIDE_A), BF16)]
        + [pltpu.VMEM((count,) + h, BF16) for h in halves[1:] + halves]
        + [pltpu.VMEM((5, lines) + h, BF16) for h in halves]
        + [
            dma((count, PARTS - 1)), dma((2, steps)), dma((steps,)), dma((2, steps)), dma((steps,)),
            dma((count, PARTS)), dma((4, lines, PARTS)), dma((2, PARTS)),
            dma((count, PARTS)), dma((4, lines, PARTS)), dma((2, PARTS)),
        ]
        + muon_scratch(count, shard_rows, tall // 2),
        compiler_params=pltpu.CompilerParams(
            collective_id=1, has_side_effects=True, vmem_limit_bytes=VMEM_LIMIT
        ),
        name="finish_and_reduce",
    )(
        meta, x, packed, gq, dkv.reshape(4, rows, width), gres, gb, lowt, gain, inner, outer,
        *momenta, d_gateup.reshape(count, shard_rows, 2 * FF), d_down.reshape(count, tall, D),
    )
    return outs[0], outs[1:4], outs[4:]


def own_kernels():
    return lax.axis_size("fsdp") == 8 and lax.axis_size("dp") == 4


def begin(*given):
    return start_remote(*given, lax.axis_size("fsdp")) if own_kernels() else start_xla(*given)


def reduce_and_update(meta, x, packed, gq, dkv, gres, gb, lowt, gain, inner, outer, momenta, d_gateup, d_down):
    if own_kernels():
        return reduce_remote(
            meta, x, packed, gq, dkv, gres, gb, lowt, gain, inner, outer, momenta, d_gateup, d_down,
            lax.axis_size("fsdp"),
        )
    dkv = lax.psum_scatter(dkv, "dp", scatter_dimension=0, tiled=True)
    input_grad, d_packed = finish(meta, x, packed, gq, dkv, gres, gb, lowt, gain, inner, outer)
    grads = tuple(reduce_rows_xla(g) for g in (d_packed, d_gateup, d_down))
    return input_grad, grads, muon_updates(grads, momenta)


def muon_updates(grads, momenta):
    packed, gateup, down = (g.astype(F32) for g in grads)
    m_query, m_keyval, m_out, m_gateup, m_down = momenta

    def moment(momentum, grad):
        return MOMENTUM_DECAY * momentum + grad

    steps = muon_exchange(
        [
            moment(m_query, packed[:, :QW]),
            moment(m_keyval[:, 0], packed[:, QW:HALF]),
            moment(m_keyval[:, 1], packed[:, O_AT + QW : O_AT + HALF]),
            moment(m_out, packed[:, O_AT : O_AT + QW]),
            moment(m_gateup[:, 0], gateup[:, :FF]),
            moment(m_gateup[:, 1], gateup[:, FF:]),
            moment(m_down, down),
        ]
    )
    return (
        jnp.stack([steps[0], steps[3]]).astype(BF16),
        jnp.pad(jnp.stack(steps[1:3]), ((0, 0), (0, 0), (0, NARROW - KVW))).astype(BF16),
        jnp.stack(steps[4:6]).astype(BF16),
        steps[6].astype(BF16),
    )


def local(
    tokens, cotangent, lengths, assignment, norm_gains, gain_momentum, w_query, w_keyval, w_out,
    w_gateup, w_down, m_query, m_keyval, m_out, m_gateup, m_down,
):
    gain_rate = GAIN_SCALE / math.sqrt(assignment.shape[1] * BLK * 3 // 4 * lax.axis_size("fsdp"))
    inner, outer, turned, steps = rope_constants()
    weights = (w_query, w_keyval, w_out, w_gateup, w_down)
    momenta = (m_query, m_keyval, m_out, m_gateup, m_down)
    meta, x, cot, queries, packed, group_kv, gateup, down = begin(
        lengths, assignment, tokens, cotangent, norm_gains, weights, inner, outer
    )
    gq, dkv, gain, lowt, act, gres, gb, d_gateup, d_down = layer(
        meta, x, cot, queries, group_kv, packed, gateup, down, turned, steps
    )
    input_grad, grads, updates = reduce_and_update(
        meta, x, packed, gq, dkv, gres, gb, lowt, gain, inner, outer, momenta, d_gateup, d_down
    )
    outs = write_outputs(gain_rate, grads, updates, norm_gains.T, gain_momentum.T, weights, momenta)
    return (act.T, input_grad.T) + tuple(g.T for g in outs[:3]) + tuple(outs[3:])


def solution(mesh):
    rows = P(("fsdp", "dp"), None)
    two, three = P("fsdp", None), P("fsdp", None, None)
    return jax.shard_map(
        local,
        mesh=mesh,
        in_specs=(rows, rows, two, two, two, two, two, three, two, three, two, two, three, two, three, two),
        out_specs=(rows, rows) + (two,) * 6 + (three,) * 3 + (two,) * 3 + (three,) * 3 + (two,) * 3,
        check_vma=False,
    )
```

```python
from functools import partial
import math

import jax
import jax.numpy as jnp
import numpy as np
from jax import lax
from jax.experimental import pallas as pl
from jax.experimental.pallas import tpu as pltpu
from jax.sharding import PartitionSpec as P

D = 576
HEADS = 9
KVH = 3
HD = 64
FF = 1536
BLK = 128
SEQS_G = 3
NS_STEPS = 5
QW = 576
KVW = 192
LONGEST = 12

EPS = 1e-05
THETA = 100000.0
MOMENTUM_DECAY = 0.95
GAIN_DECAY = 0.9
MUON_RATE = 0.03
GAIN_SCALE = 0.4
COEF_A = 3.4445
COEF_B = -4.775
COEF_C = 2.0315
SCALE = 1.0 / math.sqrt(HD)
HALF = 768
WIDE_A = 2 * (HALF + 128)
O_AT = HALF + 128
STEP = 256
F32, BF16 = jnp.float32, jnp.bfloat16


def vmem(count=1):
    return [pl.BlockSpec(memory_space=pltpu.VMEM)] * count


def dot(a, b):
    return lax.dot_general(a, b, (((1,), (0,)), ((), ())), preferred_element_type=F32)


def dot_nt(a, b):
    return lax.dot_general(a, b, (((1,), (1,)), ((), ())), preferred_element_type=F32)


def dot_tn(a, b):
    return lax.dot_general(a, b, (((0,), (0,)), ((), ())), preferred_element_type=F32)


META = 4 + LONGEST


def block_meta(lengths, assignment, first_slot, slots, meta):
    entries = assignment.shape[1]
    starts, sizes = [jnp.int32(0)], []
    for k in range(SEQS_G):
        sizes.append((lengths[0, k] + (BLK - 1)) // BLK)
        starts.append(starts[-1] + sizes[-1])

    @pl.loop(0, slots)
    def _(slot):
        mine = first_slot + slot

        def look(e, found):
            return jnp.where(assignment[0, e] == mine, e, found)

        entry = lax.fori_loop(0, entries, look, jnp.int32(0))
        first, size = entry, jnp.int32(0)
        for k in range(SEQS_G):
            inside = (entry >= starts[k]) & (entry < starts[k + 1])
            first = jnp.where(inside, starts[k], first)
            size = jnp.where(inside, lengths[0, k], size)
        place = entry - first
        meta[slot, 0] = place
        meta[slot, 1] = jnp.clip(size - place * BLK, 0, BLK)
        meta[slot, 2] = place // 2 + 1
        meta[slot, 3] = entry
        for step in range(LONGEST):
            key = assignment[0, jnp.minimum(first + step, entry)]
            meta[slot, 4 + step] = key


def rope_constants():
    freq = np.exp(np.arange(HD // 2, dtype=np.float64) * (-2.0 * math.log(THETA) / HD))
    lanes = np.tile(freq, 4)
    inner = np.arange(BLK)[:, None] * lanes[None, :]
    outer = BLK * np.arange(16)[:, None] * lanes[None, :]
    turned = inner.T[: HD // 2]
    steps = np.broadcast_to((BLK * np.arange(LONGEST))[:, None, None] * freq[None, :, None], (LONGEST, HD // 2, BLK))
    return tuple(
        np.stack([np.cos(angle), np.sin(angle)]).astype(np.float32)
        for angle in (inner, outer, turned, steps)
    )


def lane_index(rows):
    return lax.broadcasted_iota(jnp.int32, (rows, 128), 1)


def rope_tables(meta, slot, inner_ref, outer_ref):
    place, live = meta[slot, 0], meta[slot, 1]
    co, so = outer_ref[0, pl.ds(place, 1), :], outer_ref[1, pl.ds(place, 1), :]
    ci, si = inner_ref[0], inner_ref[1]
    lane = lane_index(BLK)
    row = lax.broadcasted_iota(jnp.int32, (BLK, 128), 0)
    turned = (row < live) & (lane < HD)
    cosine = jnp.where(turned, co * ci - so * si, 1.0)
    sine = jnp.where(turned, so * ci + co * si, 0.0)
    return cosine, jnp.where(lane < HD // 2, sine, 0.0), jnp.where(lane < HD // 2, 0.0, sine)


def rope(tile, tables):
    cosine, sine_low, sine_high = tables
    return (
        tile * cosine - pltpu.roll(tile, 128 - HD // 2, 1) * sine_low
        + pltpu.roll(tile, HD // 2, 1) * sine_high
    )


def turned_tables(meta, slot, turned_ref, steps_ref):
    place = meta[slot, 0]
    co, so, ci, si = steps_ref[0, place], steps_ref[1, place], turned_ref[0], turned_ref[1]
    turned = lax.broadcasted_iota(jnp.int32, (HD // 2, BLK), 1) < meta[slot, 1]
    return jnp.where(turned, co * ci - so * si, 1.0), jnp.where(turned, so * ci + co * si, 0.0)


def turned_rope_back(tile, cosine, sine):
    one, two = tile[: HD // 2], tile[HD // 2 : HD]
    return [one * cosine + two * sine, two * cosine - one * sine]


def swap(tile):
    return pltpu.roll(tile, HD, 1)


def gain_row(packed_ref, at):
    return packed_ref[:, at : at + 128].astype(F32).T[0:1, :]


def project_rows(meta, i, x_ref, wa_ref, gain, inner_ref, outer_ref, q_ref, kv_ref):
    low_lane = lane_index(BLK) < HD
    x = x_ref[i * STEP : (i + 1) * STEP, :].astype(F32)
    inv = lax.rsqrt(jnp.mean(x * x, axis=1, keepdims=True) + EPS)
    normed = (x * inv * gain).astype(BF16)
    qk = dot(normed, wa_ref[:, :HALF])
    ov = dot(normed, wa_ref[:, O_AT + 512 : O_AT + HALF])
    for b in range(STEP // BLK):
        tables = rope_tables(meta, i * (STEP // BLK) + b, inner_ref, outer_ref)
        rows = slice(i * STEP + b * BLK, i * STEP + (b + 1) * BLK)
        part = slice(b * BLK, (b + 1) * BLK)
        tiles = [qk[part, 128 * t : 128 * t + 128] for t in range(6)]
        for head in range(HEADS):
            tile = tiles[head // 2]
            tile = jnp.where(low_lane, swap(tile) if head % 2 else tile, 0.0)
            q_ref[rows, 128 * head : 128 * head + 128] = (rope(tile, tables) * SCALE).astype(BF16)
        values = [ov[part, :128], ov[part, 128:]]
        pairs = (
            (swap(tiles[4]), values[0]),
            (tiles[5], swap(values[1])),
            (swap(tiles[5]), values[1]),
        )
        for h in range(KVH):
            tile = jnp.where(low_lane, *pairs[h])
            kv_ref[rows, 128 * h : 128 * h + 128] = rope(tile, tables).astype(BF16)


def chunk_bias(meta, slot, chunk, key_axis):
    shape = (2 * BLK, BLK) if key_axis == 0 else (BLK, 2 * BLK)
    key = lax.broadcasted_iota(jnp.int32, shape, key_axis) + chunk * (2 * BLK)
    query = lax.broadcasted_iota(jnp.int32, shape, 1 - key_axis) + meta[slot, 0] * BLK
    live_end = meta[slot, 0] * BLK + meta[slot, 1]
    allowed = (key <= query) & ((query < live_end) | (key == query))
    bias = jnp.where(allowed, 0.0, -1e30)
    return jnp.concatenate([bias] * (HEADS // KVH), axis=1 - key_axis)


def chunk_blocks(meta, slot, chunk):
    return meta[slot, 4 + 2 * chunk], meta[slot, 5 + 2 * chunk]


def key_tile(kv_ref, blocks, h):
    lanes = slice(128 * h, 128 * h + 128)
    rows = [pl.ds(pl.multiple_of(block * BLK, BLK), BLK) for block in blocks]
    return jnp.concatenate([kv_ref[r, lanes] for r in rows], axis=0)


def turned_tile(kv_t_s, blocks, h):
    return jnp.concatenate([kv_t_s[block, h] for block in blocks], axis=1)


def stacked(ref, rows, h):
    at = 128 * (HEADS // KVH) * h
    return jnp.concatenate(
        [ref[rows, at + 128 * j : at + 128 * j + 128] for j in range(HEADS // KVH)], axis=0
    )


def turn_keys(kv_ref, kv_t_s):
    @pl.loop(0, kv_t_s.shape[0])
    def _(block):
        rows = pl.ds(pl.multiple_of(block * BLK, BLK), BLK)
        for h in range(KVH):
            kv_t_s[block, h] = kv_ref[rows, 128 * h : 128 * h + 128].T


def over_chunks(meta, slot, count, visit, key_axis):
    open_chunks = jnp.where(meta[slot, 1] == BLK, count - 1, 0)

    @pl.loop(0, open_chunks)
    def _(chunk):
        visit(chunk, None)

    @pl.loop(open_chunks, count)
    def _(chunk):
        visit(chunk, chunk_bias(meta, slot, chunk, key_axis))


def attention_forward(meta, q_ref, kv_ref, kv_t_s, q_t_s, low_ref, lowt_ref, mixed_s, lse_s, peak_s, accum_s):
    group = HEADS // KVH
    turn_keys(kv_ref, kv_t_s)

    @pl.loop(0, q_ref.shape[0] // BLK)
    def _(slot):
        rows = pl.ds(pl.multiple_of(slot * BLK, BLK), BLK)
        peak_s[...] = jnp.full_like(peak_s, -1e30)
        accum_s[...] = jnp.zeros_like(accum_s)
        key_row = lax.broadcasted_iota(jnp.int32, (BLK, 2 * BLK), 0) < HD
        for head in range(HEADS):
            h, j = head // group, head % group
            q_t_s[slot, h, :, BLK * j : BLK * j + BLK] = q_ref[rows, 128 * head : 128 * head + 128].T

        def visit(chunk, bias):
            blocks = chunk_blocks(meta, slot, chunk)
            for h in range(KVH):
                scores = dot(key_tile(kv_ref, blocks, h), q_t_s[slot, h])
                scores = scores if bias is None else scores + bias
                old = peak_s[h, 0:1, :]
                new = jnp.maximum(old, jnp.max(scores, axis=0, keepdims=True))
                probs = jnp.exp(scores - new).astype(BF16)
                tile = turned_tile(kv_t_s, blocks, h)
                ones = jnp.where(key_row, jnp.ones_like(tile), tile)
                accum_s[h] = accum_s[h] * jnp.exp(old - new) + dot(ones, probs)
                peak_s[h, 0:1, :] = new

        over_chunks(meta, slot, meta[slot, 2], visit, 0)

        for h in range(KVH):
            total = accum_s[h, 0:1, :]
            lse_s[slot, h, 0:1, :] = peak_s[h, 0:1, :] + jnp.log(total)
            mixed = accum_s[h, HD:, :] / total
            for j in range(group):
                head = h * group + j
                mixed_s[slot, HD * head : HD * head + HD, :] = mixed[:, BLK * j : BLK * j + BLK]
        lowt_ref[:, rows] = mixed_s[slot].astype(BF16)
        low_ref[rows, :] = mixed_s[slot].T.astype(BF16)


def feed_forward(
    meta, x_ref, cot_ref, wa_ref, wgu_ref, wd_ref, actt_ref, gres_ref, gb_ref, gain_ref,
    low_s, mixed_s, do_s, do_t_s, delta_s, second_s, second_t_s, grad_gu_s, hidden_s, gm_s, wide_s,
):
    group = HEADS // KVH
    gain = gain_row(wa_ref, O_AT + HALF)
    high_lane = lane_index(BLK) >= HD
    gain_ref[...] = jnp.zeros_like(gain_ref)
    w_out = wa_ref[:, O_AT : O_AT + QW]
    rows_all = x_ref.shape[0]
    blocks = STEP // BLK

    def living(i):
        row = lax.broadcasted_iota(jnp.int32, (BLK, 1), 0)
        return jnp.concatenate([(row < meta[i * blocks + b, 1]).astype(F32) for b in range(blocks)], axis=0)

    def normalized(i):
        residual = gres_ref[i * STEP : (i + 1) * STEP, :]
        inv = lax.rsqrt(jnp.mean(residual * residual, axis=1, keepdims=True) + EPS)
        return residual * inv, inv

    for i in range(rows_all // STEP):
        rows = slice(i * STEP, (i + 1) * STEP)
        gres_ref[rows, :] = x_ref[rows, :].astype(F32) + dot(low_s[rows, :], w_out)
        second = (normalized(i)[0] * gain).astype(BF16)
        second_s[rows, :] = second
        second_t_s[:, rows] = second.T
        gm_s[rows, :] = (cot_ref[rows, :].astype(F32) * living(i)).astype(BF16)

    width = 256

    @pl.loop(0, FF // width)
    def _(c):
        at = pl.multiple_of(c * width, width)
        here, there = pl.ds(at, width), pl.ds(pl.multiple_of(FF + at, width), width)
        gate, up = dot(second_s[...], wgu_ref[:, here]), dot(second_s[...], wgu_ref[:, there])
        grad_hidden = dot_nt(gm_s[...], wd_ref[here, :])
        sigma = jax.nn.sigmoid(gate)
        swish = gate * sigma
        hidden_s[:, here] = (swish * up).astype(BF16)
        grad_gu_s[:, there] = (grad_hidden * swish).astype(BF16)
        grad_gu_s[:, here] = (grad_hidden * up * (sigma * (1.0 + gate * (1.0 - sigma)))).astype(BF16)

    cuts = [(at, min(256, D - at)) for at in range(0, D, 256)]
    for at, wide in cuts:
        wide_s[:, at : at + wide] = dot_nt(grad_gu_s[...], wgu_ref[at : at + wide, :])
    for i in range(rows_all // STEP):
        rows = slice(i * STEP, (i + 1) * STEP)
        out = gres_ref[rows, :] + dot(hidden_s[rows, :], wd_ref[...])
        actt_ref[:, rows] = out.astype(BF16).T
        norm, inv = normalized(i)
        grad_second = wide_s[rows, :]
        grad_final = cot_ref[rows, :].astype(F32) * living(i)
        scaled = grad_second * gain
        grad_res = grad_final + inv * (scaled - norm * jnp.mean(scaled * norm, axis=1, keepdims=True))
        gres_ref[rows, :] = grad_res
        grad_branch = grad_res.astype(BF16)
        gb_ref[rows, :QW] = grad_branch
        gb_ref[rows, QW:] = jnp.zeros((STEP, 128 - HD), BF16)
        gain_ref[0:1, :] += jnp.sum(grad_second * norm, axis=0, keepdims=True)
    for at, wide in cuts:
        wide_s[:, at : at + wide] = dot_nt(gb_ref[:, :QW], w_out[at : at + wide, :])
    for i in range(rows_all // STEP):
        grad_att_low = wide_s[i * STEP : (i + 1) * STEP, :].astype(BF16)
        grad_att_t = grad_att_low.T
        grad_att = grad_att_low.astype(F32)
        for b in range(blocks):
            slot = i * blocks + b
            here = slice(i * STEP + b * BLK, i * STEP + (b + 1) * BLK)
            part = slice(b * BLK, (b + 1) * BLK)
            do_t_s[slot] = grad_att_t[:, part]
            product = grad_att_t[:, part].astype(F32) * mixed_s[slot]
            for head in range(HEADS):
                at = 128 * (head // 2)
                if head == HEADS - 1:
                    tile = jnp.concatenate([grad_att[part, at : at + HD]] * 2, axis=1)
                else:
                    tile = grad_att[part, at : at + 128]
                    tile = tile if head % 2 else swap(tile)
                tile = jnp.where(high_lane, tile, 0.0).astype(BF16)
                do_s[here, 128 * head : 128 * head + 128] = tile
                h, j = head // group, head % group
                delta_s[slot, h, 0:1, BLK * j : BLK * j + BLK] = jnp.sum(
                    product[HD * head : HD * head + HD, :], axis=0, keepdims=True
                )


def weight_grads(dgu_ref, dd_ref, second_t_s, grad_gu_s, hidden_s, gm_s):
    width = 512

    @pl.loop(0, 2 * FF // width)
    def _(c):
        here = pl.ds(pl.multiple_of(c * width, width), width)
        dgu_ref[:, here] = dot(second_t_s[...], grad_gu_s[:, here]).astype(BF16)

    @pl.loop(0, FF // width)
    def _(c):
        here = pl.ds(pl.multiple_of(c * width, width), width)
        dd_ref[here, :] = dot_tn(hidden_s[:, here], gm_s[...]).astype(BF16)


def in_parts(row):
    parts, rest = [], row
    for _ in range(3):
        parts.append(rest.astype(BF16).astype(F32))
        rest = rest - parts[-1]
    index = lax.broadcasted_iota(jnp.int32, (128, row.shape[1]), 0)
    table = jnp.zeros(index.shape, F32)
    for i, part in enumerate(parts):
        table = jnp.where(index == i, part, table)
    return table.T.astype(BF16)


def attention_backward(
    meta, q_ref, kv_ref, kv_t_s, q_t_s, turned_ref, steps_ref, do_s, do_t_s, lse_s, delta_s, gq_ref, dkv_s, dq_s,
    both_s, both_t_s,
):
    group = HEADS // KVH
    tall = group * BLK
    dkv_s[...] = jnp.zeros_like(dkv_s)
    both_t_s[...] = jnp.zeros_like(both_t_s)

    @pl.loop(0, q_ref.shape[0] // BLK)
    def _(slot):
        rows = pl.ds(pl.multiple_of(slot * BLK, BLK), BLK)
        dq_s[...] = jnp.zeros_like(dq_s)
        row = lax.broadcasted_iota(jnp.int32, (BLK, 2 * BLK), 0)
        ones = jnp.where(row < 3, 1.0, 0.0).astype(BF16)
        for h in range(KVH):
            both_s[h, :tall, :128] = stacked(q_ref, rows, h)
            both_s[h, tall:, :128] = stacked(do_s, rows, h)
            both_s[h, :tall, 128:] = in_parts(-lse_s[slot, h, 0:1, :])
            both_s[h, tall:, 128:] = in_parts(-delta_s[slot, h, 0:1, :])
            both_t_s[h, :, :tall] = q_t_s[slot, h]
            for j in range(group):
                head = h * group + j
                both_t_s[h, HD:, tall + BLK * j : tall + BLK * j + BLK] = do_t_s[slot, HD * head : HD * head + HD]

        def visit(chunk, bias):
            blocks = chunk_blocks(meta, slot, chunk)
            for h in range(KVH):
                wide = jnp.concatenate([turned_tile(kv_t_s, blocks, h), ones], axis=0)
                products = dot(both_s[h], wide)
                scores = products[:tall]
                probs = jnp.exp(scores if bias is None else scores + bias)
                grads = (probs * products[tall:]).astype(BF16)
                dq_s[h] += dot(grads, key_tile(kv_ref, blocks, h))
                sides = jnp.concatenate([grads, probs.astype(BF16)], axis=0)
                terms = dot(both_t_s[h], sides)
                dkv_s[blocks[0], h] += terms[:, :BLK]
                dkv_s[blocks[1], h] += terms[:, BLK:]

        over_chunks(meta, slot, jnp.where(meta[slot, 1] > 0, meta[slot, 2], 0), visit, 1)

        cosine, sine = turned_tables(meta, slot, turned_ref, steps_ref)
        parts = []
        for head in range(HEADS):
            h, j = head // group, head % group
            turned = dq_s[h, BLK * j : BLK * j + BLK, :].T
            parts += turned_rope_back(turned, cosine * SCALE, sine * SCALE)
        gq_ref[rows, :QW] = jnp.concatenate(parts, axis=0).T.astype(BF16)
        gq_ref[rows, QW:] = jnp.zeros((BLK, HD), BF16)


def layer_kernel(
    meta, q_ref, kv_ref, turned_ref, steps_ref, x_hbm, cot_hbm, wa_hbm, gu_hbm, d_hbm,
    gq_ref, dkv_ref, gain_ref, lowt_hbm, actt_hbm, gres_hbm, gb_hbm, dgu_hbm, dd_hbm,
    mixed_s, lse_s, delta_s, peak_s, accum_s, dq_s, do_s, second_s, second_t_s, grad_gu_s, hidden_s, gm_s, dkv_s, low_s,
    both_s, both_t_s, kv_t_s, q_t_s, do_t_s, wide_s, x_s, cot_s, wa_s, wgu_s, wd_s, lowt_s, actt_s, gres_s, gb_s, dgu_s, dd_s, load_sem, store_sem,
):
    loads = [
        pltpu.make_async_copy(source, target, load_sem.at[i])
        for i, (source, target) in enumerate(
            ((x_hbm, x_s), (wa_hbm, wa_s), (cot_hbm, cot_s), (gu_hbm, wgu_s), (d_hbm, wd_s))
        )
    ]
    stores = [
        pltpu.make_async_copy(source, target, store_sem.at[i])
        for i, (source, target) in enumerate(
            (
                (lowt_s, lowt_hbm), (actt_s, actt_hbm), (gres_s, gres_hbm), (gb_s, gb_hbm),
                (dgu_s, dgu_hbm), (dd_s, dd_hbm),
            )
        )
    ]
    for copy in loads:
        copy.start()
    attention_forward(meta, q_ref, kv_ref, kv_t_s, q_t_s, low_s, lowt_s, mixed_s, lse_s, peak_s, accum_s)
    stores[0].start()
    for copy in loads:
        copy.wait()
    feed_forward(
        meta, x_s, cot_s, wa_s, wgu_s, wd_s, actt_s, gres_s, gb_s, gain_ref,
        low_s, mixed_s, do_s, do_t_s, delta_s, second_s, second_t_s, grad_gu_s, hidden_s, gm_s, wide_s,
    )
    for copy in stores[1:4]:
        copy.start()
    weight_grads(dgu_s, dd_s, second_t_s, grad_gu_s, hidden_s, gm_s)
    for copy in stores[4:]:
        copy.start()
    attention_backward(
        meta, q_ref, kv_ref, kv_t_s, q_t_s, turned_ref, steps_ref, do_s, do_t_s, lse_s, delta_s, gq_ref, dkv_s,
        dq_s, both_s, both_t_s,
    )
    dkv_ref[...] = dkv_s[...].astype(BF16)
    for copy in stores:
        copy.wait()


VMEM_LIMIT = 62 << 20


def layer(meta, tokens, cotangent, queries, keyval, packed, gateup, down, turned, steps):
    rows, slots, group = tokens.shape[0], tokens.shape[0] // BLK, HEADS // KVH
    keys = keyval.shape[0]
    anywhere = pl.BlockSpec(memory_space=pl.ANY)
    results = [((QW, rows), BF16), ((D, rows), BF16), ((rows, D), F32), ((rows, QW + HD), BF16)]
    results += [((D, 2 * FF), BF16), ((FF, D), BF16)]
    return pl.pallas_call(
        layer_kernel,
        out_shape=(
            jax.ShapeDtypeStruct((rows, QW + HD), BF16),
            jax.ShapeDtypeStruct((keys // BLK, KVH, BLK, BLK), BF16),
            jax.ShapeDtypeStruct((8, D), F32),
        )
        + tuple(jax.ShapeDtypeStruct(*r) for r in results),
        in_specs=[pl.BlockSpec(memory_space=pltpu.SMEM)] + vmem(4) + [anywhere] * 5,
        out_specs=tuple(vmem(3)) + (anywhere,) * 6,
        scratch_shapes=[
            pltpu.VMEM((slots, QW, BLK), F32),
            pltpu.VMEM((slots, KVH, 8, group * BLK), F32),
            pltpu.VMEM((slots, KVH, 8, group * BLK), F32),
            pltpu.VMEM((KVH, 8, group * BLK), F32),
            pltpu.VMEM((KVH, BLK, group * BLK), F32),
            pltpu.VMEM((KVH, group * BLK, BLK), F32),
            pltpu.VMEM((rows, 128 * HEADS), BF16),
            pltpu.VMEM((rows, D), BF16),
            pltpu.VMEM((D, rows), BF16),
            pltpu.VMEM((rows, 2 * FF), BF16),
            pltpu.VMEM((rows, FF), BF16),
            pltpu.VMEM((rows, D), BF16),
            pltpu.VMEM((keys // BLK, KVH, BLK, BLK), F32),
            pltpu.VMEM((rows, QW), BF16),
            pltpu.VMEM((KVH, 2 * group * BLK, 256), BF16),
            pltpu.VMEM((KVH, BLK, 2 * group * BLK), BF16),
            pltpu.VMEM((keys // BLK, KVH, BLK, BLK), BF16),
            pltpu.VMEM((slots, KVH, BLK, group * BLK), BF16),
            pltpu.VMEM((slots, QW, BLK), BF16),
            pltpu.VMEM((rows, D), F32),
            pltpu.VMEM((rows, D), BF16),
            pltpu.VMEM((rows, D), BF16),
            pltpu.VMEM((D, WIDE_A), BF16),
            pltpu.VMEM((D, 2 * FF), BF16),
            pltpu.VMEM((FF, D), BF16),
        ]
        + [pltpu.VMEM(*r) for r in results]
        + [pltpu.SemaphoreType.DMA((5,)), pltpu.SemaphoreType.DMA((6,))],
        compiler_params=pltpu.CompilerParams(vmem_limit_bytes=VMEM_LIMIT),
        name="layer",
    )(meta, queries, keyval, turned, steps, tokens, cotangent, packed, gateup, down)


def normed_rows(i, x_ref, gain, normed_s):
    rows = slice(i * STEP, (i + 1) * STEP)
    x = x_ref[rows, :].astype(F32)
    inv = lax.rsqrt(jnp.mean(x * x, axis=1, keepdims=True) + EPS)
    normed_s[:, rows] = (x * inv * gain).astype(BF16).T


def input_grad_rows(
    meta, i, x_ref, wa_ref, gain, gq_ref, dkv_ref, gres_ref, turned_ref, steps_ref, int_ref, last_s, values_s
):
    low_lane = lane_index(BLK) < HD
    rows = slice(i * STEP, (i + 1) * STEP)
    x = x_ref[rows, :].astype(F32)
    inv = lax.rsqrt(jnp.mean(x * x, axis=1, keepdims=True) + EPS)
    norm = x * inv
    for b in range(STEP // BLK):
        slot = i * (STEP // BLK) + b
        here = slice(slot * BLK, slot * BLK + BLK)
        cosine, sine = turned_tables(meta, slot, turned_ref, steps_ref)
        tiles = []
        for h in range(KVH):
            tile = dkv_ref[slot, h].astype(F32)
            tiles.append(jnp.concatenate(turned_rope_back(tile, cosine, sine) + [tile[HD:]], axis=0).T)
        last = gq_ref[here, 512:640].astype(F32)
        last_s[here, :128] = jnp.where(low_lane, last, swap(tiles[0])).astype(BF16)
        last_s[here, 128:] = jnp.where(low_lane, tiles[1], swap(tiles[2])).astype(BF16)
        values_s[here, :128] = jnp.where(low_lane, 0.0, tiles[0]).astype(BF16)
        values_s[here, 128:] = jnp.where(low_lane, swap(tiles[1]), tiles[2]).astype(BF16)
    grad_normed = (
        dot_nt(gq_ref[rows, :512], wa_ref[:, :512])
        + dot_nt(last_s[rows, :], wa_ref[:, 512:HALF])
        + dot_nt(values_s[rows, :], wa_ref[:, O_AT + 512 : O_AT + HALF])
    )
    scaled = grad_normed * gain
    grad = gres_ref[rows, :] + inv * (scaled - norm * jnp.mean(scaled * norm, axis=1, keepdims=True))
    int_ref[:, rows] = grad.T
    return jnp.sum(grad_normed * norm, axis=0, keepdims=True)


def put_rows(da_ref, at, value):
    shards, rows = da_ref.shape[:2]
    for f in range(shards):
        da_ref[f, :, at : at + value.shape[1]] = value[f * rows : (f + 1) * rows].astype(BF16)


def early_grads(da_ref, normed_s, gq_ref, lowt_ref, gb_ref):
    for c in range(0, 512, 256):
        put_rows(da_ref, c, dot(normed_s[...], gq_ref[:, c : c + 256]))
        put_rows(da_ref, O_AT + c, dot(lowt_ref[...], gb_ref[:, c : c + 256]))


def late_grads(da_ref, normed_s, last_s, values_s, lowt_ref, gb_ref, gains, gain_ref):
    put_rows(da_ref, 512, dot(normed_s[...], last_s[...]))
    both = dot(lowt_ref[...], gb_ref[:, 512:640]) + dot(normed_s[...], values_s[:, :128])
    put_rows(da_ref, O_AT + 512, both)
    put_rows(da_ref, O_AT + 640, dot(normed_s[...], values_s[:, 128:]))
    put_rows(da_ref, HALF, jnp.broadcast_to(gains, (128, D)).T)
    put_rows(da_ref, O_AT + HALF, jnp.broadcast_to(gain_ref[0:1, :], (128, D)).T)


def finish_kernel(
    meta, x_ref, wa_ref, gq_ref, dkv_ref, gres_ref, gb_ref, lowt_ref, gain_ref, turned_ref, steps_ref,
    int_ref, da_ref, normed_s, last_s, values_s,
):
    gain = gain_row(wa_ref, HALF)
    gains = jnp.zeros((1, D), F32)
    for i in range(x_ref.shape[0] // STEP):
        normed_rows(i, x_ref, gain, normed_s)
        gains = gains + input_grad_rows(
            meta, i, x_ref, wa_ref, gain, gq_ref, dkv_ref, gres_ref, turned_ref, steps_ref, int_ref,
            last_s, values_s,
        )
    early_grads(da_ref, normed_s, gq_ref, lowt_ref, gb_ref)
    late_grads(da_ref, normed_s, last_s, values_s, lowt_ref, gb_ref, gains, gain_ref)


def finish_scratch(rows):
    return [pltpu.VMEM((D, rows), BF16), pltpu.VMEM((rows, 256), BF16), pltpu.VMEM((rows, 256), BF16)]


def finish(meta, tokens, packed, gq, dkv, gres, gb, lowt, gain, turned, steps):
    rows = tokens.shape[0]
    input_grad, d_packed = pl.pallas_call(
        finish_kernel,
        out_shape=(
            jax.ShapeDtypeStruct((D, rows), F32),
            jax.ShapeDtypeStruct((1, D, WIDE_A), BF16),
        ),
        in_specs=[pl.BlockSpec(memory_space=pltpu.SMEM)] + vmem(10),
        out_specs=tuple(vmem(2)),
        scratch_shapes=finish_scratch(rows),
        compiler_params=pltpu.CompilerParams(vmem_limit_bytes=VMEM_LIMIT),
        name="finish",
    )(meta, tokens, packed, gq, dkv, gres, gb, lowt, gain, turned, steps)
    return input_grad, d_packed[0]


def pack(w_query, w_keyval, w_out, w_gateup, w_down, norm_gains):
    rows = w_query.shape[0]
    spread = [jnp.broadcast_to(norm_gains[:, g : g + 1], (rows, 128)) for g in range(2)]
    packed = jnp.concatenate(
        [w_query, w_keyval[:, 0], spread[0], w_out, w_keyval[:, 1], spread[1]], axis=1
    )
    return packed.astype(BF16), w_gateup.reshape(rows, 2 * FF).astype(BF16), w_down.astype(BF16)


def for_sending(value):
    return jax.tree.map(lambda a: a.astype(jnp.bfloat16) if a.dtype == jnp.float32 else a, value)


def orthogonal(matrix):
    flipped = matrix.shape[0] > matrix.shape[1]
    iterate = matrix.T if flipped else matrix
    iterate = iterate / (jnp.sqrt(jnp.sum(iterate * iterate)) + 1e-07)
    for turn in range(NS_STEPS):
        gram_matrix = jnp.dot(iterate, iterate.T, precision=lax.Precision.HIGHEST)
        polynomial = COEF_B * gram_matrix + COEF_C * jnp.dot(
            gram_matrix, gram_matrix, precision=lax.Precision.HIGHEST
        )
        iterate = COEF_A * iterate + jnp.dot(polynomial, iterate, precision=lax.Precision.HIGHEST)
    return iterate.T if flipped else iterate


def muon_step(matrix):
    return MUON_RATE * math.sqrt(max(matrix.shape[0], matrix.shape[1])) * orthogonal(matrix)


def owner_branch(matrix_rows, matrix_cols, widest, received):
    group_size = received.shape[0]
    shard_size = matrix_rows * matrix_cols // group_size
    full_matrix = received[:, :shard_size].reshape(matrix_rows, matrix_cols)
    update_rows = muon_step(full_matrix).reshape(group_size, shard_size)
    return jnp.pad(update_rows, ((0, 0), (0, widest - shard_size)))


def zero_branch(received):
    return jnp.zeros_like(received)


def muon_exchange(pieces):
    fsdp_size, fsdp_index = lax.axis_size("fsdp"), lax.axis_index("fsdp")
    flat_sizes = [piece.size for piece in pieces]
    widest = max(flat_sizes)
    padded = [jnp.pad(piece.reshape(-1), (0, widest - piece.size)) for piece in pieces]
    outgoing = jnp.stack(padded + [jnp.zeros((widest,), F32)] * (fsdp_size - len(pieces)))
    received = lax.all_to_all(
        outgoing.astype(BF16), "fsdp", split_axis=0, concat_axis=0, tiled=True
    ).astype(F32)
    branches = [
        partial(owner_branch, piece.shape[0] * fsdp_size, piece.shape[1], widest)
        for piece in pieces
    ] + [zero_branch]
    update_rows = lax.switch(jnp.minimum(fsdp_index, len(pieces)), branches, received)
    returned = lax.all_to_all(
        update_rows.astype(BF16), "fsdp", split_axis=0, concat_axis=0, tiled=True
    ).astype(F32)
    return [returned[m, : flat_sizes[m]].reshape(pieces[m].shape) for m in range(len(pieces))]


def gather_rows_xla(shard):
    return lax.all_gather(shard, "fsdp", axis=0, tiled=True)


def reduce_rows_xla(grads):
    return lax.psum(lax.psum_scatter(grads, "fsdp", scatter_dimension=0, tiled=True), "dp")


START_SPLIT = (False, True, True, False)
REDUCE_SPLIT = (False, True, True, False, False)
START_ORDER = (
    ("z", 0, 0), ("z", 1, 0), ("z", 2, 0), ("prep",), ("side", 0, 0), ("z", 3, 0), ("z", 0, 1), ("z", 0, 2),
    ("side", 1, 0), ("side", 2, 0), ("z", 1, 1), ("side", 3, 0), ("z", 1, 2), ("side", 0, 2), ("side", 0, 1),
    ("wa",), ("side", 1, 2), ("side", 1, 1), ("proj", 0), ("z", 0, 3), ("z", 2, 2), ("z", 2, 1), ("proj", 1),
    ("side", 2, 2), ("cross", 0, 2), ("z", 1, 3), ("z", 3, 2), ("side", 3, 2), ("side", 2, 1), ("proj", 2),
    ("z", 3, 1), ("z", 2, 3), ("cross", 1, 2), ("z", 3, 3), ("side", 2, 3), ("side", 0, 3), ("side", 1, 3),
    ("side", 3, 1), ("cross", 0, 1), ("cross", 1, 1), ("kvpass", 0), ("cross", 3, 2), ("side", 3, 3),
    ("cross", 2, 2), ("cross", 2, 1), ("kvpass", 1), ("kvpass", 2), ("cross", 3, 1),
)
REDUCE_ORDER = (
    ("pp", 0, 0), ("pp", 1, 0), ("pp", 2, 0), ("kvp", 0), ("P", 0, 1), ("P", 0, 2), ("P", 0, 3), ("P", 1, 3),
    ("P", 1, 1), ("pp", 3, 0), ("P", 2, 3), ("pp", 0, 1), ("pp", 1, 1), ("P", 1, 2), ("kvx",), ("S", 0, 2),
    ("Z", 0, 3), ("P", 2, 2), ("S", 0, 1), ("prep",), ("pp", 2, 1), ("P", 2, 1), ("Z", 1, 3), ("pp", 3, 1),
    ("kvp", 1), ("da1",), ("P", 3, 1), ("Z", 2, 3), ("S", 1, 2), ("P", 3, 3), ("pp4",), ("P", 3, 2),
    ("Z", 0, 1), ("S", 1, 1), ("fin", 0), ("Z", 0, 2), ("fin", 1), ("P", 1, 4), ("Z", 1, 1), ("P", 0, 4),
    ("fin", 2), ("Z", 1, 2), ("S", 2, 1), ("S", 2, 2), ("da2",), ("Z", 2, 1), ("S", 3, 1), ("S", 3, 2),
    ("pp0",), ("P", 3, 4), ("Z", 0, 4), ("Z", 2, 2), ("P", 0, 0), ("P", 2, 4), ("P", 1, 0), ("Z", 3, 1),
    ("Z", 3, 3), ("P", 2, 0), ("Z", 0, 0), ("P", 3, 0), ("Z", 1, 4), ("Z", 2, 4), ("Z", 3, 2), ("Z", 1, 0),
    ("Z", 2, 0), ("F", 3), ("Z", 3, 4), ("Z", 3, 0), ("F", 1), ("F", 2), ("F", 4), ("F", 0),
)


WIDE_AT, TALL_AT = (2, 5), 3
SQUARE_AT, NARROW_AT = (0, 7), (6, 1)
NARROW = 256


def by_core(pair, core):
    return pair[0] + (pair[1] - pair[0]) * core


def newton_schulz(x_s, low_s, gram_s, gram_low_s, poly_s, factor):
    size, width = x_s.shape
    cuts = [(at, min(256, size - at)) for at in range(0, size, 256)]

    @pl.loop(0, NS_STEPS)
    def _(step):
        shift = jnp.where(step >= NS_STEPS - 2, 1.0, 0.0)
        first = jnp.where(step == 0, factor, 1.0)
        for at, wide in cuts:
            gram = dot_nt(low_s[...], low_s[at : at + wide, :]) * (first * first)
            row = lax.broadcasted_iota(jnp.int32, (size, wide), 0)
            column = lax.broadcasted_iota(jnp.int32, (size, wide), 1) + at
            gram = gram - jnp.where(row == column, shift, 0.0)
            gram_s[:, at : at + wide] = gram
            gram_low_s[:, at : at + wide] = gram.astype(BF16)
        for at, wide in cuts:
            square = dot(gram_low_s[...], gram_low_s[:, at : at + wide])
            poly = (COEF_B + 2.0 * COEF_C * shift) * gram_s[:, at : at + wide] + COEF_C * square
            poly_s[:, at : at + wide] = (poly * first).astype(BF16)
        keep = (COEF_A + COEF_B * shift + COEF_C * shift * shift) * first
        for at in range(0, width, 256):
            lanes = slice(at, at + 256)
            new = keep * x_s[:, lanes] + dot(poly_s[...], low_s[:, lanes])
            x_s[:, lanes] = new
            low_s[:, lanes] = new.astype(BF16)


def muon_part(
    place, a_ref, gu_ref, d_ref, mq_ref, mkv_ref, mo_ref, mgu_ref, md_ref,
    sq_out, nk_out, gu_out, d_out,
    my_gu, my_sq, my_nk, my_d, wide_s, sq_s, nk_s, tall_s, x_s, low_s, gram_s, gram_low_s, poly_s,
    in_send, in_recv, own_sem, out_send, out_recv, pair_send, pair_recv,
):
    count = 2 * place.lines
    rows, tall = my_gu.shape[0], my_d.shape[0]

    def moment(momentum, grad):
        return (MOMENTUM_DECAY * momentum + grad.astype(F32)).astype(BF16)

    my_nk[...] = jnp.zeros_like(my_nk)

    def moments_of(core, m_square):
        my_gu[...] = moment(mgu_ref[...], gu_ref[:, core * FF : core * FF + FF])
        at = core * O_AT
        my_sq[...] = moment(m_square[...], a_ref[:, at : at + QW])
        my_nk[:, :KVW] = moment(mkv_ref[...], a_ref[:, at + QW : at + HALF])
        part = slice(core * tall, (core + 1) * tall)
        my_d[...] = moment(md_ref[part, :], d_ref[part, :])

    pl.when(place.core == 0)(lambda: moments_of(0, mq_ref))
    pl.when(place.core == 1)(lambda: moments_of(1, mo_ref))

    tall_rows = pl.ds(pl.multiple_of(place.core * tall, 16), tall)
    wide_at, sq_at, nk_at = (by_core(p, place.core) for p in (WIDE_AT, SQUARE_AT, NARROW_AT))
    tall_core = 2 * place.x
    routes = (
        (my_gu, wide_s.at[place.f], wide_at, place.d),
        (my_d, tall_s.at[place.f, tall_rows], TALL_AT, tall_core),
        (my_sq, sq_s.at[place.f], sq_at, place.d),
        (my_nk, nk_s.at[place.f], nk_at, place.d),
    )

    def each_route(far, near):
        for i, (source, target, f, d) in enumerate(routes):
            here = (place.f == f) & (place.d == d)
            recv = in_recv.at[i, place.f] if i != 1 else in_recv.at[i, place.f + count * place.core]
            pl.when(jnp.logical_not(here))(
                lambda i=i, source=source, target=target, f=f, d=d, recv=recv: far(
                    remote(source, target, in_send.at[i], recv, (f, d))
                )
            )
            pl.when(here)(
                lambda i=i, source=source, target=target: near(
                    pltpu.make_async_copy(source, target, own_sem.at[i])
                )
            )

    each_route(lambda copy: copy.start(), lambda copy: copy.start())
    each_route(lambda copy: copy.wait_send(), lambda copy: copy.wait())

    def received(i, slot_of):
        for step in range(1, count):
            f = lax.rem(place.f + step, count)
            target = slot_of(f)
            remote(target, target, in_send.at[i], in_recv.at[i, f], place.sibling).wait_recv()

    def received_tall():
        for step in range(count):
            f = lax.rem(place.f + step, count)
            for core in range(2):
                if step == 0 and core == 0:
                    continue
                target = tall_s.at[f, pl.ds(core * tall, tall)]
                remote(target, target, in_send.at[1], in_recv.at[1, f + count * core], place.sibling).wait_recv()

    def scale_of():
        total = jnp.zeros((1, 1), F32)
        for at in range(0, FF, 256):
            part = x_s[:, at : at + 256]
            total = total + jnp.sum(jnp.sum(part * part, axis=0, keepdims=True), axis=1, keepdims=True)
            low_s[:, at : at + 256] = part.astype(BF16)
        return 1.0 / (jnp.sqrt(total) + 1e-07)

    is_wide, is_square, is_narrow = (place.f == at for at in (wide_at, sq_at, nk_at))
    is_tall = (place.f == TALL_AT) & (place.core == 0)
    is_small = is_square | is_narrow

    @pl.when(is_wide)
    def _():
        received(0, lambda f: wide_s.at[f])
        for f in range(count):
            x_s[f * rows : (f + 1) * rows, :] = wide_s[f].astype(F32)

    @pl.when(is_tall)
    def _():
        received_tall()
        for f in range(0, count, 2):
            pair = jnp.concatenate([tall_s[f], tall_s[f + 1]], axis=0).astype(F32)
            x_s[:, 2 * f * tall : 2 * (f + 2) * tall] = pair.T

    @pl.when(is_small)
    def _():
        x_s[...] = jnp.zeros_like(x_s)

    @pl.when(is_square)
    def _():
        received(2, lambda f: sq_s.at[f])
        for f in range(count):
            x_s[f * rows : (f + 1) * rows, :QW] = sq_s[f].astype(F32)

    @pl.when(is_narrow)
    def _():
        received(3, lambda f: nk_s.at[f])
        for f in range(count):
            x_s[f * rows : (f + 1) * rows, :NARROW] = nk_s[f].astype(F32)

    @pl.when(is_wide | is_tall | is_small)
    def _():
        newton_schulz(x_s, low_s, gram_s, gram_low_s, poly_s, scale_of())

    rate = MUON_RATE * math.sqrt(FF)
    small_rate = MUON_RATE * math.sqrt(D)

    def back(i, f, core):
        source = (
            wide_s.at[f], tall_s.at[f, pl.ds(core * tall, tall)] if i == 1 else None, sq_s.at[f], nk_s.at[f],
        )[i]
        return source, landing(i, core), (f, 2 * place.x + core)

    def landing(i, core):
        if i == 1:
            start = core * tall if isinstance(core, int) else pl.multiple_of(core * tall, 16)
            return d_out.at[pl.ds(start, tall)]
        return (gu_out, None, sq_out, nk_out)[i].at[core]

    def give(i, cores, act):
        for step in range(count):
            f = lax.rem(place.f + step, count)
            for n, core in enumerate(cores):
                source, target, device = back(i, f, core)
                if step == 0 and n == 0:
                    copy = pltpu.make_async_copy(source, target, own_sem.at[i])
                    act(copy, True)
                else:
                    slot = f + count * n
                    act(remote(source, target, out_send.at[i, slot], out_recv.at[i], device), False)

    def given(i, cores):
        give(i, cores, lambda copy, own: copy.start())
        give(i, cores, lambda copy, own: copy.wait() if own else copy.wait_send())

    @pl.when(is_wide)
    def _():
        for f in range(count):
            wide_s[f] = (x_s[f * rows : (f + 1) * rows, :] * rate).astype(BF16)
        given(0, (place.core,))

    @pl.when(is_tall)
    def _():
        for f in range(0, count, 2):
            pair = (x_s[:, 2 * f * tall : 2 * (f + 2) * tall] * rate).T
            tall_s[f] = pair[: 2 * tall].astype(BF16)
            tall_s[f + 1] = pair[2 * tall :].astype(BF16)
        given(1, (0, 1))

    @pl.when(is_square)
    def _():
        for f in range(count):
            sq_s[f] = (x_s[f * rows : (f + 1) * rows, :QW] * small_rate).astype(BF16)
        given(2, (place.core,))

    @pl.when(is_narrow)
    def _():
        for f in range(count):
            nk_s[f] = (x_s[f * rows : (f + 1) * rows, :NARROW] * small_rate).astype(BF16)
        given(3, (place.core,))

    makers = (is_wide, is_tall, is_square, is_narrow)

    def hand_over(i, core):
        target = landing(i, core)
        return remote(target, target, pair_send.at[i], pair_recv.at[i], place.sibling)

    for i in (2, 3, 1, 0):
        target = landing(i, place.core)

        def take(i=i, target=target):
            remote(target, target, pair_send.at[i], out_recv.at[i], place.sibling).wait_recv()

        pl.when(jnp.logical_not(makers[i]))(take)
        hand_over(i, place.core).start()
    for i in range(4):
        hand_over(i, 1 - place.core).wait_recv()
        hand_over(i, place.core).wait_send()


def muon_scratch(count, rows, tall):
    pieces = ((rows, FF), (rows, QW), (rows, NARROW), (tall, D))
    dma = pltpu.SemaphoreType.DMA
    return (
        [pltpu.VMEM(p, BF16) for p in pieces]
        + [pltpu.VMEM((count,) + p, BF16) for p in pieces[:3]]
        + [
            pltpu.VMEM((count, 2 * tall, D), BF16), pltpu.VMEM((D, FF), F32), pltpu.VMEM((D, FF), BF16),
            pltpu.VMEM((D, D), F32), pltpu.VMEM((D, D), BF16), pltpu.VMEM((D, D), BF16),
            dma((4,)), dma((4, 2 * count)), dma((4,)), dma((4, 2 * count)), dma((4,)), dma((4,)), dma((4,)),
        ]
    )


def halves_of(ref):
    return [ref.at[:, side, :] for side in range(2)] if len(ref.shape) == 3 else [ref]


def apart(shape):
    return (2, shape[0], shape[2]) if len(shape) == 3 else (1,) + tuple(shape)


def outputs_kernel(gain_rate, a_ref, gu_ref, d_ref, sq_ref, nk_ref, ugu_ref, ud_ref, gains_ref, gainm_ref, *refs):
    given, (gg_ref, gm_ref, gv_ref), results = refs[:10], refs[10:13], refs[13:28]
    held, made, (load_sem, store_sem) = refs[28:38], refs[38:53], refs[53:]
    loads = [
        [pltpu.make_async_copy(part, held[i].at[n], load_sem.at[i, n]) for n, part in enumerate(halves_of(given[i]))]
        for i in range(10)
    ]
    stores = [
        [pltpu.make_async_copy(made[i].at[n], part, store_sem.at[i, n]) for n, part in enumerate(halves_of(results[i]))]
        for i in range(15)
    ]
    order = ((3, 0), (3, 1), (4, 0), (0, 0), (2, 0), (1, 0), (1, 1))
    for i, n in order:
        loads[5 + i][n].start()
        loads[i][n].start()
    gain = jnp.concatenate(
        [a_ref[:, at : at + 128].astype(F32).T[0:1, :] for at in (HALF, O_AT + HALF)], axis=0
    )
    moments = GAIN_DECAY * gainm_ref[...] + gain
    gg_ref[...] = gain
    gm_ref[...] = moments
    gv_ref[...] = gains_ref[...] - gain_rate * moments
    sources = {
        (3, 0): lambda: (gu_ref[:, :FF], ugu_ref[0]),
        (3, 1): lambda: (gu_ref[:, FF:], ugu_ref[1]),
        (4, 0): lambda: (d_ref[...], ud_ref[...]),
        (0, 0): lambda: (a_ref[:, :QW], sq_ref[0]),
        (2, 0): lambda: (a_ref[:, O_AT : O_AT + QW], sq_ref[1]),
        (1, 0): lambda: (a_ref[:, QW:HALF], nk_ref[0, :, :KVW]),
        (1, 1): lambda: (a_ref[:, O_AT + QW : O_AT + HALF], nk_ref[1, :, :KVW]),
    }
    for i, n in order:
        loads[5 + i][n].wait()
        loads[i][n].wait()
        grad, update = sources[i, n]()
        grad = grad.astype(F32)
        made[3 * i][n] = grad
        made[3 * i + 1][n] = MOMENTUM_DECAY * held[5 + i][n] + grad
        made[3 * i + 2][n] = held[i][n] - update.astype(F32)
        for j in range(3):
            stores[3 * i + j][n].start()
    for copies in stores:
        for copy in copies:
            copy.wait()


def write_outputs(gain_rate, grads, updates, gains, gain_momentum, weights, momenta):
    outs = [jax.ShapeDtypeStruct(w.shape, F32) for w in weights for _ in range(3)]
    anywhere = pl.BlockSpec(memory_space=pl.ANY)
    return pl.pallas_call(
        partial(outputs_kernel, gain_rate),
        out_shape=(jax.ShapeDtypeStruct(gains.shape, F32),) * 3 + tuple(outs),
        in_specs=vmem(9) + [anywhere] * 10,
        out_specs=tuple(vmem(3)) + (anywhere,) * 15,
        scratch_shapes=[pltpu.VMEM(apart(w.shape), F32) for w in weights + momenta]
        + [pltpu.VMEM(apart(o.shape), F32) for o in outs]
        + [pltpu.SemaphoreType.DMA((10, 2)), pltpu.SemaphoreType.DMA((15, 2))],
        compiler_params=pltpu.CompilerParams(vmem_limit_bytes=VMEM_LIMIT),
        name="outputs",
    )(*grads, *updates, gains, gain_momentum, *weights, *momenta)


class Place:
    def __init__(self, lines):
        self.f, self.d = lax.axis_index("fsdp"), lax.axis_index("dp")
        self.line, self.column = self.f // 2, self.f % 2
        self.x, self.core = self.d // 2, self.d % 2
        self.lines = lines
        self.sibling = (self.f, self.d + 1 - 2 * self.core)
        self.across = (self.f, self.core + 2 * (1 - self.x))
        self.beside = (self.f + 1 - 2 * self.column, self.d)
        self.above = (self.f + 2, self.d)
        self.below = (self.f - 2, self.d)


def remote(source, target, send_sem, recv_sem, device):
    return pltpu.make_async_remote_copy(
        src_ref=source, dst_ref=target, send_sem=send_sem, recv_sem=recv_sem,
        device_id=device, device_id_type=pl.DeviceIdType.MESH,
    )


def greet(place, between, plane=False):
    barrier = pltpu.get_barrier_semaphore()

    def signal(device):
        pl.semaphore_signal(barrier, inc=1, device_id=device, device_id_type=pl.DeviceIdType.MESH)

    signal(place.sibling)
    signal(place.across)
    if plane:
        count = 2 * place.lines
        for step in range(1, count):
            f = lax.rem(place.f + step, count)
            for core in range(2):
                signal((f, 2 * place.x + core))
        between()
        pl.semaphore_wait(barrier, 2 * count)
        return
    signal(place.beside)
    pl.when(place.line > 0)(lambda: signal(place.below))
    pl.when(place.line < place.lines - 1)(lambda: signal(place.above))
    between()
    ends = (place.line == 0).astype(jnp.int32) + (place.line == place.lines - 1).astype(jnp.int32)
    pl.semaphore_wait(barrier, 5 - ends)


PARTS = 4


def half_parts(packed, gateup, down, core):
    tall = down.shape[0] // 2
    at = core * FF
    return (
        None if packed is None else packed.at[:, pl.ds(pl.multiple_of(core * O_AT, 128), O_AT)],
        gateup.at[:, pl.ds(pl.multiple_of(at, 128), FF // 2)],
        gateup.at[:, pl.ds(pl.multiple_of(at + FF // 2, 128), FF // 2)],
        down.at[pl.ds(pl.multiple_of(core * tall, 16), tall), :],
    )


def start_kernel(
    lines, lengths, assignment, xt_ref, cott_ref, gains_ref, wq_ref, wo_ref, wd_ref, inner_ref, outer_ref,
    wkv_hbm, wgu_hbm,
    meta, x_ref, cot_ref, q_ref, wa_ref, kv_out, gu_out, d_out,
    wkv_s, wgu_s, a_s, gu_s, d_s, a_out, kv_s,
    load_sem, own_sem, in_sem, pair_sem, up_sem, down_sem, side_sem, cross_sem, mate_sem,
    kv_in, kv_pair, kv_cross, kv_mate,
):
    place = Place(lines)
    shard_rows = a_s.shape[0]
    own = [
        pltpu.make_async_copy(source, target.at[place.f], own_sem.at[i])
        for i, (source, target) in enumerate(((a_s, a_out), (gu_s, gu_out), (d_s, d_out)))
    ]

    loads = [
        pltpu.make_async_copy(source.at[:, side, :], target.at[side], load_sem.at[i, side])
        for i, (source, target) in enumerate(((wkv_hbm, wkv_s), (wgu_hbm, wgu_s)))
        for side in range(2)
    ]
    for copy in loads:
        copy.start()

    def pack_first():
        for copy in loads:
            copy.wait()
        gains = jnp.broadcast_to(gains_ref[...][:, None, :], (2, 128, shard_rows))
        for side, w_ref in enumerate((wq_ref, wo_ref)):
            at = side * O_AT
            a_s[:, at : at + QW] = w_ref[...].astype(BF16)
            a_s[:, at + QW : at + HALF] = wkv_s[side].astype(BF16)
            a_s[:, at + HALF : at + O_AT] = gains[side].T.astype(BF16)
        for side in range(2):
            gu_s[:, side * FF : side * FF + FF] = wgu_s[side].astype(BF16)
        d_s[...] = wd_ref[...].astype(BF16)

    greet(place, pack_first)

    def full(shard, core):
        return half_parts(a_out.at[shard], gu_out.at[shard], d_out.at[shard], core)

    mine = half_parts(a_s, gu_s, d_s, place.core)

    def send(shard, k, sems, device, recv, source=None):
        target = full(shard, place.core)[k]
        return remote(target if source is None else source, target, sems.at[shard, k], recv.at[shard, k], device)

    def to_pair(shard, k):
        return send(shard, k, mate_sem, place.sibling, pair_sem)

    def if_sideways(k, run):
        if START_SPLIT[k]:
            pl.when(place.x == k % 2)(run)
        else:
            run()

    def on_z(t, k, action):
        for sign in (-1, 1) if t else (0,):
            shard = place.f + 2 * sign * t
            there = place.line + sign * t

            def go(shard=shard, sign=sign):
                source = None if sign else mine[k]
                if sign:
                    action(None, shard)
                if sign <= 0:
                    pl.when(place.line < lines - 1)(
                        lambda: action(send(shard, k, up_sem, place.above, in_sem, source))
                    )
                if sign >= 0:
                    pl.when(place.line > 0)(
                        lambda: action(send(shard, k, down_sem, place.below, in_sem, source))
                    )
                if_sideways(k, lambda: action(send(shard, k, side_sem, place.beside, in_sem, source)))
                if sign:
                    action(to_pair(shard, k))

            if sign:
                pl.when((there >= 0) & (there < lines))(go)
            else:
                go()

    def at_distance(base, t, run):
        if t == 0:
            run(base)
            return
        for sign in (-1, 1):
            there = place.line + sign * t
            pl.when((there >= 0) & (there < lines))(lambda sign=sign: run(base + 2 * sign * t))

    def on_side(t, k, action):
        def run(shard):
            action(None, shard)
            if START_SPLIT[k]:
                action(send(shard, k, cross_sem, place.across, in_sem))
            action(to_pair(shard, k))

        if_sideways(k, lambda: at_distance(place.beside[0], t, run))

    def on_cross(t, k, action):
        def run(shard):
            action(None, shard)
            action(to_pair(shard, k))

        if START_SPLIT[k]:
            pl.when(place.x != k % 2)(lambda: at_distance(place.beside[0], t, run))

    def start(k):
        def action(copy, shard=None):
            if copy is None:
                send(shard, k, up_sem, place.sibling, in_sem).wait_recv()
            else:
                copy.start()

        return action

    def finish_send(copy, shard=None):
        if copy is not None:
            copy.wait_send()

    def from_pair(k):
        def got(shard):
            target = full(shard, 1 - place.core)[k]
            remote(target, target, mate_sem.at[shard, k], pair_sem.at[shard, k], place.sibling).wait_recv()

        for t in range(lines):
            at_distance(place.beside[0], t, got)
            if t > 0:
                at_distance(place.f, t, got)

    def kv_rows(i):
        return pl.ds(i * STEP, STEP)

    def kv_send(i, device, sems, recv):
        return remote(kv_s.at[kv_rows(i)], kv_out.at[place.d, kv_rows(i)], sems.at[i], recv.at[i], device)

    def kv_pass(i):
        here = kv_out.at[place.across[1], kv_rows(i)]
        return remote(here, here, kv_mate.at[1, i], kv_pair.at[1, i], place.sibling)

    steps = x_ref.shape[0] // STEP
    slots = x_ref.shape[0] // BLK
    own_kv = pltpu.make_async_copy(kv_s, kv_out.at[place.d], own_sem.at[3])

    def prepare():
        for copy in own:
            copy.start()
        block_meta(lengths, assignment, place.d * slots, slots, meta)
        for i in range(steps):
            rows = slice(i * STEP, (i + 1) * STEP)
            x_ref[rows, :] = xt_ref[:, rows].T
            cot_ref[rows, :] = cott_ref[:, rows].T

    def unpack():
        own[0].wait()
        from_pair(0)
        for f in range(0, 2 * lines, 2):
            wa_ref[f * shard_rows : (f + 2) * shard_rows, :] = jnp.concatenate([a_out[f], a_out[f + 1]], axis=0)

    def project(i):
        gain = gain_row(wa_ref, HALF)
        project_rows(meta, i, x_ref, wa_ref, gain, inner_ref, outer_ref, q_ref, kv_s)
        kv_send(i, place.across, kv_cross, kv_in).start()
        kv_send(i, place.sibling, kv_mate.at[0], kv_pair.at[0]).start()

    def hand_on(i):
        kv_send(i, place.across, kv_cross, kv_in).wait_recv()
        kv_pass(i).start()

    for event, *which in START_ORDER:
        if event == "z":
            on_z(*which, start(which[1]))
        elif event == "side":
            on_side(*which, start(which[1]))
        elif event == "cross":
            on_cross(*which, start(which[1]))
        else:
            {"prep": prepare, "wa": unpack, "proj": project, "kvpass": hand_on}[event](*which)
    own_kv.start()
    for k in range(PARTS):
        if k > 0:
            from_pair(k)
        for t in range(lines):
            on_z(t, k, finish_send)
            on_side(t, k, finish_send)
            on_cross(t, k, finish_send)
    for i in range(steps):
        kv_send(i, place.sibling, kv_mate.at[0], kv_pair.at[0]).wait()
        kv_send(i, place.across, kv_cross, kv_in).wait_send()
        kv_pass(i).wait()
    for copy in own[1:] + [own_kv]:
        copy.wait()


def start_remote(lengths, assignment, tokens, cotangent, gains, weights, inner, outer, count):
    rows = tokens.shape[0]
    w_query, w_keyval, w_out, w_gateup, w_down = weights
    shard_rows, tall, steps = w_query.shape[0], w_down.shape[0], rows // STEP
    smem, anywhere = pl.BlockSpec(memory_space=pltpu.SMEM), pl.BlockSpec(memory_space=pl.ANY)
    shapes = ((shard_rows, WIDE_A), (shard_rows, 2 * FF), (tall, D))
    sems = pltpu.SemaphoreType.DMA((count, PARTS))
    meta, x, cot, queries, packed, keyval, gateup, down = pl.pallas_call(
        partial(start_kernel, count // 2),
        out_shape=(
            jax.ShapeDtypeStruct((rows // BLK, META), jnp.int32),
            jax.ShapeDtypeStruct((rows, D), BF16),
            jax.ShapeDtypeStruct((rows, D), BF16),
            jax.ShapeDtypeStruct((rows, 128 * HEADS), BF16),
            jax.ShapeDtypeStruct((D, WIDE_A), BF16),
            jax.ShapeDtypeStruct((4, rows, 2 * KVW), BF16),
            jax.ShapeDtypeStruct((count,) + shapes[1], BF16),
            jax.ShapeDtypeStruct((count,) + shapes[2], BF16),
        ),
        in_specs=[smem] * 2 + vmem(8) + [anywhere] * 2,
        out_specs=(smem,) + tuple(vmem(4)) + (anywhere,) * 3,
        scratch_shapes=[pltpu.VMEM(apart(w.shape), F32) for w in (w_keyval, w_gateup)]
        + [pltpu.VMEM(s, BF16) for s in shapes]
        + [pltpu.VMEM((count,) + shapes[0], BF16), pltpu.VMEM((rows, 2 * KVW), BF16)]
        + [pltpu.SemaphoreType.DMA((2, 2)), pltpu.SemaphoreType.DMA((4,))]
        + [sems] * 7
        + [
            pltpu.SemaphoreType.DMA((steps,)),
            pltpu.SemaphoreType.DMA((2, steps)),
            pltpu.SemaphoreType.DMA((steps,)),
            pltpu.SemaphoreType.DMA((2, steps)),
        ],
        compiler_params=pltpu.CompilerParams(
            collective_id=0, has_side_effects=True, vmem_limit_bytes=VMEM_LIMIT
        ),
        name="gather_and_project",
    )(
        lengths, assignment, tokens.T, cotangent.T, gains.T, w_query, w_out, w_down, inner, outer,
        w_keyval, w_gateup,
    )
    return (
        meta, x, cot, queries, packed, keyval.reshape(4 * rows, 2 * KVW),
        gateup.reshape(D, 2 * FF), down.reshape(FF, D),
    )


def start_kernel_plain(
    lengths, assignment, x_ref, wa_ref, inner_ref, outer_ref, meta, q_ref, kv_ref
):
    slots = x_ref.shape[0] // BLK
    block_meta(lengths, assignment, lax.axis_index("dp") * slots, slots, meta)
    gain = gain_row(wa_ref, HALF)
    for i in range(x_ref.shape[0] // STEP):
        project_rows(meta, i, x_ref, wa_ref, gain, inner_ref, outer_ref, q_ref, kv_ref)


def start_xla(lengths, assignment, tokens, cotangent, gains, weights, inner, outer):
    packed, gateup, down = (gather_rows_xla(s) for s in pack(*weights, gains))
    rows = tokens.shape[0]
    smem = pl.BlockSpec(memory_space=pltpu.SMEM)
    meta, queries, keyval = pl.pallas_call(
        start_kernel_plain,
        out_shape=(
            jax.ShapeDtypeStruct((rows // BLK, META), jnp.int32),
            jax.ShapeDtypeStruct((rows, 128 * HEADS), BF16),
            jax.ShapeDtypeStruct((rows, 2 * KVW), BF16),
        ),
        in_specs=[smem] * 2 + vmem(4),
        out_specs=(smem,) + tuple(vmem(2)),
        compiler_params=pltpu.CompilerParams(vmem_limit_bytes=VMEM_LIMIT),
        name="project",
    )(lengths, assignment, tokens, packed, inner, outer)
    keyval = lax.all_gather(keyval, "dp", axis=0, tiled=True)
    return meta, tokens, cotangent, queries, packed, keyval, gateup, down


SUMS = 5
LOADED = (3, 1, 2)


def visit_order(lines):
    return [sorted(range(lines), key=lambda other: (-abs(other - line), -other)) for line in range(lines)]


def reduce_kernel(
    lines, meta, x_ref, wa_ref, gq_ref, dkv_ref, gres_ref, gb_ref, lowt_ref, gain_ref, turned_ref, steps_ref,
    mq_ref, mo_ref, md_ref, mkv_hbm, mgu_hbm, gu_hbm, d_hbm,
    int_ref, a_out, gu_out, d_out, sq_out, nk_out, ugu_out, ud_out,
    normed_s, last_s, values_s, kv_s, kv_pair_s, kv_far_s, kv_cross_s,
    da_s, gu_s, d_s, a_pair, gu_pair, d_pair, a_in, gu_in, d_in,
    mkv_s, mgu_s, moment_sem, load_sem, kv_pair, kv_cross, kv_pair_send, kv_cross_send,
    pair_recv, recv, last_recv, pair_send, send, last_send, *muon_s
):
    place = Place(lines)
    half = FF // 2
    steps = x_ref.shape[0] // STEP
    order_table = visit_order(lines)

    def parts(a_half, gu_half, d_half):
        return (
            a_half.at[:, pl.ds(512, O_AT - 512)], gu_half.at[:, pl.ds(0, half)],
            gu_half.at[:, pl.ds(half, half)], d_half, a_half.at[:, pl.ds(0, 512)],
        )

    def core_parts(a_shard, gu_shard, d_shard, core):
        lanes = pl.multiple_of(core * O_AT, 128)
        early = late = None
        if a_shard is not None:
            early, late = a_shard.at[:, pl.ds(lanes, 512)], a_shard.at[:, pl.ds(lanes + 512, O_AT - 512)]
        if gu_shard is None:
            return late, None, None, None, early
        return (late,) + half_parts(None, gu_shard, d_shard, core)[1:] + (early,)

    def own_load(shard, k):
        source = core_parts(None, gu_hbm.at[shard], d_hbm.at[shard], place.core)[k]
        return pltpu.make_async_copy(source, pieces(shard)[k], load_sem.at[shard, k - 1])

    def pieces(shard):
        late, _, _, _, early = core_parts(da_s.at[shard], None, None, place.core)
        return (late,) + parts(a_pair.at[shard], gu_s.at[shard], d_s.at[shard])[1:4] + (early,)

    def mate(shard):
        return parts(a_pair.at[shard], gu_pair.at[shard], d_pair.at[shard])

    def inbox(way, spot):
        return parts(a_in.at[way, spot], gu_in.at[way, spot], d_in.at[way, spot])

    def order(t):
        spot = jnp.int32(0)
        for line in range(lines):
            spot = spot + order_table[line][t] * (place.line == line).astype(jnp.int32)
        return spot

    def to_pair(shard, k):
        source = core_parts(da_s.at[shard], gu_hbm.at[shard], d_hbm.at[shard], 1 - place.core)[k]
        return remote(source, mate(shard)[k], pair_send.at[shard, k], pair_recv.at[shard, k], place.sibling)

    def pass_on(shard, k, way, spot, device):
        return remote(
            mate(shard)[k], inbox(way, spot)[k], send.at[way, spot, k], recv.at[way, spot, k], device
        )

    def arrived(k, way, spot):
        target = inbox(way, spot)[k]
        remote(target, target, send.at[way, spot, k], recv.at[way, spot, k], place.sibling).wait_recv()

    def local_ready(shard, k):
        to_pair(shard, k).wait_recv()
        if k in LOADED:
            own_load(shard, k).wait()

    def total(shard, k, spot, ways):
        value = pieces(shard)[k][...].astype(F32) + mate(shard)[k][...].astype(F32)
        for way in ways:
            value = value + inbox(way, spot)[k][...].astype(F32)
        mate(shard)[k][...] = value.astype(BF16)

    def on_plane(k, run, other=None):
        if not REDUCE_SPLIT[k]:
            run(False)
            return
        pl.when(place.x == k % 2)(lambda: run(True))
        if other is not None:
            pl.when(place.x != k % 2)(other)

    def stage_pair(t, k):
        spot = order(t)
        shard = 2 * spot + 1 - place.column
        local_ready(shard, k)

        def away():
            total(shard, k, spot, ())
            pass_on(shard, k, 0, spot, place.across).start()

        if REDUCE_SPLIT[k]:
            pl.when(place.x != k % 2)(away)
        else:
            total(shard, k, spot, ())
            pass_on(shard, k, 1, spot, place.beside).start()

    def stage_side(t, k):
        spot = order(t)
        shard = 2 * spot + 1 - place.column

        def go():
            arrived(k, 0, spot)
            total(shard, k, spot, (0,))
            pass_on(shard, k, 1, spot, place.beside).start()

        if REDUCE_SPLIT[k]:
            pl.when(place.x == k % 2)(go)

    def stage_line(t, k):
        spot = order(t)
        shard = 2 * spot + place.column
        local_ready(shard, k)
        if REDUCE_SPLIT[k]:
            pl.when(place.x == k % 2)(lambda: arrived(k, 1, spot))
        else:
            arrived(k, 1, spot)

        def summed(ways):
            for way in ways:
                arrived(k, way, spot)
            if REDUCE_SPLIT[k]:
                pl.when(place.x == k % 2)(lambda: total(shard, k, spot, (1,) + ways))
                pl.when(place.x != k % 2)(lambda: total(shard, k, spot, ways))
            else:
                total(shard, k, spot, (1,) + ways)

        below, above = place.line > 0, place.line < lines - 1

        if t < lines - 1:

            @pl.when(spot > place.line)
            def _():
                pl.when(below)(lambda: summed((2,)))
                pl.when(jnp.logical_not(below))(lambda: summed(()))
                pass_on(shard, k, 2, spot, place.above).start()

            @pl.when(spot < place.line)
            def _():
                pl.when(above)(lambda: summed((3,)))
                pl.when(jnp.logical_not(above))(lambda: summed(()))
                pass_on(shard, k, 3, spot, place.below).start()

        else:
            pl.when(below & above)(lambda: summed((2, 3)))
            pl.when(jnp.logical_not(below))(lambda: summed((3,)))
            pl.when(jnp.logical_not(above))(lambda: summed((2,)))
            last(k).start()

    def last(k):
        return remote(
            mate(place.f)[k], inbox(4, 0)[k], last_send.at[0, k], last_recv.at[0, k], place.across
        )

    def share(k, core):
        target = core_parts(a_out, gu_out, d_out, core)[k]
        return remote(target, target, last_send.at[1, k], last_recv.at[1, k], place.sibling)

    def stage_last(k):
        last(k).wait_recv()
        target = core_parts(a_out, gu_out, d_out, place.core)[k]
        target[...] = added(mate(place.f)[k][...], inbox(4, 0)[k][...]).astype(BF16)
        share(k, place.core).start()

    def every(act, ks):
        for t in range(lines):
            for column in (1 - place.column, place.column):
                for k in ks:
                    act(2 * order(t) + column, k)

    targets = ((1 - place.core) + 2 * (1 - place.x), (1 - place.core) + 2 * place.x)

    def kv_rows(i):
        return pl.ds(i * (STEP // BLK), STEP // BLK)

    def kv_to_pair(w, i):
        return remote(
            dkv_ref.at[targets[w], kv_rows(i)], kv_pair_s.at[w, kv_rows(i)], kv_pair_send.at[w, i],
            kv_pair.at[w, i], place.sibling,
        )

    def kv_across(i):
        return remote(
            kv_far_s.at[kv_rows(i)], kv_cross_s.at[kv_rows(i)], kv_cross_send.at[i], kv_cross.at[i], place.across
        )

    def momenta(act):
        for core in range(2):

            def loads(core=core):
                act(pltpu.make_async_copy(mkv_hbm.at[:, core, :], mkv_s, moment_sem.at[0]))
                act(pltpu.make_async_copy(mgu_hbm.at[:, core, :], mgu_s, moment_sem.at[1]))

            pl.when(place.core == core)(loads)

    momenta(lambda copy: copy.start())
    greet(place, lambda: every(lambda shard, k: own_load(shard, k).start(), LOADED), True)
    gain = gain_row(wa_ref, HALF)
    gains = [jnp.zeros((1, D), F32)]

    def send_pair(t, side):
        shard = 2 * order(t) + (place.column if side else 1 - place.column)
        for k in LOADED:
            to_pair(shard, k).start()

    def send_kv(w):
        for i in range(steps):
            kv_to_pair(w, i).start()

    def cross_kv():
        for i in range(steps):
            kv_to_pair(0, i).wait_recv()
            kv_far_s[kv_rows(i)] = added(dkv_ref[place.across[1], kv_rows(i)], kv_pair_s[0, kv_rows(i)]).astype(BF16)
            kv_across(i).start()

    def finish_rows(i):
        kv_to_pair(1, i).wait_recv()
        kv_across(i).wait_recv()
        mine = added(dkv_ref[place.d, kv_rows(i)], kv_pair_s[1, kv_rows(i)])
        kv_s[kv_rows(i)] = (mine + kv_cross_s[kv_rows(i)].astype(F32)).astype(BF16)
        gains[0] = gains[0] + input_grad_rows(
            meta, i, x_ref, wa_ref, gain, gq_ref, kv_s, gres_ref, turned_ref, steps_ref, int_ref,
            last_s, values_s,
        )

    def normed_all():
        for i in range(steps):
            normed_rows(i, x_ref, gain, normed_s)

    def pair_all(k):
        every(lambda shard, k: to_pair(shard, k).start(), (k,))

    stages = {
        "pp": send_pair, "kvp": send_kv, "kvx": cross_kv, "fin": finish_rows,
        "prep": normed_all, "da1": lambda: early_grads(da_s, normed_s, gq_ref, lowt_ref, gb_ref),
        "da2": lambda: late_grads(da_s, normed_s, last_s, values_s, lowt_ref, gb_ref, gains[0], gain_ref),
        "pp4": lambda: pair_all(4), "pp0": lambda: pair_all(0),
        "P": stage_pair, "S": stage_side, "Z": stage_line, "F": stage_last,
    }
    for event, *which in REDUCE_ORDER:
        stages[event](*which)
    momenta(lambda copy: copy.wait())
    muon_part(
        place, a_out, gu_out, d_out, mq_ref, mkv_s, mo_ref, mgu_s, md_ref,
        sq_out, nk_out, ugu_out, ud_out, *muon_s
    )
    for k in range(SUMS):
        share(k, 1 - place.core).wait_recv()
        share(k, place.core).wait_send()
        last(k).wait_send()
    every(lambda shard, k: to_pair(shard, k).wait_send(), range(SUMS))
    for i in range(steps):
        kv_to_pair(0, i).wait_send()
        kv_to_pair(1, i).wait_send()
        kv_across(i).wait_send()
    for t in range(lines):
        spot = order(t)
        for k in range(SUMS):
            other, own = 2 * spot + 1 - place.column, 2 * spot + place.column
            on_plane(
                k,
                lambda split: pass_on(other, k, 1, spot, place.beside).wait_send(),
                lambda: pass_on(other, k, 0, spot, place.across).wait_send(),
            )
            if t < lines - 1:
                pl.when(spot > place.line)(lambda: pass_on(own, k, 2, spot, place.above).wait_send())
                pl.when(spot < place.line)(lambda: pass_on(own, k, 3, spot, place.below).wait_send())


def added(one, two):
    return one.astype(F32) + two.astype(F32)


def reduce_remote(meta, x, packed, gq, dkv, gres, gb, lowt, gain, turned, steps_of, momenta, d_gateup, d_down, count):
    lines, rows = count // 2, x.shape[0]
    shard_rows, tall = D // count, FF // count
    m_query, m_keyval, m_out, m_gateup, m_down = momenta
    steps, blocks = rows // STEP, (rows // BLK,) + dkv.shape[1:]
    halves = ((shard_rows, O_AT), (shard_rows, FF), (tall // 2, D))
    anywhere = pl.BlockSpec(memory_space=pl.ANY)
    dma = pltpu.SemaphoreType.DMA
    outs = pl.pallas_call(
        partial(reduce_kernel, lines),
        out_shape=(
            jax.ShapeDtypeStruct((D, rows), F32),
            jax.ShapeDtypeStruct((shard_rows, WIDE_A), BF16),
            jax.ShapeDtypeStruct((shard_rows, 2 * FF), BF16),
            jax.ShapeDtypeStruct((tall, D), BF16),
            jax.ShapeDtypeStruct((2, shard_rows, QW), BF16),
            jax.ShapeDtypeStruct((2, shard_rows, NARROW), BF16),
            jax.ShapeDtypeStruct((2, shard_rows, FF), BF16),
            jax.ShapeDtypeStruct((tall, D), BF16),
        ),
        in_specs=[pl.BlockSpec(memory_space=pltpu.SMEM)] + vmem(13) + [anywhere] * 4,
        out_specs=tuple(vmem(8)),
        scratch_shapes=finish_scratch(rows)
        + [pltpu.VMEM(blocks, BF16), pltpu.VMEM((2,) + blocks, BF16)]
        + [pltpu.VMEM(blocks, BF16)] * 2
        + [pltpu.VMEM((count, shard_rows, WIDE_A), BF16)]
        + [pltpu.VMEM((count,) + h, BF16) for h in halves[1:] + halves]
        + [pltpu.VMEM((5, lines) + h, BF16) for h in halves]
        + [
            pltpu.VMEM((shard_rows, KVW), F32), pltpu.VMEM((shard_rows, FF), F32), dma((2,)),
            dma((count, 3)), dma((2, steps)), dma((steps,)), dma((2, steps)), dma((steps,)),
            dma((count, SUMS)), dma((4, lines, SUMS)), dma((2, SUMS)),
            dma((count, SUMS)), dma((4, lines, SUMS)), dma((2, SUMS)),
        ]
        + muon_scratch(count, shard_rows, tall // 2),
        compiler_params=pltpu.CompilerParams(
            collective_id=1, has_side_effects=True, vmem_limit_bytes=VMEM_LIMIT
        ),
        name="finish_and_reduce",
    )(
        meta, x, packed, gq, dkv.reshape((4,) + blocks), gres, gb, lowt, gain, turned, steps_of,
        m_query, m_out, m_down, m_keyval, m_gateup,
        d_gateup.reshape(count, shard_rows, 2 * FF), d_down.reshape(count, tall, D),
    )
    return outs[0], outs[1:4], outs[4:]


def own_kernels():
    return lax.axis_size("fsdp") == 8 and lax.axis_size("dp") == 4


def begin(*given):
    return start_remote(*given, lax.axis_size("fsdp")) if own_kernels() else start_xla(*given)


def reduce_and_update(meta, x, packed, gq, dkv, gres, gb, lowt, gain, turned, steps, momenta, d_gateup, d_down):
    if own_kernels():
        return reduce_remote(
            meta, x, packed, gq, dkv, gres, gb, lowt, gain, turned, steps, momenta, d_gateup, d_down,
            lax.axis_size("fsdp"),
        )
    dkv = lax.psum_scatter(dkv, "dp", scatter_dimension=0, tiled=True)
    input_grad, d_packed = finish(meta, x, packed, gq, dkv, gres, gb, lowt, gain, turned, steps)
    grads = tuple(reduce_rows_xla(g) for g in (d_packed, d_gateup, d_down))
    return input_grad, grads, muon_updates(grads, momenta)


def muon_updates(grads, momenta):
    packed, gateup, down = (g.astype(F32) for g in grads)
    m_query, m_keyval, m_out, m_gateup, m_down = momenta

    def moment(momentum, grad):
        return MOMENTUM_DECAY * momentum + grad

    steps = muon_exchange(
        [
            moment(m_query, packed[:, :QW]),
            moment(m_keyval[:, 0], packed[:, QW:HALF]),
            moment(m_keyval[:, 1], packed[:, O_AT + QW : O_AT + HALF]),
            moment(m_out, packed[:, O_AT : O_AT + QW]),
            moment(m_gateup[:, 0], gateup[:, :FF]),
            moment(m_gateup[:, 1], gateup[:, FF:]),
            moment(m_down, down),
        ]
    )
    return (
        jnp.stack([steps[0], steps[3]]).astype(BF16),
        jnp.pad(jnp.stack(steps[1:3]), ((0, 0), (0, 0), (0, NARROW - KVW))).astype(BF16),
        jnp.stack(steps[4:6]).astype(BF16),
        steps[6].astype(BF16),
    )


def local(
    tokens, cotangent, lengths, assignment, norm_gains, gain_momentum, w_query, w_keyval, w_out,
    w_gateup, w_down, m_query, m_keyval, m_out, m_gateup, m_down,
):
    gain_rate = GAIN_SCALE / math.sqrt(assignment.shape[1] * BLK * 3 // 4 * lax.axis_size("fsdp"))
    inner, outer, turned, steps = rope_constants()
    weights = (w_query, w_keyval, w_out, w_gateup, w_down)
    momenta = (m_query, m_keyval, m_out, m_gateup, m_down)
    meta, x, cot, queries, packed, group_kv, gateup, down = begin(
        lengths, assignment, tokens, cotangent, norm_gains, weights, inner, outer
    )
    gq, dkv, gain, lowt, act, gres, gb, d_gateup, d_down = layer(
        meta, x, cot, queries, group_kv, packed, gateup, down, turned, steps
    )
    input_grad, grads, updates = reduce_and_update(
        meta, x, packed, gq, dkv, gres, gb, lowt, gain, turned, steps, momenta, d_gateup, d_down
    )
    outs = write_outputs(gain_rate, grads, updates, norm_gains.T, gain_momentum.T, weights, momenta)
    return (act.T, input_grad.T) + tuple(g.T for g in outs[:3]) + tuple(outs[3:])


def solution(mesh):
    rows = P(("fsdp", "dp"), None)
    two, three = P("fsdp", None), P("fsdp", None, None)
    return jax.shard_map(
        local,
        mesh=mesh,
        in_specs=(rows, rows, two, two, two, two, two, three, two, three, two, two, three, two, three, two),
        out_specs=(rows, rows) + (two,) * 6 + (three,) * 3 + (two,) * 3 + (three,) * 3 + (two,) * 3,
        check_vma=False,
    )
```
